32 devices in a mesh: seq: 8 (over y, x, core), batch: 4 (over z).
Axes of the slice: x: 2, y: 2, z: 4, core: 2. Of those that a mesh axis runs over, the one named last changes fastest.
Arguments:
- inputs: bfloat16 [8, 1024, 512], P('batch', 'seq'), may hold values from -6 to 6
- doc_lengths: int32 [8, 8], P('batch'), may hold values from 1 to 960, as said below
- norm_gain: float32 [2, 512], replicated, may hold values from 0.1 to 1.9
- decay_log: float32 [2, 384], replicated
- frequency: float32 [2, 384], replicated, may hold values from 0.5 to 30
- step_log: float32 [2, 384], replicated
- in_weight: bfloat16 [2, 512, 768], replicated, may hold values from -0.25 to 0.25
- skip_weight: float32 [2, 512], replicated, may hold values from -4 to 4
- out_weight: bfloat16 [2, 1536, 512], replicated, may hold values from -0.15625 to 0.15625
- glu_weight: bfloat16 [2, 512, 512], replicated, may hold values from -0.25 to 0.25
- cotangent: bfloat16 [8, 1024, 512], P('batch', 'seq'), may hold values from -6 to 6
Outputs:
- output: bfloat16 [8, 1024, 512], P('batch', 'seq')
- input_grad: bfloat16 [8, 1024, 512], P('batch', 'seq')
- gain_grad: float32 [2, 512], replicated
- decay_log_grad: float32 [2, 384], replicated
- frequency_grad: float32 [2, 384], replicated
- step_log_grad: float32 [2, 384], replicated
- in_weight_grad: float32 [2, 512, 768], replicated
- skip_grad: float32 [2, 512], replicated
- out_weight_grad: float32 [2, 1536, 512], replicated
- glu_grad: float32 [2, 512, 512], replicated
The draws below stay inside these ranges and needn't reach their ends.
Inputs may be any that keep to these rules, and one draw needn't show every extreme that they name: `doc_lengths`: each row's lengths sum to at most 1024; of the 2 rows of each batch index, one holds a document of exactly 960 positions.
All inputs are finite; a program needn't handle non-finite values.
Results may differ from the reference program's by a relative error of at most 0.015.
Values sent between devices are 32-bit elements; how exact they have to be, the bound alone decides.
No kernel may reach another device: no remote copies, remote signals or barrier semaphores. Data moves between devices by JAX's collectives and lax.ppermute only.
A program may use at most 192 MiB of HBM per device.

```python
import math
import jax
import jax.numpy as jnp
from jax import lax

H = 512
P_SIZE = 384
LAYERS = 2
MICRO = 2
DOCS = 8
STRETCH = 128
TIME = 1024
ROWS = 8


def rates_and_steps(key, slow_share):
    pick_key, fast_key, slow_key, step_key = jax.random.split(key, 4)
    layout = (LAYERS, P_SIZE)
    picked = jax.random.uniform(pick_key, layout)
    fast_rate = jnp.exp(jax.random.uniform(fast_key, layout, minval=math.log(1.0 / 50.0), maxval=math.log(1.0 / 30.0)))
    slow_rate = jnp.exp(jax.random.uniform(slow_key, layout, minval=math.log(0.1 / TIME), maxval=math.log(2.0 / TIME)))
    chosen_rate = jnp.where(picked < slow_share, slow_rate, fast_rate)
    step_values = jax.random.uniform(step_key, layout, minval=math.log(0.005), maxval=math.log(0.05))
    return ((jnp.log(chosen_rate) - step_values).astype(jnp.float32), step_values.astype(jnp.float32))


def draw_decay_log(key, part):
    drawn = rates_and_steps(key, 0.5)
    return drawn[0]


def draw_step_log(key, part):
    drawn = rates_and_steps(key, 0.5)
    return drawn[1]


def draw_doc_lengths(key, part):
    key = jax.random.fold_in(key, 7)
    row_key, slot_key, small_key, drawn_key = jax.random.split(key, 4)
    groups = ROWS // MICRO
    long_row = jax.random.randint(row_key, (groups,), 0, MICRO)
    long_slot = jax.random.randint(slot_key, (ROWS, 1), 0, DOCS)
    small_docs = jax.random.randint(small_key, (ROWS, DOCS), 1, STRETCH // 16 + 1)
    drawn_docs = jax.random.randint(drawn_key, (ROWS, DOCS), max(1, TIME // (2 * DOCS)), TIME // DOCS + 1)
    slot_ids = jnp.arange(DOCS, dtype=jnp.int32)[None, :]
    long_docs = jnp.where(slot_ids == long_slot, TIME - STRETCH // 2, small_docs)
    row_ids = jnp.arange(ROWS, dtype=jnp.int32)
    holds_long = row_ids % MICRO == jnp.repeat(long_row, MICRO)
    return jnp.where(holds_long[:, None], long_docs, drawn_docs).astype(jnp.int32)


def steps_of(stream_key, extent, cuts, smallest, largest):
    factor_of = 1.0
    for position, parts in cuts:
        steps = jax.random.uniform(jax.random.fold_in(jax.random.fold_in(stream_key, 6), position), (parts,), jnp.float32, smallest / len(cuts), largest / len(cuts))
        factor_of = factor_of * jnp.repeat(jnp.exp(steps), extent[position] // parts).reshape((-1,) + (1,) * (len(extent) - 1 - position))
    return factor_of


def bell_draw(key, extent, width, most, cuts=(), kind=jnp.bfloat16):
    level = steps_of(key, extent, cuts, -0.22, 0.18) if cuts else 1.0
    entries = jax.random.normal(key, extent, jnp.float32) * width * level
    return jnp.minimum(jnp.maximum(entries, -most), most).astype(kind)


def setup_inputs(seed: int = 0) -> dict:
    arg_keys = jax.random.split(jax.random.key(seed), 12)
    return {
        "inputs": bell_draw(arg_keys[0], (ROWS, TIME, H), 1.0, 6.0, ((0, 4), (1, 8))),
        "doc_lengths": draw_doc_lengths(jax.random.fold_in(arg_keys[11], 71), 0),
        "norm_gain": jnp.clip(1.0 + 0.18 * jax.random.normal(arg_keys[2], (LAYERS, H), jnp.float32), 0.1, 1.9),
        "decay_log": draw_decay_log(jax.random.fold_in(arg_keys[11], 71), 0),
        "frequency": jnp.clip(jax.random.uniform(arg_keys[4], (LAYERS, P_SIZE), jnp.float32, 0.5, 30.0), 0.5, 30.0),
        "step_log": draw_step_log(jax.random.fold_in(arg_keys[11], 71), 0),
        "in_weight": bell_draw(arg_keys[6], (LAYERS, H, 2 * P_SIZE), H ** -0.5, 0.25),
        "skip_weight": bell_draw(arg_keys[7], (LAYERS, H), 1.0, 4.0, (), jnp.float32),
        "out_weight": bell_draw(arg_keys[8], (LAYERS, 4 * P_SIZE, H), (4 * P_SIZE) ** -0.5, 0.15625),
        "glu_weight": bell_draw(arg_keys[9], (LAYERS, H, H), H ** -0.5, 0.25),
        "cotangent": bell_draw(arg_keys[10], (ROWS, TIME, H), 1.0, 6.0, ((0, 4), (1, 8))),
    }


epsilon = 1e-05
highest = lax.Precision.HIGHEST

@jax.custom_vjp
def low(v):
    return lax.optimization_barrier(v.astype(jnp.bfloat16)).astype(jnp.float32)

@jax.custom_vjp
def low_back(v):
    return v

def low_keep(v):
    return (low(v), None)

def low_pass(kept, grad):
    return (grad,)

def back_keep(v):
    return (v, None)

def back_low(kept, grad):
    return (low(grad),)
low.defvjp(low_keep, low_pass)
low_back.defvjp(back_keep, back_low)

def complex_mul(left_real, left_imag, right_real, right_imag):
    return (left_real * right_real - left_imag * right_imag, left_real * right_imag + left_imag * right_real)

def compose(former, latter):
    factor_real, factor_imag = complex_mul(latter[0], latter[1], former[0], former[1])
    carried_real, carried_imag = complex_mul(latter[0], latter[1], former[2], former[3])
    return (factor_real, factor_imag, carried_real + latter[2], carried_imag + latter[3])

def discretize(decay_log, frequency, step_log, in_weight):
    step_size = jnp.exp(step_log)
    pole_real = -jnp.exp(decay_log)
    shrink = step_size * pole_real
    rotation = step_size * frequency
    radius = jnp.exp(shrink)
    decay_real = radius * jnp.cos(rotation)
    decay_imag = radius * jnp.sin(rotation)
    minus_real = jnp.expm1(shrink) * jnp.cos(rotation) - 2.0 * jnp.sin(0.5 * rotation) ** 2
    modulus = pole_real * pole_real + frequency * frequency
    factor_real = (minus_real * pole_real + decay_imag * frequency) / modulus
    factor_imag = (decay_imag * pole_real - minus_real * frequency) / modulus
    state_width = decay_log.shape[0]
    weight_real = in_weight[:, :state_width]
    weight_imag = in_weight[:, state_width:]
    bar_real = factor_real * weight_real - factor_imag * weight_imag
    bar_imag = factor_real * weight_imag + factor_imag * weight_real
    return (decay_real, decay_imag, jnp.concatenate([bar_real, bar_imag], axis=1))

def mixer_layer(values, norm_gain, decay_log, frequency, step_log, in_weight, skip_weight, out_weight, glu_weight, starts, endings, validity):
    average = lax.optimization_barrier(jnp.mean(values, axis=-1, keepdims=True))
    centered = values - average
    inverse = lax.rsqrt(lax.optimization_barrier(jnp.mean(centered * centered, axis=-1, keepdims=True)) + epsilon)
    scaled = low(centered * inverse * norm_gain * validity[:, None])
    decay_real, decay_imag, bar_weight = discretize(decay_log, frequency, step_log, in_weight)
    drive_terms = low_back(jnp.dot(scaled, low(bar_weight), precision=highest))
    state_width = decay_real.shape[0]
    keep_ahead = (1.0 - starts)[:, None]
    keep_behind = (1.0 - endings)[:, None]
    forward_scan = lax.associative_scan(compose, (decay_real * keep_ahead, decay_imag * keep_ahead, drive_terms[:, :state_width], drive_terms[:, state_width:]), axis=0)
    reverse_scan = lax.associative_scan(compose, (decay_real * keep_behind, decay_imag * keep_behind, drive_terms[:, :state_width], drive_terms[:, state_width:]), axis=0, reverse=True)
    states = low(jnp.concatenate([forward_scan[2], forward_scan[3], reverse_scan[2], reverse_scan[3]], axis=1))
    mixed_out = low_back(jnp.dot(states, out_weight, precision=highest)) + skip_weight * scaled
    activated = low(jax.nn.gelu(mixed_out))
    logits = low_back(jnp.dot(activated, glu_weight, precision=highest))
    return values + validity[:, None] * activated * jax.nn.sigmoid(logits)

def row_block(values, lengths, weights):
    positions = jnp.arange(TIME, dtype=jnp.int32)
    offsets = jnp.concatenate([jnp.zeros((1,), jnp.int32), jnp.cumsum(lengths).astype(jnp.int32)])
    starts = jnp.any(positions[:, None] == offsets[None, :], axis=1).astype(jnp.float32)
    endings = jnp.any(positions[:, None] + 1 == offsets[None, :], axis=1).astype(jnp.float32)
    validity = (positions < offsets[-1]).astype(jnp.float32)
    for layer_index in range(LAYERS):
        values = mixer_layer(values, *[stacked[layer_index] for stacked in weights], starts, endings, validity)
    return values

def reference(inputs, doc_lengths, norm_gain, decay_log, frequency, step_log, in_weight, skip_weight, out_weight, glu_weight, cotangent):
    weights = (norm_gain, decay_log, frequency, step_log, in_weight.astype(jnp.float32), skip_weight, out_weight.astype(jnp.float32), glu_weight.astype(jnp.float32))

    def forward(values, params):

        def one_row(row_pair):
            return row_block(row_pair[0], row_pair[1], params)
        return lax.map(jax.checkpoint(one_row), (values, doc_lengths))
    output, pullback = jax.vjp(forward, inputs.astype(jnp.float32), weights)
    grad_inputs, gradients = pullback(cotangent.astype(jnp.float32))
    return (output.astype(jnp.bfloat16), grad_inputs.astype(jnp.bfloat16), gradients[0], gradients[1], gradients[2], gradients[3], gradients[4], gradients[5], gradients[6], gradients[7])
```

```python
import functools
import math

import jax
import jax.numpy as jnp
from jax import lax
from jax.experimental import pallas as pl
from jax.experimental.pallas import tpu as pltpu
from jax.sharding import PartitionSpec as P

epsilon = 1e-05
chunk_count = 8
lane_count = 128
block_rows = 32
vmem_bytes = 56 * 1024 * 1024
gelu_scale = math.sqrt(2.0 / math.pi)
gelu_cubic = 0.044715
f32 = jnp.float32
bf16 = jnp.bfloat16


def complex_mul(left_real, left_imag, right_real, right_imag):
    return (
        left_real * right_real - left_imag * right_imag,
        left_real * right_imag + left_imag * right_real,
    )


def complex_power(real, imag, exponent):
    result = None
    while exponent:
        if exponent & 1:
            result = (real, imag) if result is None else complex_mul(*result, real, imag)
        exponent >>= 1
        if exponent:
            real, imag = complex_mul(real, imag, real, imag)
    return result


def rates(decay_log, frequency, step_log):
    step_size = jnp.exp(step_log)
    pole_real = -jnp.exp(decay_log)
    shrink = step_size * pole_real
    rotation = step_size * frequency
    radius = jnp.exp(shrink)
    decay_real = radius * jnp.cos(rotation)
    decay_imag = radius * jnp.sin(rotation)
    minus_real = jnp.expm1(shrink) * jnp.cos(rotation) - 2.0 * jnp.sin(0.5 * rotation) ** 2
    modulus = pole_real * pole_real + frequency * frequency
    factor_real = (minus_real * pole_real + decay_imag * frequency) / modulus
    factor_imag = (decay_imag * pole_real - minus_real * frequency) / modulus
    return (decay_real, decay_imag, factor_real, factor_imag)


def dot(left, right):
    return lax.dot_general(left, right, (((1,), (0,)), ((), ())), preferred_element_type=f32)


def dot_right(left, right):
    return lax.dot_general(left, right, (((1,), (1,)), ((), ())), preferred_element_type=f32)


def dot_left(left, right):
    return lax.dot_general(left, right, (((0,), (0,)), ((), ())), preferred_element_type=f32)


def spread(narrow, width):
    return jnp.concatenate([narrow] * (width // lane_count), axis=1)


def order_matrix(count, inverse):
    rows = lax.broadcasted_iota(jnp.int32, (count, count), 0)
    cols = lax.broadcasted_iota(jnp.int32, (count, count), 1)
    if inverse:
        rows, cols = cols, rows
    source = lax.rem(rows, chunk_count) * (count // chunk_count) + lax.div(rows, chunk_count)
    return jnp.where(cols == source, 1.0, 0.0).astype(bf16)


def over_blocks(count, body):
    def one(index, carry):
        body(pl.ds(pl.multiple_of(index * block_rows, block_rows), block_rows))
        return carry

    lax.fori_loop(0, count // block_rows, one, 0)


def normalize(values):
    average = jnp.mean(values, axis=-1, keepdims=True)
    centered = values - average
    inverse = lax.rsqrt(jnp.mean(centered * centered, axis=-1, keepdims=True) + epsilon)
    return centered * inverse, inverse


def gelu_parts(mixed):
    square = mixed * mixed
    bend = jnp.tanh(gelu_scale * mixed * (1.0 + gelu_cubic * square))
    half = 0.5 + 0.5 * bend
    slope = half + 0.5 * mixed * (1.0 - bend * bend) * gelu_scale * (
        1.0 + 3.0 * gelu_cubic * square
    )
    return mixed * half, slope


def write_flags(place, docs_ref, flags_ref, blocks_ref, length):
    row_count, doc_count = docs_ref.shape
    span = row_count * length // chunk_count
    per_row = chunk_count // row_count
    offsets = []
    for row in range(row_count):
        running = [jnp.int32(0)]
        for doc in range(doc_count):
            running.append(running[-1] + docs_ref[row, doc])
        offsets.append(running)

    def by_row(row_of, member):
        chosen = jnp.full(row_of.shape, offsets[0][member], jnp.int32)
        for row in range(1, row_count):
            chosen = jnp.where(row_of == row, offsets[row][member], chosen)
        return chosen

    chunk = lax.broadcasted_iota(jnp.int32, (chunk_count, lane_count), 0)
    row_of = lax.div(chunk, per_row)
    bounds = [by_row(row_of, member) for member in range(doc_count + 1)]
    base = place * length + lax.rem(chunk, per_row) * span
    for step in range(span):
        position = base + step
        starts = position == bounds[0]
        endings = position + 1 == bounds[0]
        for bound in bounds[1:]:
            starts = starts | (position == bound)
            endings = endings | (position + 1 == bound)
        window = pl.ds(chunk_count * step, chunk_count)
        flags_ref[0, window, :] = jnp.where(starts, 0.0, 1.0)
        flags_ref[1, window, :] = jnp.where(endings, 0.0, 1.0)
        flags_ref[2, window, :] = jnp.where(position < bounds[-1], 1.0, 0.0)
    entry = lax.broadcasted_iota(jnp.int32, blocks_ref.shape[1:], 0)
    row_of = lax.rem(entry, row_count)
    first = lax.div(entry, row_count) * length
    starts = jnp.zeros(entry.shape, jnp.bool_)
    endings = starts
    for member in range(doc_count + 1):
        bound = by_row(row_of, member)
        starts = starts | ((bound >= first) & (bound < first + length))
        endings = endings | ((bound > first) & (bound <= first + length))
    blocks_ref[0] = jnp.where(starts, 0.0, 1.0)
    blocks_ref[1] = jnp.where(endings, 0.0, 1.0)


def chunk_keeps(flags_ref):
    span = flags_ref.shape[1] // chunk_count
    ahead = flags_ref[0, :chunk_count, :]
    behind = flags_ref[1, :chunk_count, :]
    for step in range(1, span):
        window = pl.ds(chunk_count * step, chunk_count)
        ahead = ahead * flags_ref[0, window, :]
        behind = behind * flags_ref[1, window, :]
    return ahead, behind


def toward(array, distance, reverse):
    return pltpu.roll(array, chunk_count - distance if reverse else distance, axis=0)


def chunk_prefix(ends, factor, entering, per_row, reverse):
    width = ends[0].shape[1]
    chunk = lax.broadcasted_iota(jnp.int32, (chunk_count, width), 0)
    within = lax.rem(chunk, per_row)
    within = per_row - 1 - within if reverse else within
    first = within == 0
    total_real, total_imag = ends
    if entering is not None:
        moved_real, moved_imag = complex_mul(*factor, *entering)
        total_real = total_real + jnp.where(first, moved_real, 0.0)
        total_imag = total_imag + jnp.where(first, moved_imag, 0.0)
    distance = 1
    while distance < per_row:
        reach = within >= distance
        near_real = toward(total_real, distance, reverse)
        near_imag = toward(total_imag, distance, reverse)
        moved_real, moved_imag = complex_mul(*factor, near_real, near_imag)
        total_real = total_real + jnp.where(reach, moved_real, 0.0)
        total_imag = total_imag + jnp.where(reach, moved_imag, 0.0)
        if 2 * distance < per_row:
            far_real = toward(factor[0], distance, reverse)
            far_imag = toward(factor[1], distance, reverse)
            both_real, both_imag = complex_mul(*factor, far_real, far_imag)
            factor = (
                jnp.where(reach, both_real, factor[0]),
                jnp.where(reach, both_imag, factor[1]),
            )
        distance *= 2
    enter_real = toward(total_real, 1, reverse)
    enter_imag = toward(total_imag, 1, reverse)
    none = (jnp.zeros_like(total_real),) * 2 if entering is None else entering
    return (
        (total_real, total_imag),
        (jnp.where(first, none[0], enter_real), jnp.where(first, none[1], enter_imag)),
    )


def sweep(flags_ref, pole_real, pole_imag, forward_at, reverse_at, start, put_forward, put_reverse):
    width = pole_real.shape[1]
    span = flags_ref.shape[1] // chunk_count

    def one(step, state):
        ahead_real, ahead_imag, behind_real, behind_imag = state
        here = pl.ds(pl.multiple_of(chunk_count * step, chunk_count), chunk_count)
        there = pl.ds(pl.multiple_of(chunk_count * (span - 1 - step), chunk_count), chunk_count)
        keep = spread(flags_ref[0, here, :], width)
        moved_real, moved_imag = complex_mul(pole_real * keep, pole_imag * keep, ahead_real, ahead_imag)
        drive_real, drive_imag = forward_at(here)
        ahead_real = moved_real + drive_real
        ahead_imag = moved_imag + drive_imag
        keep = spread(flags_ref[1, there, :], width)
        moved_real, moved_imag = complex_mul(
            pole_real * keep, pole_imag * keep, behind_real, behind_imag
        )
        drive_real, drive_imag = reverse_at(there)
        behind_real = moved_real + drive_real
        behind_imag = moved_imag + drive_imag
        if put_forward is not None:
            put_forward(here, ahead_real, ahead_imag)
            put_reverse(there, behind_real, behind_imag)
        return (ahead_real, ahead_imag, behind_real, behind_imag)

    return lax.fori_loop(0, span, one, start, unroll=4)


def local_totals(flags_ref, pole_real, pole_imag, forward_at, reverse_at, ends_ref, totals_ref):
    width = pole_real.shape[1]
    span = flags_ref.shape[1] // chunk_count
    row_count = totals_ref.shape[0] // 4
    per_row = chunk_count // row_count
    pole_real = jnp.broadcast_to(pole_real, (chunk_count, width))
    pole_imag = jnp.broadcast_to(pole_imag, (chunk_count, width))
    zero = jnp.zeros((chunk_count, width), f32)
    ends = sweep(
        flags_ref, pole_real, pole_imag, forward_at, reverse_at, (zero,) * 4, None, None
    )
    for member in range(4):
        ends_ref[:, member * width : (member + 1) * width] = ends[member]
    power_real, power_imag = complex_power(pole_real, pole_imag, span)
    for direction, keep in enumerate(chunk_keeps(flags_ref)):
        keep = spread(keep, width)
        pair = ends[2 * direction : 2 * direction + 2]
        totals, unused = chunk_prefix(
            pair, (power_real * keep, power_imag * keep), None, per_row, direction == 1
        )
        for part in range(2):
            for row in range(row_count):
                chunk = row * per_row if direction == 1 else (row + 1) * per_row - 1
                entry = (2 * direction + part) * row_count + row
                totals_ref[entry : entry + 1, :] = totals[part][chunk : chunk + 1, :]


def chunk_entrances(place, gathered_ref, flags_ref, blocks_ref, ends_ref, pole_real, pole_imag, length):
    width = pole_real.shape[1]
    span = flags_ref.shape[1] // chunk_count
    row_count = chunk_count * span // length
    per_row = chunk_count // row_count
    device_count = gathered_ref.shape[0] // (4 * row_count)
    pole_real = jnp.broadcast_to(pole_real, (chunk_count, width))
    pole_imag = jnp.broadcast_to(pole_imag, (chunk_count, width))
    power_real, power_imag = complex_power(pole_real, pole_imag, span)
    device_real, device_imag = complex_power(power_real, power_imag, per_row)
    device_real = device_real[:row_count]
    device_imag = device_imag[:row_count]
    entrances = []
    for direction, keep in enumerate(chunk_keeps(flags_ref)):
        real = jnp.zeros((row_count, width), f32)
        imag = real
        for lap in range(device_count):
            source = device_count - 1 - lap if direction == 1 else lap
            live = source > place if direction == 1 else source < place
            open_ = spread(
                blocks_ref[direction, source * row_count : (source + 1) * row_count, :], width
            )
            moved_real, moved_imag = complex_mul(device_real * open_, device_imag * open_, real, imag)
            first = (4 * source + 2 * direction) * row_count
            moved_real = moved_real + gathered_ref[first : first + row_count, :]
            moved_imag = moved_imag + gathered_ref[first + row_count : first + 2 * row_count, :]
            real = jnp.where(live, moved_real, real)
            imag = jnp.where(live, moved_imag, imag)
        entering = tuple(
            jnp.concatenate(
                [
                    jnp.broadcast_to(part[row : row + 1, :], (per_row, width))
                    for row in range(row_count)
                ],
                axis=0,
            )
            for part in (real, imag)
        )
        keep = spread(keep, width)
        first = 2 * direction * width
        ends = (ends_ref[:, first : first + width], ends_ref[:, first + width : first + 2 * width])
        unused, entrance = chunk_prefix(
            ends, (power_real * keep, power_imag * keep), entering, per_row, direction == 1
        )
        entrances.extend(entrance)
    return tuple(entrances)


def layer_poles(tables_ref, layer):
    return tables_ref[4 * layer : 4 * layer + 1, :], tables_ref[4 * layer + 1 : 4 * layer + 2, :]


def layer_factors(tables_ref, layer):
    return tables_ref[4 * layer + 2 : 4 * layer + 3, :], tables_ref[4 * layer + 3 : 4 * layer + 4, :]


def write_bar(tables_ref, layer, in_ref, bar_ref):
    width = tables_ref.shape[1]
    factor_real, factor_imag = layer_factors(tables_ref, layer)

    def body(rows):
        weight_real = in_ref[rows, :width].astype(f32)
        weight_imag = in_ref[rows, width:].astype(f32)
        real, imag = complex_mul(factor_real, factor_imag, weight_real, weight_imag)
        bar_ref[rows, :width] = real.astype(bf16)
        bar_ref[rows, width:] = imag.astype(bf16)

    over_blocks(in_ref.shape[0], body)


def pair_at(ref, first, width):
    def at(rows):
        return ref[rows, first : first + width], ref[rows, first + width : first + 2 * width]

    return at


def drive_totals(flags_ref, tables_ref, layer, scaled_ref, in_ref, bar_ref, drive_ref, ends_ref, totals_ref):
    width = tables_ref.shape[1]
    write_bar(tables_ref, layer, in_ref.ready(), bar_ref)
    drive_ref[...] = dot(scaled_ref[...], bar_ref[...])
    at = pair_at(drive_ref, 0, width)
    local_totals(flags_ref, *layer_poles(tables_ref, layer), at, at, ends_ref, totals_ref)


def settled_states(
    place, gathered_ref, flags_ref, blocks_ref, tables_ref, layer, drive_ref, ends_ref, length,
    states_ref, low_ref, enter_ref,
):
    width = tables_ref.shape[1]
    pole_real, pole_imag = layer_poles(tables_ref, layer)
    entrances = chunk_entrances(
        place, gathered_ref, flags_ref, blocks_ref, ends_ref, pole_real, pole_imag, length
    )
    for member in range(4):
        enter_ref[:, member * width : (member + 1) * width] = entrances[member]

    def put_forward(rows, real, imag):
        states_ref[rows, :width] = real
        states_ref[rows, width : 2 * width] = imag

    def put_reverse(rows, real, imag):
        states_ref[rows, 2 * width : 3 * width] = real
        states_ref[rows, 3 * width :] = imag

    at = pair_at(drive_ref, 0, width)
    sweep(
        flags_ref,
        jnp.broadcast_to(pole_real, (chunk_count, width)),
        jnp.broadcast_to(pole_imag, (chunk_count, width)),
        at, at, entrances, put_forward, put_reverse,
    )

    def body(rows):
        low_ref[rows, :] = states_ref[rows, :].astype(bf16)

    over_blocks(states_ref.shape[0], body)


def mix_and_gate(layer, low_ref, scaled_ref, out_ref, glu_ref, skip_ref, mixed_ref, act_ref, gate_ref):
    mixed_ref[...] = dot(low_ref[...], out_ref.ready()[...])
    skip = skip_ref[layer : layer + 1, :]

    def body(rows):
        mixed = mixed_ref[rows, :] + skip * scaled_ref[rows, :].astype(f32)
        mixed_ref[rows, :] = mixed
        act_ref[rows, :] = gelu_parts(mixed)[0].astype(bf16)

    over_blocks(mixed_ref.shape[0], body)
    gate_ref[...] = dot(act_ref[...], glu_ref.ready()[...])


def back_tail(
    layer, flags_ref, tables_ref, grad_ref, mixed_ref, act_ref, gate_ref, scaled_ref, low_ref,
    out_ref, glu_ref, skip_ref, logits_ref, work_ref, mixed_low_ref,
    d_mixed_ref, d_states_ref, glu_grad_ref, out_grad_ref, skip_grad_ref, ends_ref, totals_ref,
):
    width = tables_ref.shape[1]
    model = mixed_ref.shape[1]

    def first(rows):
        valid = spread(flags_ref[2, rows, :], model)
        gate = gate_ref[rows, :]
        rate = grad_ref[rows, :] * valid * gate
        logits_ref[rows, :] = (rate * act_ref[rows, :].astype(f32) * (1.0 - gate)).astype(bf16)

    over_blocks(mixed_ref.shape[0], first)
    glu_grad_ref[...] = dot_left(act_ref[...], logits_ref[...])
    work_ref[...] = dot_right(logits_ref[...], glu_ref.ready()[...])
    skip_grad_ref[...] = jnp.zeros(skip_grad_ref.shape, f32)

    def second(rows):
        valid = spread(flags_ref[2, rows, :], model)
        d_act = grad_ref[rows, :] * valid * gate_ref[rows, :] + work_ref[rows, :]
        d_mixed = d_act * gelu_parts(mixed_ref[rows, :])[1]
        d_mixed_ref[rows, :] = d_mixed
        mixed_low_ref[rows, :] = d_mixed.astype(bf16)
        skip_grad_ref[...] += jnp.sum(
            d_mixed * scaled_ref[rows, :].astype(f32), axis=0, keepdims=True
        )

    over_blocks(mixed_ref.shape[0], second)
    d_states_ref[...] = dot_right(mixed_low_ref[...], out_ref.ready()[...])
    out_grad_ref[...] = dot_left(low_ref[...], mixed_low_ref[...])
    pole_real, pole_imag = layer_poles(tables_ref, layer)
    local_totals(
        flags_ref, pole_real, -pole_imag, pair_at(d_states_ref, 2 * width, width),
        pair_at(d_states_ref, 0, width), ends_ref, totals_ref,
    )


def back_front(
    place, layer, length, gathered_ref, flags_ref, blocks_ref, tables_ref, gain_ref, skip_ref, in_ref,
    d_states_ref, ends_ref, states_ref, enter_ref, scaled_ref, values_ref, d_mixed_ref, grad_ref,
    lam_ref, mu_ref, low_ref, bar_ref, work_ref,
    in_grad_ref, gain_grad_ref, rate_grad_ref, put_gradient,
):
    width = tables_ref.shape[1]
    model = values_ref.shape[1]
    count = values_ref.shape[0]
    pole_real, pole_imag = layer_poles(tables_ref, layer)
    entrances = chunk_entrances(
        place, gathered_ref, flags_ref, blocks_ref, ends_ref, pole_real, -pole_imag, length
    )

    def put_forward(rows, real, imag):
        mu_ref[rows, :width] = real
        mu_ref[rows, width:] = imag

    def put_reverse(rows, real, imag):
        lam_ref[rows, :width] = real
        lam_ref[rows, width:] = imag

    sweep(
        flags_ref,
        jnp.broadcast_to(pole_real, (chunk_count, width)),
        jnp.broadcast_to(-pole_imag, (chunk_count, width)),
        pair_at(d_states_ref, 2 * width, width), pair_at(d_states_ref, 0, width),
        entrances, put_forward, put_reverse,
    )
    span = count // chunk_count

    def decay_terms(here, before_real, before_imag, after_real, after_imag, sums):
        keep = spread(flags_ref[0, here, :], width)
        lam_real, lam_imag = lam_ref[here, :width], lam_ref[here, width:]
        mu_real, mu_imag = mu_ref[here, :width], mu_ref[here, width:]
        real = keep * (lam_real * before_real + lam_imag * before_imag)
        imag = keep * (lam_imag * before_real - lam_real * before_imag)
        keep = spread(flags_ref[1, here, :], width)
        real = real + keep * (mu_real * after_real + mu_imag * after_imag)
        imag = imag + keep * (mu_imag * after_real - mu_real * after_imag)
        return sums[0] + real, sums[1] + imag

    def window(step):
        start = chunk_count * step
        return pl.ds(start if isinstance(step, int) else pl.multiple_of(start, chunk_count), chunk_count)

    def before_at(step):
        rows = window(step)
        return states_ref[rows, :width], states_ref[rows, width : 2 * width]

    def after_at(step):
        rows = window(step)
        return states_ref[rows, 2 * width : 3 * width], states_ref[rows, 3 * width :]

    def middle(step, sums):
        return decay_terms(window(step), *before_at(step - 1), *after_at(step + 1), sums)

    zero = jnp.zeros((chunk_count, width), f32)
    sums = decay_terms(
        window(0), enter_ref[:, :width], enter_ref[:, width : 2 * width], *after_at(1), (zero, zero)
    )
    sums = lax.fori_loop(1, span - 1, middle, sums, unroll=2)
    sums = decay_terms(
        window(span - 1), *before_at(span - 2),
        enter_ref[:, 2 * width : 3 * width], enter_ref[:, 3 * width :], sums,
    )
    rate_grad_ref[0:1, :] = jnp.sum(sums[0], axis=0, keepdims=True)
    rate_grad_ref[1:2, :] = jnp.sum(sums[1], axis=0, keepdims=True)

    def narrow(rows):
        low_ref[rows, :] = (lam_ref[rows, :] + mu_ref[rows, :]).astype(bf16)

    over_blocks(count, narrow)
    in_ref = in_ref.ready()
    write_bar(tables_ref, layer, in_ref, bar_ref)
    work_ref[...] = dot_right(low_ref[...], bar_ref[...])
    skip = skip_ref[layer : layer + 1, :]
    gain = gain_ref[layer : layer + 1, :]
    gain_grad_ref[...] = jnp.zeros(gain_grad_ref.shape, f32)

    def norm_back(rows):
        valid = spread(flags_ref[2, rows, :], model)
        normed, inverse = normalize(values_ref[rows, :].astype(f32))
        d_scaled = (work_ref[rows, :] + d_mixed_ref[rows, :] * skip) * valid
        gain_grad_ref[...] += jnp.sum(d_scaled * normed, axis=0, keepdims=True)
        d_normed = d_scaled * gain
        put_gradient(
            rows,
            inverse
            * (
                d_normed
                - jnp.mean(d_normed, axis=-1, keepdims=True)
                - normed * jnp.mean(d_normed * normed, axis=-1, keepdims=True)
            )
            + grad_ref[rows, :].astype(f32),
        )

    over_blocks(count, norm_back)
    in_grad_ref[...] = dot_left(scaled_ref[...], low_ref[...])
    factor_real, factor_imag = layer_factors(tables_ref, layer)
    rate_grad_ref[2:4, :] = jnp.zeros((2, width), f32)

    def weigh(rows):
        grad_real, grad_imag = in_grad_ref[rows, :width], in_grad_ref[rows, width:]
        weight_real = in_ref[rows, :width].astype(f32)
        weight_imag = in_ref[rows, width:].astype(f32)
        rate_grad_ref[2:3, :] += jnp.sum(
            grad_real * weight_real + grad_imag * weight_imag, axis=0, keepdims=True
        )
        rate_grad_ref[3:4, :] += jnp.sum(
            grad_imag * weight_real - grad_real * weight_imag, axis=0, keepdims=True
        )
        in_grad_ref[rows, :width] = factor_real * grad_real + factor_imag * grad_imag
        in_grad_ref[rows, width:] = factor_real * grad_imag - factor_imag * grad_real

    over_blocks(in_ref.shape[0], weigh)


def first_kernel(
    length, place_ref, docs_ref, inputs_ref, gain_ref, tables_ref, in_ref,
    flags_ref, blocks_ref, values_ref, scaled_ref, drive_ref, ends_ref, totals_ref, bar_ref,
):
    write_flags(place_ref[0], docs_ref, flags_ref, blocks_ref, length)
    count, model = values_ref.shape
    values_ref[...] = dot(
        order_matrix(count, False), inputs_ref[...].reshape(count, model)
    ).astype(bf16)
    gain = gain_ref[0:1, :]

    def body(rows):
        normed, unused = normalize(values_ref[rows, :].astype(f32))
        valid = spread(flags_ref[2, rows, :], model)
        scaled_ref[rows, :] = (normed * gain * valid).astype(bf16)

    over_blocks(count, body)
    drive_totals(
        flags_ref, tables_ref, 0, scaled_ref, in_ref, bar_ref, drive_ref, ends_ref, totals_ref
    )


def middle_kernel(
    layer, length, place_ref, gathered_ref, flags_ref, blocks_ref, tables_ref, gain_ref, skip_ref,
    drive_ref, ends_ref, values_ref, scaled_ref, out_ref, glu_ref, in_ref,
    states_ref, low_ref, enter_ref, mixed_ref, act_ref, gate_ref,
    next_values_ref, next_scaled_ref, next_drive_ref, next_ends_ref, next_totals_ref, bar_ref,
):
    settled_states(
        place_ref[0], gathered_ref, flags_ref, blocks_ref, tables_ref, layer, drive_ref, ends_ref, length,
        states_ref, low_ref, enter_ref,
    )
    mix_and_gate(
        layer, low_ref, scaled_ref, out_ref, glu_ref, skip_ref, mixed_ref, act_ref, gate_ref
    )
    model = values_ref.shape[1]
    gain = gain_ref[layer + 1 : layer + 2, :]

    def body(rows):
        valid = spread(flags_ref[2, rows, :], model)
        gate = jax.nn.sigmoid(gate_ref[rows, :])
        gate_ref[rows, :] = gate
        result = values_ref[rows, :].astype(f32) + valid * act_ref[rows, :].astype(f32) * gate
        next_values_ref[rows, :] = result
        normed, unused = normalize(result)
        next_scaled_ref[rows, :] = (normed * gain * valid).astype(bf16)

    over_blocks(values_ref.shape[0], body)
    drive_totals(
        flags_ref, tables_ref, layer + 1, next_scaled_ref, in_ref, bar_ref, next_drive_ref,
        next_ends_ref, next_totals_ref,
    )


def turn_kernel(
    layer, length, place_ref, gathered_ref, flags_ref, blocks_ref, tables_ref, skip_ref,
    drive_ref, ends_ref, values_ref, scaled_ref, out_ref, glu_ref, cotangent_ref,
    output_ref, grad_ref, states_ref, enter_ref, d_mixed_ref, d_states_ref,
    glu_grad_ref, out_grad_ref, skip_grad_ref, back_ends_ref, back_totals_ref,
    low_ref, mixed_ref, act_ref, gate_ref, result_ref, logits_ref, work_ref, mixed_low_ref,
):
    settled_states(
        place_ref[0], gathered_ref, flags_ref, blocks_ref, tables_ref, layer, drive_ref, ends_ref, length,
        states_ref, low_ref, enter_ref,
    )
    mix_and_gate(
        layer, low_ref, scaled_ref, out_ref, glu_ref, skip_ref, mixed_ref, act_ref, gate_ref
    )
    count, model = values_ref.shape

    def body(rows):
        valid = spread(flags_ref[2, rows, :], model)
        gate = jax.nn.sigmoid(gate_ref[rows, :])
        gate_ref[rows, :] = gate
        result = values_ref[rows, :] + valid * act_ref[rows, :].astype(f32) * gate
        result_ref[rows, :] = result.astype(bf16)

    over_blocks(count, body)
    output_ref[...] = (
        dot(order_matrix(count, True), result_ref[...]).astype(bf16).reshape(output_ref.shape)
    )
    grad_ref[...] = dot(order_matrix(count, False), cotangent_ref[...].reshape(count, model))
    back_tail(
        layer, flags_ref, tables_ref, grad_ref, mixed_ref, act_ref, gate_ref, scaled_ref, low_ref,
        out_ref, glu_ref, skip_ref, logits_ref, work_ref, mixed_low_ref,
        d_mixed_ref, d_states_ref, glu_grad_ref, out_grad_ref, skip_grad_ref, back_ends_ref,
        back_totals_ref,
    )


def back_middle_kernel(
    layer, length, place_ref, gathered_ref, flags_ref, blocks_ref, tables_ref, gain_ref, skip_ref, in_ref,
    d_states_ref, ends_ref, states_ref, enter_ref, scaled_ref, values_ref, d_mixed_ref, grad_ref,
    out_ref, glu_ref, below_mixed_ref, below_act_ref, below_gate_ref, below_scaled_ref, below_low_ref,
    in_grad_ref, gain_grad_ref, rate_grad_ref, next_grad_ref, below_d_mixed_ref, below_d_states_ref,
    glu_grad_ref, out_grad_ref, skip_grad_ref, below_ends_ref, below_totals_ref,
    lam_ref, mu_ref, low_ref, bar_ref, work_ref, logits_ref, mixed_low_ref,
):
    def put_gradient(rows, gradient):
        next_grad_ref[rows, :] = gradient

    back_front(
        place_ref[0], layer, length, gathered_ref, flags_ref, blocks_ref, tables_ref, gain_ref, skip_ref,
        in_ref, d_states_ref, ends_ref, states_ref, enter_ref, scaled_ref, values_ref, d_mixed_ref,
        grad_ref, lam_ref, mu_ref, low_ref, bar_ref, work_ref,
        in_grad_ref, gain_grad_ref, rate_grad_ref, put_gradient,
    )
    back_tail(
        layer - 1, flags_ref, tables_ref, next_grad_ref, below_mixed_ref, below_act_ref, below_gate_ref,
        below_scaled_ref, below_low_ref, out_ref, glu_ref, skip_ref, logits_ref, work_ref, mixed_low_ref,
        below_d_mixed_ref, below_d_states_ref, glu_grad_ref, out_grad_ref, skip_grad_ref,
        below_ends_ref, below_totals_ref,
    )


def back_last_kernel(
    length, place_ref, gathered_ref, flags_ref, blocks_ref, tables_ref, gain_ref, skip_ref, in_ref,
    d_states_ref, ends_ref, states_ref, enter_ref, scaled_ref, values_ref, d_mixed_ref, grad_ref,
    in_grad_ref, gain_grad_ref, rate_grad_ref, input_grad_ref,
    lam_ref, mu_ref, low_ref, bar_ref, work_ref, result_ref,
):
    def put_gradient(rows, gradient):
        result_ref[rows, :] = gradient.astype(bf16)

    back_front(
        place_ref[0], 0, length, gathered_ref, flags_ref, blocks_ref, tables_ref, gain_ref, skip_ref,
        in_ref, d_states_ref, ends_ref, states_ref, enter_ref, scaled_ref, values_ref, d_mixed_ref,
        grad_ref, lam_ref, mu_ref, low_ref, bar_ref, work_ref,
        in_grad_ref, gain_grad_ref, rate_grad_ref, put_gradient,
    )
    count = result_ref.shape[0]
    input_grad_ref[...] = (
        dot(order_matrix(count, True), result_ref[...]).astype(bf16).reshape(input_grad_ref.shape)
    )


class Fetch:
    def __init__(self, stack_ref, layer, target, semaphore):
        self.copy = pltpu.make_async_copy(stack_ref.at[layer], target, semaphore)
        self.target = target
        self.waiting = True
        self.copy.start()

    def ready(self):
        if self.waiting:
            self.copy.wait()
            self.waiting = False
        return self.target


def call(body, name, operands, outs, scratch):
    scalars = {"place", "docs"}
    arrays = []
    specs = []
    layers = {}
    for position, (key, operand) in enumerate(operands):
        space = pltpu.SMEM if key in scalars else pltpu.VMEM
        if isinstance(operand, tuple):
            operand, layers[position] = operand
            space = pl.ANY
        specs.append(pl.BlockSpec(memory_space=space))
        arrays.append(operand)
    fetched = [
        pltpu.VMEM(arrays[position].shape[1:], arrays[position].dtype) for position in layers
    ]

    def kernel(*refs):
        given = list(refs[: len(arrays)])
        rest = refs[len(arrays) : len(refs) - len(fetched) - 1]
        targets = refs[len(refs) - len(fetched) - 1 : -1]
        for index, (position, layer) in enumerate(layers.items()):
            given[position] = Fetch(given[position], layer, targets[index], refs[-1].at[index])
        body(*given, *rest)

    return pl.pallas_call(
        kernel,
        name=name,
        in_specs=specs,
        out_specs=[pl.BlockSpec(memory_space=pltpu.VMEM)] * len(outs),
        out_shape=[jax.ShapeDtypeStruct(shape, kind) for shape, kind in outs],
        scratch_shapes=[pltpu.VMEM(shape, kind) for shape, kind in scratch]
        + fetched
        + [pltpu.SemaphoreType.DMA((max(1, len(fetched)),))],
        compiler_params=pltpu.CompilerParams(vmem_limit_bytes=vmem_bytes),
    )(*arrays)


def on_device(
    inputs,
    doc_lengths,
    norm_gain,
    decay_log,
    frequency,
    step_log,
    in_weight,
    skip_weight,
    out_weight,
    glu_weight,
    cotangent,
):
    row_count, length, model = inputs.shape
    layer_count, width = decay_log.shape
    count = row_count * length
    device_count = lax.axis_size("seq")
    place = lax.axis_index("seq").astype(jnp.int32).reshape(1)
    rate_tables, rates_back = jax.vjp(rates, decay_log, frequency, step_log)
    tables = jnp.stack(rate_tables, axis=1).reshape(4 * layer_count, width)

    def gather(totals):
        return lax.all_gather(totals, "seq", axis=0, tiled=True)

    flags_out = ((3, count, lane_count), f32)
    blocks_out = ((2, device_count * row_count, lane_count), f32)
    wide_out = ((count, 4 * width), f32)
    ends_out = ((chunk_count, 4 * width), f32)
    totals_out = ((4 * row_count, width), f32)
    tokens = ((count, model), f32)
    tokens_low = ((count, model), bf16)
    drive_out = ((count, 2 * width), f32)
    bar_out = ((model, 2 * width), bf16)
    glu_out = ((model, model), f32)
    out_out = ((4 * width, model), f32)
    in_out = ((model, 2 * width), f32)
    vector = ((1, model), f32)

    flags, blocks, values, scaled, drive, ends, totals = call(
        functools.partial(first_kernel, length),
        "first",
        (
            ("place", place),
            ("docs", doc_lengths),
            ("inputs", inputs),
            ("gain", norm_gain),
            ("tables", tables),
            ("in", (in_weight, 0)),
        ),
        (flags_out, blocks_out, tokens_low, tokens_low, drive_out, ends_out, totals_out),
        (bar_out,),
    )
    shared = (("flags", flags), ("blocks", blocks), ("tables", tables))
    kept = []
    for layer in range(layer_count - 1):
        gathered = gather(totals)
        (
            states, low, enter, mixed, act, gate, next_values, next_scaled, drive, ends, totals,
        ) = call(
            functools.partial(middle_kernel, layer, length),
            "middle",
            (
                ("place", place),
                ("gathered", gathered),
                *shared,
                ("gain", norm_gain),
                ("skip", skip_weight),
                ("drive", drive),
                ("ends", ends),
                ("values", values),
                ("scaled", scaled),
                ("out", (out_weight, layer)),
                ("glu", (glu_weight, layer)),
                ("in", (in_weight, layer + 1)),
            ),
            (
                wide_out, ((count, 4 * width), bf16), ends_out, tokens, tokens_low, tokens,
                tokens, tokens_low, drive_out, ends_out, totals_out,
            ),
            (bar_out,),
        )
        kept.append((states, low, enter, mixed, act, gate, values, scaled))
        values, scaled = next_values, next_scaled
    layer = layer_count - 1
    gathered = gather(totals)
    (
        output, grad, states, enter, d_mixed, d_states, glu_grad, out_grad, skip_grad, ends, totals,
    ) = call(
        functools.partial(turn_kernel, layer, length),
        "turn",
        (
            ("place", place),
            ("gathered", gathered),
            *shared,
            ("skip", skip_weight),
            ("drive", drive),
            ("ends", ends),
            ("values", values),
            ("scaled", scaled),
            ("out", (out_weight, layer)),
            ("glu", (glu_weight, layer)),
            ("cotangent", cotangent),
        ),
        (
            (inputs.shape, bf16), tokens, wide_out, ends_out, tokens, wide_out,
            glu_out, out_out, vector, ends_out, totals_out,
        ),
        (
            ((count, 4 * width), bf16), tokens, tokens_low, tokens, tokens_low, tokens_low, tokens,
            tokens_low,
        ),
    )
    glu_grads, out_grads, skip_grads = [glu_grad], [out_grad], [skip_grad]
    in_grads, gain_grads, rate_grads = [], [], []
    back_scratch = (
        drive_out, drive_out, ((count, 2 * width), bf16), bar_out, tokens,
    )
    rate_out = ((4, width), f32)
    for layer in reversed(range(1, layer_count)):
        gathered = gather(totals)
        low_states, low, low_enter, mixed, act, gate, low_values, low_scaled = kept[layer - 1]
        (
            in_grad, gain_grad, rate_grad, grad, d_mixed, d_states, glu_grad, out_grad, skip_grad, ends,
            totals,
        ) = call(
            functools.partial(back_middle_kernel, layer, length),
            "back_middle",
            (
                ("place", place),
                ("gathered", gathered),
                *shared,
                ("gain", norm_gain),
                ("skip", skip_weight),
                ("in", (in_weight, layer)),
                ("d_states", d_states),
                ("ends", ends),
                ("states", states),
                ("enter", enter),
                ("scaled", scaled),
                ("values", values),
                ("d_mixed", d_mixed),
                ("grad", grad),
                ("out", (out_weight, layer - 1)),
                ("glu", (glu_weight, layer - 1)),
                ("mixed", mixed),
                ("act", act),
                ("gate", gate),
                ("below_scaled", low_scaled),
                ("low", low),
            ),
            (
                in_out, vector, rate_out, tokens, tokens, wide_out, glu_out, out_out, vector, ends_out,
                totals_out,
            ),
            back_scratch + (tokens_low, tokens_low),
        )
        in_grads.append(in_grad)
        gain_grads.append(gain_grad)
        rate_grads.append(rate_grad)
        glu_grads.append(glu_grad)
        out_grads.append(out_grad)
        skip_grads.append(skip_grad)
        states, enter, values, scaled = low_states, low_enter, low_values, low_scaled
    gathered = gather(totals)
    in_grad, gain_grad, rate_grad, input_grad = call(
        functools.partial(back_last_kernel, length),
        "back_last",
        (
            ("place", place),
            ("gathered", gathered),
            *shared,
            ("gain", norm_gain),
            ("skip", skip_weight),
            ("in", (in_weight, 0)),
            ("d_states", d_states),
            ("ends", ends),
            ("states", states),
            ("enter", enter),
            ("scaled", scaled),
            ("values", values),
            ("d_mixed", d_mixed),
            ("grad", grad),
        ),
        (in_out, vector, rate_out, (inputs.shape, bf16)),
        back_scratch + (tokens_low,),
    )
    in_grads.append(in_grad)
    gain_grads.append(gain_grad)
    rate_grads.append(rate_grad)

    def stack(terms):
        return jnp.stack(terms[::-1])

    in_sum, out_sum, glu_sum, rate_sum, gain_sum, skip_sum = lax.psum(
        (
            stack(in_grads),
            stack(out_grads),
            stack(glu_grads),
            stack(rate_grads),
            stack(gain_grads),
            stack(skip_grads),
        ),
        ("seq", "batch"),
    )
    decay_grad, frequency_grad, step_grad = rates_back(
        tuple(rate_sum[:, member] for member in range(4))
    )
    return (
        output,
        input_grad,
        gain_sum[:, 0],
        decay_grad,
        frequency_grad,
        step_grad,
        in_sum,
        skip_sum[:, 0],
        out_sum,
        glu_sum,
    )


def solution(mesh):
    in_specs = (
        P("batch", "seq", None),
        P("batch", None),
        P(),
        P(),
        P(),
        P(),
        P(),
        P(),
        P(),
        P(),
        P("batch", "seq", None),
    )
    out_specs = (
        P("batch", "seq", None),
        P("batch", "seq", None),
        P(),
        P(),
        P(),
        P(),
        P(),
        P(),
        P(),
        P(),
    )
    return jax.shard_map(
        on_device, mesh=mesh, in_specs=in_specs, out_specs=out_specs, check_vma=False
    )
```

```python
import functools
import math

import jax
import jax.numpy as jnp
from jax import lax
from jax.experimental import pallas as pl
from jax.experimental.pallas import tpu as pltpu
from jax.sharding import PartitionSpec as P

epsilon = 1e-05
chunk_count = 8
lane_count = 128
block_rows = 32
vmem_bytes = 32 * 1024 * 1024
gelu_scale = math.sqrt(2.0 / math.pi)
gelu_cubic = 0.044715
f32 = jnp.float32
bf16 = jnp.bfloat16


def complex_mul(left_real, left_imag, right_real, right_imag):
    return (
        left_real * right_real - left_imag * right_imag,
        left_real * right_imag + left_imag * right_real,
    )


def complex_power(real, imag, exponent):
    result = None
    while exponent:
        if exponent & 1:
            result = (real, imag) if result is None else complex_mul(*result, real, imag)
        exponent >>= 1
        if exponent:
            real, imag = complex_mul(real, imag, real, imag)
    return result


def rates(decay_log, frequency, step_log):
    step_size = jnp.exp(step_log)
    pole_real = -jnp.exp(decay_log)
    shrink = step_size * pole_real
    rotation = step_size * frequency
    radius = jnp.exp(shrink)
    decay_real = radius * jnp.cos(rotation)
    decay_imag = radius * jnp.sin(rotation)
    minus_real = jnp.expm1(shrink) * jnp.cos(rotation) - 2.0 * jnp.sin(0.5 * rotation) ** 2
    modulus = pole_real * pole_real + frequency * frequency
    factor_real = (minus_real * pole_real + decay_imag * frequency) / modulus
    factor_imag = (decay_imag * pole_real - minus_real * frequency) / modulus
    return (decay_real, decay_imag, factor_real, factor_imag)


def dot(left, right):
    return lax.dot_general(left, right, (((1,), (0,)), ((), ())), preferred_element_type=f32)


def dot_right(left, right):
    return lax.dot_general(left, right, (((1,), (1,)), ((), ())), preferred_element_type=f32)


def dot_left(left, right):
    return lax.dot_general(left, right, (((0,), (0,)), ((), ())), preferred_element_type=f32)


def spread(narrow, width):
    return jnp.concatenate([narrow] * (width // lane_count), axis=1)


def order_matrix(count, inverse):
    rows = lax.broadcasted_iota(jnp.int32, (count, count), 0)
    cols = lax.broadcasted_iota(jnp.int32, (count, count), 1)
    if inverse:
        rows, cols = cols, rows
    source = lax.rem(rows, chunk_count) * (count // chunk_count) + lax.div(rows, chunk_count)
    return jnp.where(cols == source, 1.0, 0.0).astype(bf16)


def over_blocks(count, body):
    def one(index, carry):
        body(pl.ds(pl.multiple_of(index * block_rows, block_rows), block_rows))
        return carry

    lax.fori_loop(0, count // block_rows, one, 0)


def normalize(values):
    average = jnp.mean(values, axis=-1, keepdims=True)
    centered = values - average
    inverse = lax.rsqrt(jnp.mean(centered * centered, axis=-1, keepdims=True) + epsilon)
    return centered * inverse, inverse


def gelu_parts(mixed):
    square = mixed * mixed
    bend = jnp.tanh(gelu_scale * mixed * (1.0 + gelu_cubic * square))
    half = 0.5 + 0.5 * bend
    slope = half + 0.5 * mixed * (1.0 - bend * bend) * gelu_scale * (
        1.0 + 3.0 * gelu_cubic * square
    )
    return mixed * half, slope


def write_flags(place, docs_ref, flags_ref, blocks_ref, length):
    row_count, doc_count = docs_ref.shape
    span = row_count * length // chunk_count
    per_row = chunk_count // row_count
    offsets = []
    for row in range(row_count):
        running = [jnp.int32(0)]
        for doc in range(doc_count):
            running.append(running[-1] + docs_ref[row, doc])
        offsets.append(running)

    def by_row(row_of, member):
        chosen = jnp.full(row_of.shape, offsets[0][member], jnp.int32)
        for row in range(1, row_count):
            chosen = jnp.where(row_of == row, offsets[row][member], chosen)
        return chosen

    chunk = lax.broadcasted_iota(jnp.int32, (chunk_count, lane_count), 0)
    row_of = lax.div(chunk, per_row)
    bounds = [by_row(row_of, member) for member in range(doc_count + 1)]
    base = place * length + lax.rem(chunk, per_row) * span
    for step in range(span):
        position = base + step
        starts = position == bounds[0]
        endings = position + 1 == bounds[0]
        for bound in bounds[1:]:
            starts = starts | (position == bound)
            endings = endings | (position + 1 == bound)
        window = pl.ds(chunk_count * step, chunk_count)
        flags_ref[0, window, :] = jnp.where(starts, 0.0, 1.0)
        flags_ref[1, window, :] = jnp.where(endings, 0.0, 1.0)
        flags_ref[2, window, :] = jnp.where(position < bounds[-1], 1.0, 0.0)
    entry = lax.broadcasted_iota(jnp.int32, blocks_ref.shape[1:], 0)
    row_of = lax.rem(entry, row_count)
    first = lax.div(entry, row_count) * length
    starts = jnp.zeros(entry.shape, jnp.bool_)
    endings = starts
    for member in range(doc_count + 1):
        bound = by_row(row_of, member)
        starts = starts | ((bound >= first) & (bound < first + length))
        endings = endings | ((bound > first) & (bound <= first + length))
    blocks_ref[0] = jnp.where(starts, 0.0, 1.0)
    blocks_ref[1] = jnp.where(endings, 0.0, 1.0)


def chunk_keeps(flags_ref):
    span = flags_ref.shape[1] // chunk_count
    ahead = flags_ref[0, :chunk_count, :]
    behind = flags_ref[1, :chunk_count, :]
    for step in range(1, span):
        window = pl.ds(chunk_count * step, chunk_count)
        ahead = ahead * flags_ref[0, window, :]
        behind = behind * flags_ref[1, window, :]
    return ahead, behind


def toward(array, distance, reverse):
    return pltpu.roll(array, chunk_count - distance if reverse else distance, axis=0)


def chunk_prefix(ends, factor, entering, per_row, reverse):
    width = ends[0].shape[1]
    chunk = lax.broadcasted_iota(jnp.int32, (chunk_count, width), 0)
    within = lax.rem(chunk, per_row)
    within = per_row - 1 - within if reverse else within
    first = within == 0
    total_real, total_imag = ends
    if entering is not None:
        moved_real, moved_imag = complex_mul(*factor, *entering)
        total_real = total_real + jnp.where(first, moved_real, 0.0)
        total_imag = total_imag + jnp.where(first, moved_imag, 0.0)
    distance = 1
    while distance < per_row:
        reach = within >= distance
        near_real = toward(total_real, distance, reverse)
        near_imag = toward(total_imag, distance, reverse)
        moved_real, moved_imag = complex_mul(*factor, near_real, near_imag)
        total_real = total_real + jnp.where(reach, moved_real, 0.0)
        total_imag = total_imag + jnp.where(reach, moved_imag, 0.0)
        if 2 * distance < per_row:
            far_real = toward(factor[0], distance, reverse)
            far_imag = toward(factor[1], distance, reverse)
            both_real, both_imag = complex_mul(*factor, far_real, far_imag)
            factor = (
                jnp.where(reach, both_real, factor[0]),
                jnp.where(reach, both_imag, factor[1]),
            )
        distance *= 2
    enter_real = toward(total_real, 1, reverse)
    enter_imag = toward(total_imag, 1, reverse)
    none = (jnp.zeros_like(total_real),) * 2 if entering is None else entering
    return (
        (total_real, total_imag),
        (jnp.where(first, none[0], enter_real), jnp.where(first, none[1], enter_imag)),
    )


def sweep(flags_ref, pole_real, pole_imag, forward_at, reverse_at, start, put_forward, put_reverse):
    width = pole_real.shape[1]
    span = flags_ref.shape[1] // chunk_count

    def one(step, state):
        ahead_real, ahead_imag, behind_real, behind_imag = state
        here = pl.ds(pl.multiple_of(chunk_count * step, chunk_count), chunk_count)
        there = pl.ds(pl.multiple_of(chunk_count * (span - 1 - step), chunk_count), chunk_count)
        keep = spread(flags_ref[0, here, :], width)
        moved_real, moved_imag = complex_mul(pole_real * keep, pole_imag * keep, ahead_real, ahead_imag)
        drive_real, drive_imag = forward_at(here)
        ahead_real = moved_real + drive_real
        ahead_imag = moved_imag + drive_imag
        keep = spread(flags_ref[1, there, :], width)
        moved_real, moved_imag = complex_mul(
            pole_real * keep, pole_imag * keep, behind_real, behind_imag
        )
        drive_real, drive_imag = reverse_at(there)
        behind_real = moved_real + drive_real
        behind_imag = moved_imag + drive_imag
        if put_forward is not None:
            put_forward(here, ahead_real, ahead_imag)
            put_reverse(there, behind_real, behind_imag)
        return (ahead_real, ahead_imag, behind_real, behind_imag)

    return lax.fori_loop(0, span, one, start, unroll=4)


def local_totals(flags_ref, pole_real, pole_imag, forward_at, reverse_at, ends_ref, totals_ref):
    width = pole_real.shape[1]
    span = flags_ref.shape[1] // chunk_count
    row_count = totals_ref.shape[0] // 4
    per_row = chunk_count // row_count
    pole_real = jnp.broadcast_to(pole_real, (chunk_count, width))
    pole_imag = jnp.broadcast_to(pole_imag, (chunk_count, width))
    zero = jnp.zeros((chunk_count, width), f32)
    ends = sweep(
        flags_ref, pole_real, pole_imag, forward_at, reverse_at, (zero,) * 4, None, None
    )
    for member in range(4):
        ends_ref[:, member * width : (member + 1) * width] = ends[member]
    power_real, power_imag = complex_power(pole_real, pole_imag, span)
    for direction, keep in enumerate(chunk_keeps(flags_ref)):
        keep = spread(keep, width)
        pair = ends[2 * direction : 2 * direction + 2]
        totals, unused = chunk_prefix(
            pair, (power_real * keep, power_imag * keep), None, per_row, direction == 1
        )
        for part in range(2):
            for row in range(row_count):
                chunk = row * per_row if direction == 1 else (row + 1) * per_row - 1
                entry = (2 * direction + part) * row_count + row
                totals_ref[entry : entry + 1, :] = totals[part][chunk : chunk + 1, :]


def chunk_entrances(place, gathered_ref, flags_ref, blocks_ref, ends_ref, pole_real, pole_imag, length):
    width = pole_real.shape[1]
    span = flags_ref.shape[1] // chunk_count
    row_count = chunk_count * span // length
    per_row = chunk_count // row_count
    device_count = gathered_ref.shape[0] // (4 * row_count)
    pole_real = jnp.broadcast_to(pole_real, (chunk_count, width))
    pole_imag = jnp.broadcast_to(pole_imag, (chunk_count, width))
    power_real, power_imag = complex_power(pole_real, pole_imag, span)
    device_real, device_imag = complex_power(power_real, power_imag, per_row)
    device_real = device_real[:row_count]
    device_imag = device_imag[:row_count]
    entrances = []
    for direction, keep in enumerate(chunk_keeps(flags_ref)):
        real = jnp.zeros((row_count, width), f32)
        imag = real
        for lap in range(device_count):
            source = device_count - 1 - lap if direction == 1 else lap
            live = source > place if direction == 1 else source < place
            open_ = spread(
                blocks_ref[direction, source * row_count : (source + 1) * row_count, :], width
            )
            moved_real, moved_imag = complex_mul(device_real * open_, device_imag * open_, real, imag)
            first = (4 * source + 2 * direction) * row_count
            moved_real = moved_real + gathered_ref[first : first + row_count, :]
            moved_imag = moved_imag + gathered_ref[first + row_count : first + 2 * row_count, :]
            real = jnp.where(live, moved_real, real)
            imag = jnp.where(live, moved_imag, imag)
        entering = tuple(
            jnp.concatenate(
                [
                    jnp.broadcast_to(part[row : row + 1, :], (per_row, width))
                    for row in range(row_count)
                ],
                axis=0,
            )
            for part in (real, imag)
        )
        keep = spread(keep, width)
        first = 2 * direction * width
        ends = (ends_ref[:, first : first + width], ends_ref[:, first + width : first + 2 * width])
        unused, entrance = chunk_prefix(
            ends, (power_real * keep, power_imag * keep), entering, per_row, direction == 1
        )
        entrances.extend(entrance)
    return tuple(entrances)


def layer_poles(tables_ref, layer):
    return tables_ref[4 * layer : 4 * layer + 1, :], tables_ref[4 * layer + 1 : 4 * layer + 2, :]


def layer_factors(tables_ref, layer):
    return tables_ref[4 * layer + 2 : 4 * layer + 3, :], tables_ref[4 * layer + 3 : 4 * layer + 4, :]


def write_bar(tables_ref, layer, in_ref, bar_ref):
    width = tables_ref.shape[1]
    factor_real, factor_imag = layer_factors(tables_ref, layer)

    def body(rows):
        weight_real = in_ref[rows, :width].astype(f32)
        weight_imag = in_ref[rows, width:].astype(f32)
        real, imag = complex_mul(factor_real, factor_imag, weight_real, weight_imag)
        bar_ref[rows, :width] = real.astype(bf16)
        bar_ref[rows, width:] = imag.astype(bf16)

    over_blocks(in_ref.shape[0], body)


def pair_at(ref, first, width):
    def at(rows):
        return ref[rows, first : first + width], ref[rows, first + width : first + 2 * width]

    return at


def drive_totals(flags_ref, tables_ref, layer, scaled_ref, in_ref, bar_ref, drive_ref, ends_ref, totals_ref):
    width = tables_ref.shape[1]
    write_bar(tables_ref, layer, in_ref.ready(), bar_ref)
    drive_ref[...] = dot(scaled_ref[...], bar_ref[...])
    at = pair_at(drive_ref, 0, width)
    local_totals(flags_ref, *layer_poles(tables_ref, layer), at, at, ends_ref, totals_ref)


def settled_states(
    place, gathered_ref, flags_ref, blocks_ref, tables_ref, layer, drive_ref, ends_ref, length,
    states_ref, low_ref, enter_ref,
):
    width = tables_ref.shape[1]
    pole_real, pole_imag = layer_poles(tables_ref, layer)
    entrances = chunk_entrances(
        place, gathered_ref, flags_ref, blocks_ref, ends_ref, pole_real, pole_imag, length
    )
    for member in range(4):
        enter_ref[:, member * width : (member + 1) * width] = entrances[member]

    def put_forward(rows, real, imag):
        states_ref[rows, :width] = real
        states_ref[rows, width : 2 * width] = imag

    def put_reverse(rows, real, imag):
        states_ref[rows, 2 * width : 3 * width] = real
        states_ref[rows, 3 * width :] = imag

    at = pair_at(drive_ref, 0, width)
    sweep(
        flags_ref,
        jnp.broadcast_to(pole_real, (chunk_count, width)),
        jnp.broadcast_to(pole_imag, (chunk_count, width)),
        at, at, entrances, put_forward, put_reverse,
    )

    def body(rows):
        low_ref[rows, :] = states_ref[rows, :].astype(bf16)

    over_blocks(states_ref.shape[0], body)


def mix_and_gate(layer, low_ref, scaled_ref, out_ref, glu_ref, skip_ref, mixed_ref, act_ref, gate_ref):
    mixed_ref[...] = dot(low_ref[...], out_ref.ready()[...])
    skip = skip_ref[layer : layer + 1, :]

    def body(rows):
        mixed = mixed_ref[rows, :] + skip * scaled_ref[rows, :].astype(f32)
        mixed_ref[rows, :] = mixed
        act_ref[rows, :] = gelu_parts(mixed)[0].astype(bf16)

    over_blocks(mixed_ref.shape[0], body)
    gate_ref[...] = dot(act_ref[...], glu_ref.ready()[...])


def back_tail(
    layer, flags_ref, tables_ref, grad_ref, mixed_ref, act_ref, gate_ref, scaled_ref, low_ref,
    out_ref, glu_ref, skip_ref, logits_ref, work_ref, mixed_low_ref,
    d_mixed_ref, d_states_ref, glu_grad_ref, out_grad_ref, skip_grad_ref, ends_ref, totals_ref, emit,
):
    width = tables_ref.shape[1]
    model = mixed_ref.shape[1]

    def first(rows):
        valid = spread(flags_ref[2, rows, :], model)
        gate = gate_ref[rows, :]
        rate = grad_ref[rows, :] * valid * gate
        logits_ref[rows, :] = (rate * act_ref[rows, :].astype(f32) * (1.0 - gate)).astype(bf16)

    over_blocks(mixed_ref.shape[0], first)
    glu_grad_ref[...] = dot_left(act_ref[...], logits_ref[...])
    emit.put("glu", glu_grad_ref)
    work_ref[...] = dot_right(logits_ref[...], glu_ref.ready()[...])
    skip_grad_ref[...] = jnp.zeros(skip_grad_ref.shape, f32)

    def second(rows):
        valid = spread(flags_ref[2, rows, :], model)
        d_act = grad_ref[rows, :] * valid * gate_ref[rows, :] + work_ref[rows, :]
        d_mixed = d_act * gelu_parts(mixed_ref[rows, :])[1]
        d_mixed_ref[rows, :] = d_mixed
        mixed_low_ref[rows, :] = d_mixed.astype(bf16)
        skip_grad_ref[...] += jnp.sum(
            d_mixed * scaled_ref[rows, :].astype(f32), axis=0, keepdims=True
        )

    over_blocks(mixed_ref.shape[0], second)
    out_grad_ref[...] = dot_left(low_ref[...], mixed_low_ref[...])
    emit.put("out", out_grad_ref)
    d_states_ref[...] = dot_right(mixed_low_ref[...], out_ref.ready()[...])
    pole_real, pole_imag = layer_poles(tables_ref, layer)
    local_totals(
        flags_ref, pole_real, -pole_imag, pair_at(d_states_ref, 2 * width, width),
        pair_at(d_states_ref, 0, width), ends_ref, totals_ref,
    )


def back_front(
    place, layer, length, gathered_ref, flags_ref, blocks_ref, tables_ref, gain_ref, skip_ref, in_ref,
    d_states_ref, ends_ref, states_ref, enter_ref, scaled_ref, values_ref, d_mixed_ref, grad_ref,
    lam_ref, mu_ref, low_ref, bar_ref, work_ref,
    in_grad_ref, gain_grad_ref, rate_grad_ref, put_gradient, emit,
):
    width = tables_ref.shape[1]
    model = values_ref.shape[1]
    count = values_ref.shape[0]
    pole_real, pole_imag = layer_poles(tables_ref, layer)
    entrances = chunk_entrances(
        place, gathered_ref, flags_ref, blocks_ref, ends_ref, pole_real, -pole_imag, length
    )

    def put_forward(rows, real, imag):
        mu_ref[rows, :width] = real
        mu_ref[rows, width:] = imag

    def put_reverse(rows, real, imag):
        lam_ref[rows, :width] = real
        lam_ref[rows, width:] = imag

    sweep(
        flags_ref,
        jnp.broadcast_to(pole_real, (chunk_count, width)),
        jnp.broadcast_to(-pole_imag, (chunk_count, width)),
        pair_at(d_states_ref, 2 * width, width), pair_at(d_states_ref, 0, width),
        entrances, put_forward, put_reverse,
    )
    span = count // chunk_count

    def decay_terms(here, before_real, before_imag, after_real, after_imag, sums):
        keep = spread(flags_ref[0, here, :], width)
        lam_real, lam_imag = lam_ref[here, :width], lam_ref[here, width:]
        mu_real, mu_imag = mu_ref[here, :width], mu_ref[here, width:]
        real = keep * (lam_real * before_real + lam_imag * before_imag)
        imag = keep * (lam_imag * before_real - lam_real * before_imag)
        keep = spread(flags_ref[1, here, :], width)
        real = real + keep * (mu_real * after_real + mu_imag * after_imag)
        imag = imag + keep * (mu_imag * after_real - mu_real * after_imag)
        return sums[0] + real, sums[1] + imag

    def window(step):
        start = chunk_count * step
        return pl.ds(start if isinstance(step, int) else pl.multiple_of(start, chunk_count), chunk_count)

    def before_at(step):
        rows = window(step)
        return states_ref[rows, :width], states_ref[rows, width : 2 * width]

    def after_at(step):
        rows = window(step)
        return states_ref[rows, 2 * width : 3 * width], states_ref[rows, 3 * width :]

    def middle(step, sums):
        return decay_terms(window(step), *before_at(step - 1), *after_at(step + 1), sums)

    zero = jnp.zeros((chunk_count, width), f32)
    sums = decay_terms(
        window(0), enter_ref[:, :width], enter_ref[:, width : 2 * width], *after_at(1), (zero, zero)
    )
    sums = lax.fori_loop(1, span - 1, middle, sums, unroll=2)
    sums = decay_terms(
        window(span - 1), *before_at(span - 2),
        enter_ref[:, 2 * width : 3 * width], enter_ref[:, 3 * width :], sums,
    )
    rate_grad_ref[0:1, :] = jnp.sum(sums[0], axis=0, keepdims=True)
    rate_grad_ref[1:2, :] = jnp.sum(sums[1], axis=0, keepdims=True)

    def narrow(rows):
        low_ref[rows, :] = (lam_ref[rows, :] + mu_ref[rows, :]).astype(bf16)

    over_blocks(count, narrow)
    in_ref = in_ref.ready()
    write_bar(tables_ref, layer, in_ref, bar_ref)
    work_ref[...] = dot_right(low_ref[...], bar_ref[...])
    skip = skip_ref[layer : layer + 1, :]
    gain = gain_ref[layer : layer + 1, :]
    gain_grad_ref[...] = jnp.zeros(gain_grad_ref.shape, f32)

    def norm_back(rows):
        valid = spread(flags_ref[2, rows, :], model)
        normed, inverse = normalize(values_ref[rows, :].astype(f32))
        d_scaled = (work_ref[rows, :] + d_mixed_ref[rows, :] * skip) * valid
        gain_grad_ref[...] += jnp.sum(d_scaled * normed, axis=0, keepdims=True)
        d_normed = d_scaled * gain
        put_gradient(
            rows,
            inverse
            * (
                d_normed
                - jnp.mean(d_normed, axis=-1, keepdims=True)
                - normed * jnp.mean(d_normed * normed, axis=-1, keepdims=True)
            )
            + grad_ref[rows, :].astype(f32),
        )

    over_blocks(count, norm_back)
    in_grad_ref[...] = dot_left(scaled_ref[...], low_ref[...])
    factor_real, factor_imag = layer_factors(tables_ref, layer)
    rate_grad_ref[2:4, :] = jnp.zeros((2, width), f32)

    def weigh(rows):
        grad_real, grad_imag = in_grad_ref[rows, :width], in_grad_ref[rows, width:]
        weight_real = in_ref[rows, :width].astype(f32)
        weight_imag = in_ref[rows, width:].astype(f32)
        rate_grad_ref[2:3, :] += jnp.sum(
            grad_real * weight_real + grad_imag * weight_imag, axis=0, keepdims=True
        )
        rate_grad_ref[3:4, :] += jnp.sum(
            grad_imag * weight_real - grad_real * weight_imag, axis=0, keepdims=True
        )
        in_grad_ref[rows, :width] = factor_real * grad_real + factor_imag * grad_imag
        in_grad_ref[rows, width:] = factor_real * grad_imag - factor_imag * grad_real

    over_blocks(in_ref.shape[0], weigh)
    emit.put("in", in_grad_ref)


def first_kernel(
    length, place_ref, docs_ref, inputs_ref, gain_ref, tables_ref, in_ref,
    flags_ref, blocks_ref, values_ref, scaled_ref, drive_ref, ends_ref, totals_ref, bar_ref,
):
    write_flags(place_ref[0], docs_ref, flags_ref, blocks_ref, length)
    count, model = values_ref.shape
    values_ref[...] = dot(
        order_matrix(count, False), inputs_ref[...].reshape(count, model)
    ).astype(bf16)
    gain = gain_ref[0:1, :]

    def body(rows):
        normed, unused = normalize(values_ref[rows, :].astype(f32))
        valid = spread(flags_ref[2, rows, :], model)
        scaled_ref[rows, :] = (normed * gain * valid).astype(bf16)

    over_blocks(count, body)
    drive_totals(
        flags_ref, tables_ref, 0, scaled_ref, in_ref, bar_ref, drive_ref, ends_ref, totals_ref
    )


def middle_kernel(
    layer, length, place_ref, gathered_ref, flags_ref, blocks_ref, tables_ref, gain_ref, skip_ref,
    drive_ref, ends_ref, values_ref, scaled_ref, out_ref, glu_ref, in_ref,
    states_ref, low_ref, enter_ref, mixed_ref, act_ref, gate_ref,
    next_values_ref, next_scaled_ref, next_drive_ref, next_ends_ref, next_totals_ref, bar_ref,
):
    settled_states(
        place_ref[0], gathered_ref, flags_ref, blocks_ref, tables_ref, layer, drive_ref, ends_ref, length,
        states_ref, low_ref, enter_ref,
    )
    mix_and_gate(
        layer, low_ref, scaled_ref, out_ref, glu_ref, skip_ref, mixed_ref, act_ref, gate_ref
    )
    model = values_ref.shape[1]
    gain = gain_ref[layer + 1 : layer + 2, :]

    def body(rows):
        valid = spread(flags_ref[2, rows, :], model)
        gate = jax.nn.sigmoid(gate_ref[rows, :])
        gate_ref[rows, :] = gate
        result = values_ref[rows, :].astype(f32) + valid * act_ref[rows, :].astype(f32) * gate
        next_values_ref[rows, :] = result
        normed, unused = normalize(result)
        next_scaled_ref[rows, :] = (normed * gain * valid).astype(bf16)

    over_blocks(values_ref.shape[0], body)
    drive_totals(
        flags_ref, tables_ref, layer + 1, next_scaled_ref, in_ref, bar_ref, next_drive_ref,
        next_ends_ref, next_totals_ref,
    )


def turn_kernel(
    layer, length, place_ref, gathered_ref, flags_ref, blocks_ref, tables_ref, skip_ref,
    drive_ref, ends_ref, values_ref, scaled_ref, out_ref, glu_ref, cotangent_ref,
    output_ref, grad_ref, states_ref, enter_ref, d_mixed_ref, d_states_ref,
    keep_ref, send_ref, skip_grad_ref, back_ends_ref, back_totals_ref,
    low_ref, mixed_ref, act_ref, gate_ref, result_ref, logits_ref, work_ref, mixed_low_ref,
    glu_grad_ref, out_grad_ref,
):
    emit = Emit(tail_layout(values_ref.shape[1], tables_ref.shape[1]), keep_ref, send_ref)
    settled_states(
        place_ref[0], gathered_ref, flags_ref, blocks_ref, tables_ref, layer, drive_ref, ends_ref, length,
        states_ref, low_ref, enter_ref,
    )
    mix_and_gate(
        layer, low_ref, scaled_ref, out_ref, glu_ref, skip_ref, mixed_ref, act_ref, gate_ref
    )
    count, model = values_ref.shape

    def body(rows):
        valid = spread(flags_ref[2, rows, :], model)
        gate = jax.nn.sigmoid(gate_ref[rows, :])
        gate_ref[rows, :] = gate
        result = values_ref[rows, :] + valid * act_ref[rows, :].astype(f32) * gate
        result_ref[rows, :] = result.astype(bf16)

    over_blocks(count, body)
    output_ref[...] = (
        dot(order_matrix(count, True), result_ref[...]).astype(bf16).reshape(output_ref.shape)
    )
    grad_ref[...] = dot(order_matrix(count, False), cotangent_ref[...].reshape(count, model))
    back_tail(
        layer, flags_ref, tables_ref, grad_ref, mixed_ref, act_ref, gate_ref, scaled_ref, low_ref,
        out_ref, glu_ref, skip_ref, logits_ref, work_ref, mixed_low_ref,
        d_mixed_ref, d_states_ref, glu_grad_ref, out_grad_ref, skip_grad_ref, back_ends_ref,
        back_totals_ref, emit,
    )


def back_middle_kernel(
    layer, length, place_ref, gathered_ref, flags_ref, blocks_ref, tables_ref, gain_ref, skip_ref, in_ref,
    d_states_ref, ends_ref, states_ref, enter_ref, scaled_ref, values_ref, d_mixed_ref, grad_ref,
    out_ref, glu_ref, below_mixed_ref, below_act_ref, below_gate_ref, below_scaled_ref, below_low_ref,
    keep_ref, send_ref, in_keep_ref, in_send_ref, gain_grad_ref, rate_grad_ref, next_grad_ref,
    below_d_mixed_ref,
    below_d_states_ref, skip_grad_ref, below_ends_ref, below_totals_ref,
    lam_ref, mu_ref, low_ref, bar_ref, work_ref, logits_ref, mixed_low_ref,
    in_grad_ref, glu_grad_ref, out_grad_ref,
):
    model, width = values_ref.shape[1], tables_ref.shape[1]
    emit = Emit(tail_layout(model, width), keep_ref, send_ref)
    in_emit = Emit(in_layout(model, width), in_keep_ref, in_send_ref)

    def put_gradient(rows, gradient):
        next_grad_ref[rows, :] = gradient

    back_front(
        place_ref[0], layer, length, gathered_ref, flags_ref, blocks_ref, tables_ref, gain_ref, skip_ref,
        in_ref, d_states_ref, ends_ref, states_ref, enter_ref, scaled_ref, values_ref, d_mixed_ref,
        grad_ref, lam_ref, mu_ref, low_ref, bar_ref, work_ref,
        in_grad_ref, gain_grad_ref, rate_grad_ref, put_gradient, in_emit,
    )
    back_tail(
        layer - 1, flags_ref, tables_ref, next_grad_ref, below_mixed_ref, below_act_ref, below_gate_ref,
        below_scaled_ref, below_low_ref, out_ref, glu_ref, skip_ref, logits_ref, work_ref, mixed_low_ref,
        below_d_mixed_ref, below_d_states_ref, glu_grad_ref, out_grad_ref, skip_grad_ref,
        below_ends_ref, below_totals_ref, emit,
    )


def back_last_kernel(
    length, place_ref, gathered_ref, flags_ref, blocks_ref, tables_ref, gain_ref, skip_ref, in_ref,
    d_states_ref, ends_ref, states_ref, enter_ref, scaled_ref, values_ref, d_mixed_ref, grad_ref,
    *rest,
):
    layer_count = gain_ref.shape[0]
    skip_grads = rest[:layer_count]
    rest = rest[layer_count:]
    gain_grads = rest[: layer_count - 1]
    rate_grads = rest[layer_count - 1 : 2 * layer_count - 2]
    (
        keep_ref, send_ref, input_grad_ref,
        lam_ref, mu_ref, low_ref, bar_ref, work_ref, result_ref,
        in_grad_ref, gain_grad_ref, rate_grad_ref, small_ref,
    ) = rest[2 * layer_count - 2 :]
    emit = Emit(last_layout(values_ref.shape[1], tables_ref.shape[1]), keep_ref, send_ref)
    def put_gradient(rows, gradient):
        result_ref[rows, :] = gradient.astype(bf16)

    back_front(
        place_ref[0], 0, length, gathered_ref, flags_ref, blocks_ref, tables_ref, gain_ref, skip_ref,
        in_ref, d_states_ref, ends_ref, states_ref, enter_ref, scaled_ref, values_ref, d_mixed_ref,
        grad_ref, lam_ref, mu_ref, low_ref, bar_ref, work_ref,
        in_grad_ref, gain_grad_ref, rate_grad_ref, put_gradient, emit,
    )
    small_ref[...] = jnp.zeros(small_ref.shape, f32)
    row = 0
    for vectors in ((gain_grad_ref, *gain_grads), skip_grads, (rate_grad_ref, *rate_grads)):
        for vector_ref in vectors:
            for line in range(vector_ref.shape[0]):
                for first in range(0, vector_ref.shape[1], lane_count):
                    small_ref[row : row + 1, :] = vector_ref[line : line + 1, first : first + lane_count]
                    row += 1
    emit.put("small", small_ref)
    count = result_ref.shape[0]
    input_grad_ref[...] = (
        dot(order_matrix(count, True), result_ref[...]).astype(bf16).reshape(input_grad_ref.shape)
    )


halvings = 3
half_blocks = 1 << halvings
tail_kind = "plane"
in_kind = "plane"
last_kind = "plane"
round_order = "bacdbacdbcadbcadbcadbcdacbdcdc"


def mesh_bits():
    seq_bits = lax.axis_size("seq").bit_length() - 1
    batch_bits = lax.axis_size("batch").bit_length() - 1
    deep = [1 << place for place in range(batch_bits)]
    core = 1 << batch_bits
    plane = [core << place for place in range(1, seq_bits)]
    return deep, core, plane[: len(plane) // 2], plane[len(plane) // 2 :]


def axis_orders(kind):
    deep, core, across, along = mesh_bits()
    orders = {
        "plane": (across + along + deep, along + across + deep),
        "deep": (deep + across + along, deep + along + across),
        "mixed": (across + along + deep, along + deep + across),
    }
    return core, orders[kind]


def half_bases(kind):
    core, orders = axis_orders(kind)
    index = lax.axis_index("seq") * lax.axis_size("batch") + lax.axis_index("batch")
    side = lax.rem(lax.div(index, core), 2)
    numbers = []
    for order in orders:
        number = 0
        for bit in order[:halvings]:
            number = 2 * number + lax.rem(lax.div(index, bit), 2)
        numbers.append(number)
    keep = (1 - side) * numbers[0] + side * numbers[1]
    send = (1 - side) * numbers[1] + side * numbers[0]
    return side * half_blocks + keep, (1 - side) * half_blocks + send


def swap(array, first, second):
    core = mesh_bits()[1]
    total = lax.axis_size("seq") * lax.axis_size("batch")
    pairs = [(index, index ^ (second if index & core else first)) for index in range(total)]
    return lax.ppermute(array, ("seq", "batch"), pairs)


class UnitSum:
    def __init__(self, keep, send, kind):
        self.core, orders = axis_orders(kind)
        self.steps = list(zip(*orders))
        self.parts = [keep]
        self.top = keep.shape[0]
        self.runs = None
        self.rounds = self.plan(send)
        self.outgoing = next(self.rounds)

    def added(self, low, high):
        total = self.parts[0][low:high]
        for part in self.parts[1:]:
            total = total + part[low:high]
        return total

    def plan(self, send):
        sent = yield send
        self.parts.append(swap(sent, self.core, self.core))
        for step, (first, second) in enumerate(self.steps):
            if step < halvings:
                self.top //= 2
                sent = yield self.added(self.top, 2 * self.top)
                self.parts.append(swap(sent, first, second))
            else:
                own = yield self.added(0, self.top)
                self.parts = [own, swap(own, first, second)]
        full = self.added(0, self.top)
        for first, second in self.steps[halvings - 1 : 0 : -1]:
            full = yield full
            full = jnp.concatenate([full, swap(full, first, second)])
        full = yield full
        rest = swap(full, *self.steps[0])
        other = swap(full, self.core, self.core)
        rest = yield rest
        self.runs = (full, rest, other, swap(rest, self.core, self.core))
        yield None

    def launch(self, sent):
        self.outgoing = self.rounds.send(sent)


class Line:
    def __init__(self):
        self.last = ()

    def advance(self, units, payload=()):
        units = [unit for unit in units if unit.runs is None]
        sends, payload, unused = lax.optimization_barrier(
            ([unit.outgoing for unit in units], payload, self.last)
        )
        for unit, sent in zip(units, sends):
            unit.launch(sent)
        self.last = sends
        return payload


def aligned(first, rows):
    return pl.ds(pl.multiple_of(first, 8), rows)


class Layout:
    def __init__(self, rows, columns, kind):
        self.rows, self.columns, self.kind = rows, columns, kind
        self.sections = {}

    def add(self, key, array_rows, array_first, block_first, count, columns=slice(None)):
        self.sections.setdefault(key, []).append(
            (
                lambda owner: (aligned(owner * array_rows + array_first, count), slice(None)),
                lambda place: (aligned(place * self.rows + block_first, count), columns),
            )
        )

    def half(self):
        return ((half_blocks * self.rows, self.columns), f32)


def tail_layout(model, width):
    out_rows = 4 * width // (2 * half_blocks)
    glu_rows = model // (2 * half_blocks)
    layout = Layout(out_rows + glu_rows, model, tail_kind)
    layout.add("out", out_rows, 0, 0, out_rows)
    layout.add("glu", glu_rows, 0, out_rows, glu_rows)
    return layout


def in_layout(model, width):
    rows = model // (2 * half_blocks)
    layout = Layout(rows, 2 * width, in_kind)
    layout.add("in", rows, 0, 0, rows)
    return layout


def last_layout(model, width):
    rows = model // (2 * half_blocks)
    pieces = rows // 8
    wide = 2 * width
    layout = Layout(8, pieces * wide + lane_count, last_kind)
    for piece in range(pieces):
        layout.add("in", rows, 8 * piece, 0, 8, slice(piece * wide, (piece + 1) * wide))
    layout.add("small", 8, 0, 0, 8, slice(pieces * wide, pieces * wide + lane_count))
    return layout


class Emit:
    def __init__(self, layout, keep_ref, send_ref):
        self.sections = layout.sections
        self.halves = (keep_ref, send_ref)
        self.bases = half_bases(layout.kind)

    def put(self, key, array_ref):
        def one(place, carry):
            for half in (1, 0):
                owner = lax.bitwise_xor(self.bases[half], place)
                for array_at, block_at in self.sections[key]:
                    self.halves[half][block_at(place)] = array_ref[array_at(owner)]
            return carry

        lax.fori_loop(0, half_blocks, one, 0)


run_places = ((0, 0), (0, half_blocks // 2), (1, 0), (1, half_blocks // 2))


def place_kernel(layouts, goals, *refs):
    outs = refs[len(refs) - 1 - len(goals) : -1]
    semaphores = refs[-1]
    targets = []
    for out, writes in zip(outs, goals):
        targets.append([out if layer is None else out.at[layer] for unused, unused_too, layer in writes])
    for unit, layout in enumerate(layouts):
        bases = half_bases(layout.kind)
        for run, (half, first) in zip(refs[4 * unit : 4 * unit + 4], run_places):

            def one(place, carry, run=run, half=half, first=first, unit=unit, layout=layout):
                owner = lax.bitwise_xor(bases[half], first + place)
                for index, writes in enumerate(goals):
                    for target, (source, key, unused) in zip(targets[index], writes):
                        if source != unit:
                            continue
                        for array_at, block_at in layout.sections[key]:
                            pltpu.make_async_copy(
                                run.at[block_at(place)],
                                target.at[array_at(owner)],
                                semaphores.at[index],
                            ).start()
                return carry

            lax.fori_loop(0, half_blocks // 2, one, 0)
    for index, group in enumerate(targets):
        for target in group:
            pltpu.make_async_copy(target, target, semaphores.at[index]).wait()


def place_units(name, units, goals, sums):
    operands = []
    aliases = {}
    for unit, unused in units:
        operands.extend(("run", run) for run in unit.runs)
    for index, (key, unused, unused_too) in enumerate(goals):
        if key in sums:
            aliases[len(operands)] = index
            operands.append(("before", (sums[key], None)))
    outs = call(
        functools.partial(
            place_kernel, [layout for unused, layout in units], [writes for *unused, writes in goals]
        ),
        name,
        operands,
        tuple((shape, f32) for unused, shape, unused_too in goals),
        (pltpu.SemaphoreType.DMA((len(goals),)),),
        written=range(len(goals)),
        aliases=aliases,
        plain=True,
    )
    for (key, unused, unused_too), out in zip(goals, outs):
        sums[key] = out


class Fetch:
    def __init__(self, stack_ref, layer, target, semaphore):
        self.copy = pltpu.make_async_copy(stack_ref.at[layer], target, semaphore)
        self.target = target
        self.waiting = True
        self.copy.start()

    def ready(self):
        if self.waiting:
            self.copy.wait()
            self.waiting = False
        return self.target


def call(body, name, operands, outs, scratch, written=(), aliases=None, plain=False, micros=4, final=()):
    scalars = {"place", "docs"}
    arrays = []
    specs = []
    layers = {}
    for position, (key, operand) in enumerate(operands):
        space = pltpu.SMEM if key in scalars else pltpu.VMEM
        if isinstance(operand, tuple):
            operand, layer = operand
            if layer is not None:
                layers[position] = layer
            space = pl.ANY
        specs.append(pl.BlockSpec(memory_space=space))
        arrays.append(operand)
    fetched = [
        pltpu.VMEM(arrays[position].shape[1:], arrays[position].dtype) for position in layers
    ]

    def kernel(*refs):
        if plain:
            body(*refs)
            return
        given = list(refs[: len(arrays)])
        rest = refs[len(arrays) : len(refs) - len(fetched) - 1]
        targets = refs[len(refs) - len(fetched) - 1 : -1]
        for index, (position, layer) in enumerate(layers.items()):
            given[position] = Fetch(given[position], layer, targets[index], refs[-1].at[index])
        body(*given, *rest)

    return pl.pallas_call(
        kernel,
        name=name,
        in_specs=specs,
        out_specs=[
            pl.BlockSpec(memory_space=pl.ANY if place in written else pltpu.VMEM)
            for place in range(len(outs))
        ],
        out_shape=[
            jax.ShapeDtypeStruct(shape, kind)
            if place in written or place in final
            else pltpu.VMEM(shape, kind)
            for place, (shape, kind) in enumerate(outs)
        ],
        scratch_shapes=[
            entry if not isinstance(entry, tuple) else pltpu.VMEM(*entry) for entry in scratch
        ]
        + fetched
        + ([] if plain else [pltpu.SemaphoreType.DMA((max(1, len(fetched)),))]),
        input_output_aliases=aliases or {},
        cost_estimate=pl.CostEstimate(
            flops=micros * 1_000_000_000, bytes_accessed=micros * 3_600_000, transcendentals=0
        ),
        compiler_params=pltpu.CompilerParams(vmem_limit_bytes=vmem_bytes),
    )(*arrays)


def on_device(
    inputs,
    doc_lengths,
    norm_gain,
    decay_log,
    frequency,
    step_log,
    in_weight,
    skip_weight,
    out_weight,
    glu_weight,
    cotangent,
):
    row_count, length, model = inputs.shape
    layer_count, width = decay_log.shape
    count = row_count * length
    device_count = lax.axis_size("seq")
    place = lax.axis_index("seq").astype(jnp.int32).reshape(1)
    rate_tables, rates_back = jax.vjp(rates, decay_log, frequency, step_log)
    tables = jnp.stack(rate_tables, axis=1).reshape(4 * layer_count, width)

    def gather(totals):
        return lax.all_gather(totals, "seq", axis=0, tiled=True)

    flags_out = ((3, count, lane_count), f32)
    blocks_out = ((2, device_count * row_count, lane_count), f32)
    wide_out = ((count, 4 * width), f32)
    ends_out = ((chunk_count, 4 * width), f32)
    totals_out = ((4 * row_count, width), f32)
    tokens = ((count, model), f32)
    tokens_low = ((count, model), bf16)
    drive_out = ((count, 2 * width), f32)
    bar_out = ((model, 2 * width), bf16)
    glu_out = ((model, model), f32)
    out_out = ((4 * width, model), f32)
    in_out = ((model, 2 * width), f32)
    vector = ((1, model), f32)

    flags, blocks, values, scaled, drive, ends, totals = call(
        functools.partial(first_kernel, length),
        "first",
        (
            ("place", place),
            ("docs", doc_lengths),
            ("inputs", inputs),
            ("gain", norm_gain),
            ("tables", tables),
            ("in", (in_weight, 0)),
        ),
        (flags_out, blocks_out, tokens_low, tokens_low, drive_out, ends_out, totals_out),
        (bar_out,),
    )
    shared = (("flags", flags), ("blocks", blocks), ("tables", tables))
    kept = []
    for layer in range(layer_count - 1):
        gathered = gather(totals)
        (
            states, low, enter, mixed, act, gate, next_values, next_scaled, drive, ends, totals,
        ) = call(
            functools.partial(middle_kernel, layer, length),
            "middle",
            (
                ("place", place),
                ("gathered", gathered),
                *shared,
                ("gain", norm_gain),
                ("skip", skip_weight),
                ("drive", drive),
                ("ends", ends),
                ("values", values),
                ("scaled", scaled),
                ("out", (out_weight, layer)),
                ("glu", (glu_weight, layer)),
                ("in", (in_weight, layer + 1)),
            ),
            (
                wide_out, ((count, 4 * width), bf16), ends_out, tokens, tokens_low, tokens,
                tokens, tokens_low, drive_out, ends_out, totals_out,
            ),
            (bar_out,),
        )
        kept.append((states, low, enter, mixed, act, gate, values, scaled))
        values, scaled = next_values, next_scaled
    layer = layer_count - 1
    gathered = gather(totals)

    whole = {"out": (layer_count, 4 * width, model), "glu": (layer_count, model, model)}
    whole["in"] = (layer_count, model, 2 * width)
    sums = {}
    tail_part = tail_layout(model, width)
    in_part = in_layout(model, width)
    last_part = last_layout(model, width)
    line = Line()
    (
        output, grad, states, enter, d_mixed, d_states, keep, send, skip_grad, ends, totals,
    ) = call(
        functools.partial(turn_kernel, layer, length),
        "turn",
        (
            ("place", place),
            ("gathered", gathered),
            *shared,
            ("skip", skip_weight),
            ("drive", drive),
            ("ends", ends),
            ("values", values),
            ("scaled", scaled),
            ("out", (out_weight, layer)),
            ("glu", (glu_weight, layer)),
            ("cotangent", cotangent),
        ),
        (
            (inputs.shape, bf16), tokens, wide_out, ends_out, tokens, wide_out,
            tail_part.half(), tail_part.half(), vector, ends_out, totals_out,
        ),
        (
            ((count, 4 * width), bf16), tokens, tokens_low, tokens, tokens_low, tokens_low, tokens,
            tokens_low, glu_out, out_out,
        ),
        final=(0,),
        micros=10,
    )
    units = [UnitSum(keep, send, tail_kind)]
    tail_units = [units[0]]
    in_units = []
    skip_grads = [skip_grad]
    gain_grads, rate_grads = [], []
    back_scratch = (
        drive_out, drive_out, ((count, 2 * width), bf16), bar_out, tokens,
    )
    rate_out = ((4, width), f32)
    small_out = ((8 * 2 * half_blocks, lane_count), f32)
    for layer in reversed(range(1, layer_count)):
        if layer == layer_count - 1:
            totals = line.advance(units, totals)
        gathered = gather(totals)
        gathered = line.advance(units, gathered)
        low_states, low, low_enter, mixed, act, gate, low_values, low_scaled = kept[layer - 1]
        (
            keep, send, in_keep, in_send, gain_grad, rate_grad, grad, d_mixed, d_states, skip_grad, ends,
            totals,
        ) = call(
            functools.partial(back_middle_kernel, layer, length),
            "back_middle",
            (
                ("place", place),
                ("gathered", gathered),
                *shared,
                ("gain", norm_gain),
                ("skip", skip_weight),
                ("in", (in_weight, layer)),
                ("d_states", d_states),
                ("ends", ends),
                ("states", states),
                ("enter", enter),
                ("scaled", scaled),
                ("values", values),
                ("d_mixed", d_mixed),
                ("grad", grad),
                ("out", (out_weight, layer - 1)),
                ("glu", (glu_weight, layer - 1)),
                ("mixed", mixed),
                ("act", act),
                ("gate", gate),
                ("below_scaled", low_scaled),
                ("low", low),
            ),
            (
                tail_part.half(), tail_part.half(), in_part.half(), in_part.half(), vector, rate_out,
                tokens, tokens, wide_out, vector, ends_out, totals_out,
            ),
            back_scratch + (tokens_low, tokens_low, in_out, glu_out, out_out),
            micros=14,
        )
        fresh = [UnitSum(keep, send, tail_kind), UnitSum(in_keep, in_send, in_kind)]
        line.advance(fresh)
        tail_units.append(fresh[0])
        in_units.append(fresh[1])
        gain_grads.insert(0, gain_grad)
        rate_grads.insert(0, rate_grad)
        skip_grads.insert(0, skip_grad)
        states, enter, values, scaled = low_states, low_enter, low_values, low_scaled
        totals = line.advance(units, totals)
        units = fresh + units
    gathered = gather(totals)
    gathered = line.advance(units, gathered)
    keep, send, input_grad = call(
        functools.partial(back_last_kernel, length),
        "back_last",
        (
            ("place", place),
            ("gathered", gathered),
            *shared,
            ("gain", norm_gain),
            ("skip", skip_weight),
            ("in", (in_weight, 0)),
            ("d_states", d_states),
            ("ends", ends),
            ("states", states),
            ("enter", enter),
            ("scaled", scaled),
            ("values", values),
            ("d_mixed", d_mixed),
            ("grad", grad),
            *(("skip_grad", term) for term in skip_grads),
            *(("gain_grad", term) for term in gain_grads),
            *(("rate_grad", term) for term in rate_grads),
        ),
        (last_part.half(), last_part.half(), (inputs.shape, bf16)),
        back_scratch
        + (
            tokens_low, in_out, vector, rate_out, small_out,
        ),
        final=(2,),
        micros=10,
    )
    last_unit = UnitSum(keep, send, last_kind)
    line.advance([last_unit])
    named = {"a": tail_units[0], "b": tail_units[-1], "c": last_unit, "d": (in_units or [last_unit])[-1]}
    for name in round_order:
        line.advance([named[name]])
    for unit in tail_units + in_units + [last_unit]:
        while unit.runs is None:
            line.advance([unit])
    for index, unit in enumerate(tail_units):
        layer = layer_count - 1 - index
        place_units(
            "place_tail",
            [(unit, tail_part)],
            [("out", whole["out"], [(0, "out", layer)]), ("glu", whole["glu"], [(0, "glu", layer)])],
            sums,
        )
    ends = [(unit, in_part) for unit in in_units] + [(last_unit, last_part)]
    place_units(
        "place_last",
        ends,
        [
            (
                "in",
                whole["in"],
                [(index, "in", layer_count - 1 - index) for index in range(layer_count)],
            ),
            ("small", small_out[0], [(len(ends) - 1, "small", None)]),
        ],
        sums,
    )
    small = sums["small"]

    def taken(first, shape):
        rows = math.prod(shape) // lane_count
        return small[first : first + rows].reshape(shape), first + rows

    gain_sum, row = taken(0, (layer_count, model))
    skip_sum, row = taken(row, (layer_count, model))
    rate_sum, row = taken(row, (layer_count, 4, width))
    decay_grad, frequency_grad, step_grad = rates_back(
        tuple(rate_sum[:, member] for member in range(4))
    )
    return (
        output,
        input_grad,
        gain_sum,
        decay_grad,
        frequency_grad,
        step_grad,
        sums["in"],
        skip_sum,
        sums["out"],
        sums["glu"],
    )


def solution(mesh):
    in_specs = (
        P("batch", "seq", None),
        P("batch", None),
        P(),
        P(),
        P(),
        P(),
        P(),
        P(),
        P(),
        P(),
        P("batch", "seq", None),
    )
    out_specs = (
        P("batch", "seq", None),
        P("batch", "seq", None),
        P(),
        P(),
        P(),
        P(),
        P(),
        P(),
        P(),
        P(),
    )
    return jax.shard_map(
        on_device, mesh=mesh, in_specs=in_specs, out_specs=out_specs, check_vma=False
    )
```

```python
import functools
import math

import jax
import jax.numpy as jnp
from jax import lax
from jax.experimental import pallas as pl
from jax.experimental.pallas import tpu as pltpu
from jax.sharding import PartitionSpec as P

epsilon = 1e-05
chunk_count = 8
lane_count = 128
block_rows = 32
vmem_bytes = 32 * 1024 * 1024
gelu_scale = math.sqrt(2.0 / math.pi)
gelu_cubic = 0.044715
f32 = jnp.float32
bf16 = jnp.bfloat16


def complex_mul(left_real, left_imag, right_real, right_imag):
    return (
        left_real * right_real - left_imag * right_imag,
        left_real * right_imag + left_imag * right_real,
    )


def complex_power(real, imag, exponent):
    result = None
    while exponent:
        if exponent & 1:
            result = (real, imag) if result is None else complex_mul(*result, real, imag)
        exponent >>= 1
        if exponent:
            real, imag = complex_mul(real, imag, real, imag)
    return result


def rates(decay_log, frequency, step_log):
    step_size = jnp.exp(step_log)
    pole_real = -jnp.exp(decay_log)
    shrink = step_size * pole_real
    rotation = step_size * frequency
    radius = jnp.exp(shrink)
    decay_real = radius * jnp.cos(rotation)
    decay_imag = radius * jnp.sin(rotation)
    minus_real = jnp.expm1(shrink) * jnp.cos(rotation) - 2.0 * jnp.sin(0.5 * rotation) ** 2
    modulus = pole_real * pole_real + frequency * frequency
    factor_real = (minus_real * pole_real + decay_imag * frequency) / modulus
    factor_imag = (decay_imag * pole_real - minus_real * frequency) / modulus
    return (decay_real, decay_imag, factor_real, factor_imag)


def dot(left, right):
    return lax.dot_general(left, right, (((1,), (0,)), ((), ())), preferred_element_type=f32)


def dot_right(left, right):
    return lax.dot_general(left, right, (((1,), (1,)), ((), ())), preferred_element_type=f32)


def dot_left(left, right):
    return lax.dot_general(left, right, (((0,), (0,)), ((), ())), preferred_element_type=f32)


def spread(narrow, width):
    return jnp.concatenate([narrow] * (width // lane_count), axis=1)


def order_matrix(count, inverse):
    rows = lax.broadcasted_iota(jnp.int32, (count, count), 0)
    cols = lax.broadcasted_iota(jnp.int32, (count, count), 1)
    if inverse:
        rows, cols = cols, rows
    source = lax.rem(rows, chunk_count) * (count // chunk_count) + lax.div(rows, chunk_count)
    return jnp.where(cols == source, 1.0, 0.0).astype(bf16)


def over_blocks(count, body):
    def one(index, carry):
        body(pl.ds(pl.multiple_of(index * block_rows, block_rows), block_rows))
        return carry

    lax.fori_loop(0, count // block_rows, one, 0, unroll=min(8, count // block_rows))


def normalize(values):
    average = jnp.mean(values, axis=-1, keepdims=True)
    centered = values - average
    inverse = lax.rsqrt(jnp.mean(centered * centered, axis=-1, keepdims=True) + epsilon)
    return centered * inverse, inverse


def gelu_parts(mixed):
    square = mixed * mixed
    bend = jnp.tanh(gelu_scale * mixed * (1.0 + gelu_cubic * square))
    half = 0.5 + 0.5 * bend
    slope = half + 0.5 * mixed * (1.0 - bend * bend) * gelu_scale * (
        1.0 + 3.0 * gelu_cubic * square
    )
    return mixed * half, slope


def write_flags(place, docs_ref, flags_ref, blocks_ref, length):
    row_count, doc_count = docs_ref.shape
    span = row_count * length // chunk_count
    per_row = chunk_count // row_count
    offsets = []
    for row in range(row_count):
        running = [jnp.int32(0)]
        for doc in range(doc_count):
            running.append(running[-1] + docs_ref[row, doc])
        offsets.append(running)

    def by_row(row_of, member):
        chosen = jnp.full(row_of.shape, offsets[0][member], jnp.int32)
        for row in range(1, row_count):
            chosen = jnp.where(row_of == row, offsets[row][member], chosen)
        return chosen

    chunk = lax.broadcasted_iota(jnp.int32, (chunk_count, lane_count), 0)
    row_of = lax.div(chunk, per_row)
    bounds = [by_row(row_of, member) for member in range(doc_count + 1)]
    base = place * length + lax.rem(chunk, per_row) * span
    for step in range(span):
        position = base + step
        starts = position == bounds[0]
        endings = position + 1 == bounds[0]
        for bound in bounds[1:]:
            starts = starts | (position == bound)
            endings = endings | (position + 1 == bound)
        window = pl.ds(chunk_count * step, chunk_count)
        flags_ref[0, window, :] = jnp.where(starts, 0.0, 1.0)
        flags_ref[1, window, :] = jnp.where(endings, 0.0, 1.0)
        flags_ref[2, window, :] = jnp.where(position < bounds[-1], 1.0, 0.0)
    entry = lax.broadcasted_iota(jnp.int32, blocks_ref.shape[1:], 0)
    row_of = lax.rem(entry, row_count)
    first = lax.div(entry, row_count) * length
    starts = jnp.zeros(entry.shape, jnp.bool_)
    endings = starts
    for member in range(doc_count + 1):
        bound = by_row(row_of, member)
        starts = starts | ((bound >= first) & (bound < first + length))
        endings = endings | ((bound > first) & (bound <= first + length))
    blocks_ref[0] = jnp.where(starts, 0.0, 1.0)
    blocks_ref[1] = jnp.where(endings, 0.0, 1.0)


def chunk_keeps(flags_ref):
    span = flags_ref.shape[1] // chunk_count
    ahead = flags_ref[0, :chunk_count, :]
    behind = flags_ref[1, :chunk_count, :]
    for step in range(1, span):
        window = pl.ds(chunk_count * step, chunk_count)
        ahead = ahead * flags_ref[0, window, :]
        behind = behind * flags_ref[1, window, :]
    return ahead, behind


def toward(array, distance, reverse):
    return pltpu.roll(array, chunk_count - distance if reverse else distance, axis=0)


def chunk_prefix(ends, factor, entering, per_row, reverse):
    width = ends[0].shape[1]
    chunk = lax.broadcasted_iota(jnp.int32, (chunk_count, width), 0)
    within = lax.rem(chunk, per_row)
    within = per_row - 1 - within if reverse else within
    first = within == 0
    total_real, total_imag = ends
    if entering is not None:
        moved_real, moved_imag = complex_mul(*factor, *entering)
        total_real = total_real + jnp.where(first, moved_real, 0.0)
        total_imag = total_imag + jnp.where(first, moved_imag, 0.0)
    distance = 1
    while distance < per_row:
        reach = within >= distance
        near_real = toward(total_real, distance, reverse)
        near_imag = toward(total_imag, distance, reverse)
        moved_real, moved_imag = complex_mul(*factor, near_real, near_imag)
        total_real = total_real + jnp.where(reach, moved_real, 0.0)
        total_imag = total_imag + jnp.where(reach, moved_imag, 0.0)
        if 2 * distance < per_row:
            far_real = toward(factor[0], distance, reverse)
            far_imag = toward(factor[1], distance, reverse)
            both_real, both_imag = complex_mul(*factor, far_real, far_imag)
            factor = (
                jnp.where(reach, both_real, factor[0]),
                jnp.where(reach, both_imag, factor[1]),
            )
        distance *= 2
    enter_real = toward(total_real, 1, reverse)
    enter_imag = toward(total_imag, 1, reverse)
    none = (jnp.zeros_like(total_real),) * 2 if entering is None else entering
    return (
        (total_real, total_imag),
        (jnp.where(first, none[0], enter_real), jnp.where(first, none[1], enter_imag)),
    )


def sweep(flags_ref, pole_real, pole_imag, forward_at, reverse_at, start, put_forward, put_reverse):
    width = pole_real.shape[1]
    span = flags_ref.shape[1] // chunk_count

    def one(step, state):
        ahead_real, ahead_imag, behind_real, behind_imag = state
        here = pl.ds(pl.multiple_of(chunk_count * step, chunk_count), chunk_count)
        there = pl.ds(pl.multiple_of(chunk_count * (span - 1 - step), chunk_count), chunk_count)
        keep = spread(flags_ref[0, here, :], width)
        moved_real, moved_imag = complex_mul(pole_real * keep, pole_imag * keep, ahead_real, ahead_imag)
        drive_real, drive_imag = forward_at(here)
        ahead_real = moved_real + drive_real
        ahead_imag = moved_imag + drive_imag
        keep = spread(flags_ref[1, there, :], width)
        moved_real, moved_imag = complex_mul(
            pole_real * keep, pole_imag * keep, behind_real, behind_imag
        )
        drive_real, drive_imag = reverse_at(there)
        behind_real = moved_real + drive_real
        behind_imag = moved_imag + drive_imag
        if put_forward is not None:
            put_forward(here, ahead_real, ahead_imag)
            put_reverse(there, behind_real, behind_imag)
        return (ahead_real, ahead_imag, behind_real, behind_imag)

    return lax.fori_loop(0, span, one, start, unroll=4)


def local_totals(flags_ref, pole_real, pole_imag, forward_at, reverse_at, ends_ref, totals_ref):
    width = pole_real.shape[1]
    span = flags_ref.shape[1] // chunk_count
    row_count = totals_ref.shape[0] // 4
    per_row = chunk_count // row_count
    pole_real = jnp.broadcast_to(pole_real, (chunk_count, width))
    pole_imag = jnp.broadcast_to(pole_imag, (chunk_count, width))
    zero = jnp.zeros((chunk_count, width), f32)
    ends = sweep(
        flags_ref, pole_real, pole_imag, forward_at, reverse_at, (zero,) * 4, None, None
    )
    for member in range(4):
        ends_ref[:, member * width : (member + 1) * width] = ends[member]
    power_real, power_imag = complex_power(pole_real, pole_imag, span)
    for direction, keep in enumerate(chunk_keeps(flags_ref)):
        keep = spread(keep, width)
        pair = ends[2 * direction : 2 * direction + 2]
        totals, unused = chunk_prefix(
            pair, (power_real * keep, power_imag * keep), None, per_row, direction == 1
        )
        for part in range(2):
            for row in range(row_count):
                chunk = row * per_row if direction == 1 else (row + 1) * per_row - 1
                entry = (2 * direction + part) * row_count + row
                totals_ref[entry : entry + 1, :] = totals[part][chunk : chunk + 1, :]


def chunk_entrances(place, gathered_ref, flags_ref, blocks_ref, ends_ref, pole_real, pole_imag, length):
    width = pole_real.shape[1]
    span = flags_ref.shape[1] // chunk_count
    row_count = chunk_count * span // length
    per_row = chunk_count // row_count
    device_count = gathered_ref.shape[0] // (4 * row_count)
    pole_real = jnp.broadcast_to(pole_real, (chunk_count, width))
    pole_imag = jnp.broadcast_to(pole_imag, (chunk_count, width))
    power_real, power_imag = complex_power(pole_real, pole_imag, span)
    device_real, device_imag = complex_power(power_real, power_imag, per_row)
    device_real = device_real[:row_count]
    device_imag = device_imag[:row_count]
    entrances = []
    for direction, keep in enumerate(chunk_keeps(flags_ref)):
        real = jnp.zeros((row_count, width), f32)
        imag = real
        for lap in range(device_count):
            source = device_count - 1 - lap if direction == 1 else lap
            live = source > place if direction == 1 else source < place
            open_ = spread(
                blocks_ref[direction, source * row_count : (source + 1) * row_count, :], width
            )
            moved_real, moved_imag = complex_mul(device_real * open_, device_imag * open_, real, imag)
            first = (4 * source + 2 * direction) * row_count
            moved_real = moved_real + gathered_ref[first : first + row_count, :]
            moved_imag = moved_imag + gathered_ref[first + row_count : first + 2 * row_count, :]
            real = jnp.where(live, moved_real, real)
            imag = jnp.where(live, moved_imag, imag)
        entering = tuple(
            jnp.concatenate(
                [
                    jnp.broadcast_to(part[row : row + 1, :], (per_row, width))
                    for row in range(row_count)
                ],
                axis=0,
            )
            for part in (real, imag)
        )
        keep = spread(keep, width)
        first = 2 * direction * width
        ends = (ends_ref[:, first : first + width], ends_ref[:, first + width : first + 2 * width])
        unused, entrance = chunk_prefix(
            ends, (power_real * keep, power_imag * keep), entering, per_row, direction == 1
        )
        entrances.extend(entrance)
    return tuple(entrances)


def layer_poles(tables_ref, layer):
    return tables_ref[4 * layer : 4 * layer + 1, :], tables_ref[4 * layer + 1 : 4 * layer + 2, :]


def layer_factors(tables_ref, layer):
    return tables_ref[4 * layer + 2 : 4 * layer + 3, :], tables_ref[4 * layer + 3 : 4 * layer + 4, :]


def write_bar(tables_ref, layer, in_ref, bar_ref):
    width = tables_ref.shape[1]
    factor_real, factor_imag = layer_factors(tables_ref, layer)

    def body(rows):
        weight_real = in_ref[rows, :width].astype(f32)
        weight_imag = in_ref[rows, width:].astype(f32)
        real, imag = complex_mul(factor_real, factor_imag, weight_real, weight_imag)
        bar_ref[rows, :width] = real.astype(bf16)
        bar_ref[rows, width:] = imag.astype(bf16)

    over_blocks(in_ref.shape[0], body)


def pair_at(ref, first, width):
    def at(rows):
        return ref[rows, first : first + width], ref[rows, first + width : first + 2 * width]

    return at


def drive_totals(flags_ref, tables_ref, layer, scaled_ref, in_ref, bar_ref, drive_ref, ends_ref, totals_ref):
    width = tables_ref.shape[1]
    write_bar(tables_ref, layer, in_ref.ready(), bar_ref)
    drive_ref[...] = dot(scaled_ref[...], bar_ref[...])
    at = pair_at(drive_ref, 0, width)
    local_totals(flags_ref, *layer_poles(tables_ref, layer), at, at, ends_ref, totals_ref)


def settled_states(
    place, gathered_ref, flags_ref, blocks_ref, tables_ref, layer, drive_ref, ends_ref, length,
    states_ref, low_ref, enter_ref,
):
    width = tables_ref.shape[1]
    pole_real, pole_imag = layer_poles(tables_ref, layer)
    entrances = chunk_entrances(
        place, gathered_ref, flags_ref, blocks_ref, ends_ref, pole_real, pole_imag, length
    )
    for member in range(4):
        enter_ref[:, member * width : (member + 1) * width] = entrances[member]

    def put_forward(rows, real, imag):
        states_ref[rows, :width] = real
        states_ref[rows, width : 2 * width] = imag

    def put_reverse(rows, real, imag):
        states_ref[rows, 2 * width : 3 * width] = real
        states_ref[rows, 3 * width :] = imag

    at = pair_at(drive_ref, 0, width)
    sweep(
        flags_ref,
        jnp.broadcast_to(pole_real, (chunk_count, width)),
        jnp.broadcast_to(pole_imag, (chunk_count, width)),
        at, at, entrances, put_forward, put_reverse,
    )

    def body(rows):
        low_ref[rows, :] = states_ref[rows, :].astype(bf16)

    over_blocks(states_ref.shape[0], body)


def mix_and_gate(layer, low_ref, scaled_ref, out_ref, glu_ref, skip_ref, mixed_ref, act_ref, gate_ref):
    mixed_ref[...] = dot(low_ref[...], out_ref.ready()[...])
    skip = skip_ref[layer : layer + 1, :]

    def body(rows):
        mixed = mixed_ref[rows, :] + skip * scaled_ref[rows, :].astype(f32)
        mixed_ref[rows, :] = mixed
        act_ref[rows, :] = gelu_parts(mixed)[0].astype(bf16)

    over_blocks(mixed_ref.shape[0], body)
    gate_ref[...] = dot(act_ref[...], glu_ref.ready()[...])


def back_tail(
    layer, flags_ref, tables_ref, grad_ref, mixed_ref, act_ref, gate_ref, scaled_ref, low_ref,
    out_ref, glu_ref, skip_ref, logits_ref, work_ref, mixed_low_ref,
    d_mixed_ref, d_states_ref, glu_grad_ref, out_grad_ref, skip_grad_ref, ends_ref, totals_ref, emit,
):
    width = tables_ref.shape[1]
    model = mixed_ref.shape[1]

    def first(rows):
        valid = spread(flags_ref[2, rows, :], model)
        gate = gate_ref[rows, :]
        rate = grad_ref[rows, :] * valid * gate
        logits_ref[rows, :] = (rate * act_ref[rows, :].astype(f32) * (1.0 - gate)).astype(bf16)

    over_blocks(mixed_ref.shape[0], first)
    glu_grad_ref[...] = dot_left(act_ref[...], logits_ref[...])
    emit.put("glu", glu_grad_ref)
    work_ref[...] = dot_right(logits_ref[...], glu_ref.ready()[...])
    skip_grad_ref[...] = jnp.zeros(skip_grad_ref.shape, f32)

    def second(rows):
        valid = spread(flags_ref[2, rows, :], model)
        d_act = grad_ref[rows, :] * valid * gate_ref[rows, :] + work_ref[rows, :]
        d_mixed = d_act * gelu_parts(mixed_ref[rows, :])[1]
        d_mixed_ref[rows, :] = d_mixed
        mixed_low_ref[rows, :] = d_mixed.astype(bf16)
        skip_grad_ref[...] += jnp.sum(
            d_mixed * scaled_ref[rows, :].astype(f32), axis=0, keepdims=True
        )

    over_blocks(mixed_ref.shape[0], second)
    out_grad_ref[...] = dot_left(low_ref[...], mixed_low_ref[...])
    emit.put("out", out_grad_ref)
    d_states_ref[...] = dot_right(mixed_low_ref[...], out_ref.ready()[...])
    pole_real, pole_imag = layer_poles(tables_ref, layer)
    local_totals(
        flags_ref, pole_real, -pole_imag, pair_at(d_states_ref, 2 * width, width),
        pair_at(d_states_ref, 0, width), ends_ref, totals_ref,
    )


def back_front(
    place, layer, length, gathered_ref, flags_ref, blocks_ref, tables_ref, gain_ref, skip_ref, in_ref,
    d_states_ref, ends_ref, states_ref, enter_ref, scaled_ref, values_ref, d_mixed_ref, grad_ref,
    lam_ref, mu_ref, low_ref, bar_ref, work_ref,
    in_grad_ref, gain_grad_ref, rate_grad_ref, put_gradient, emit,
):
    width = tables_ref.shape[1]
    model = values_ref.shape[1]
    count = values_ref.shape[0]
    pole_real, pole_imag = layer_poles(tables_ref, layer)
    entrances = chunk_entrances(
        place, gathered_ref, flags_ref, blocks_ref, ends_ref, pole_real, -pole_imag, length
    )

    def put_forward(rows, real, imag):
        mu_ref[rows, :width] = real
        mu_ref[rows, width:] = imag

    def put_reverse(rows, real, imag):
        lam_ref[rows, :width] = real
        lam_ref[rows, width:] = imag

    sweep(
        flags_ref,
        jnp.broadcast_to(pole_real, (chunk_count, width)),
        jnp.broadcast_to(-pole_imag, (chunk_count, width)),
        pair_at(d_states_ref, 2 * width, width), pair_at(d_states_ref, 0, width),
        entrances, put_forward, put_reverse,
    )
    span = count // chunk_count

    def decay_terms(here, before_real, before_imag, after_real, after_imag, sums):
        keep = spread(flags_ref[0, here, :], width)
        lam_real, lam_imag = lam_ref[here, :width], lam_ref[here, width:]
        mu_real, mu_imag = mu_ref[here, :width], mu_ref[here, width:]
        real = keep * (lam_real * before_real + lam_imag * before_imag)
        imag = keep * (lam_imag * before_real - lam_real * before_imag)
        keep = spread(flags_ref[1, here, :], width)
        real = real + keep * (mu_real * after_real + mu_imag * after_imag)
        imag = imag + keep * (mu_imag * after_real - mu_real * after_imag)
        return sums[0] + real, sums[1] + imag

    def window(step):
        start = chunk_count * step
        return pl.ds(start if isinstance(step, int) else pl.multiple_of(start, chunk_count), chunk_count)

    def before_at(step):
        rows = window(step)
        return states_ref[rows, :width], states_ref[rows, width : 2 * width]

    def after_at(step):
        rows = window(step)
        return states_ref[rows, 2 * width : 3 * width], states_ref[rows, 3 * width :]

    def middle(step, sums):
        return decay_terms(window(step), *before_at(step - 1), *after_at(step + 1), sums)

    zero = jnp.zeros((chunk_count, width), f32)
    sums = decay_terms(
        window(0), enter_ref[:, :width], enter_ref[:, width : 2 * width], *after_at(1), (zero, zero)
    )
    sums = lax.fori_loop(1, span - 1, middle, sums, unroll=2)
    sums = decay_terms(
        window(span - 1), *before_at(span - 2),
        enter_ref[:, 2 * width : 3 * width], enter_ref[:, 3 * width :], sums,
    )
    rate_grad_ref[0:1, :] = jnp.sum(sums[0], axis=0, keepdims=True)
    rate_grad_ref[1:2, :] = jnp.sum(sums[1], axis=0, keepdims=True)

    def narrow(rows):
        low_ref[rows, :] = (lam_ref[rows, :] + mu_ref[rows, :]).astype(bf16)

    over_blocks(count, narrow)
    in_ref = in_ref.ready()
    write_bar(tables_ref, layer, in_ref, bar_ref)
    work_ref[...] = dot_right(low_ref[...], bar_ref[...])
    skip = skip_ref[layer : layer + 1, :]
    gain = gain_ref[layer : layer + 1, :]
    gain_grad_ref[...] = jnp.zeros(gain_grad_ref.shape, f32)

    def norm_back(rows):
        valid = spread(flags_ref[2, rows, :], model)
        normed, inverse = normalize(values_ref[rows, :].astype(f32))
        d_scaled = (work_ref[rows, :] + d_mixed_ref[rows, :] * skip) * valid
        gain_grad_ref[...] += jnp.sum(d_scaled * normed, axis=0, keepdims=True)
        d_normed = d_scaled * gain
        put_gradient(
            rows,
            inverse
            * (
                d_normed
                - jnp.mean(d_normed, axis=-1, keepdims=True)
                - normed * jnp.mean(d_normed * normed, axis=-1, keepdims=True)
            )
            + grad_ref[rows, :].astype(f32),
        )

    over_blocks(count, norm_back)
    in_grad_ref[...] = dot_left(scaled_ref[...], low_ref[...])
    factor_real, factor_imag = layer_factors(tables_ref, layer)
    rate_grad_ref[2:4, :] = jnp.zeros((2, width), f32)

    def weigh(rows):
        grad_real, grad_imag = in_grad_ref[rows, :width], in_grad_ref[rows, width:]
        weight_real = in_ref[rows, :width].astype(f32)
        weight_imag = in_ref[rows, width:].astype(f32)
        rate_grad_ref[2:3, :] += jnp.sum(
            grad_real * weight_real + grad_imag * weight_imag, axis=0, keepdims=True
        )
        rate_grad_ref[3:4, :] += jnp.sum(
            grad_imag * weight_real - grad_real * weight_imag, axis=0, keepdims=True
        )
        in_grad_ref[rows, :width] = factor_real * grad_real + factor_imag * grad_imag
        in_grad_ref[rows, width:] = factor_real * grad_imag - factor_imag * grad_real

    over_blocks(in_ref.shape[0], weigh)
    emit.put("in", in_grad_ref)


def first_kernel(
    length, place_ref, docs_ref, inputs_ref, gain_ref, tables_ref, in_ref,
    flags_ref, blocks_ref, values_ref, scaled_ref, drive_ref, ends_ref, totals_ref, bar_ref,
):
    write_flags(place_ref[0], docs_ref, flags_ref, blocks_ref, length)
    count, model = values_ref.shape
    values_ref[...] = dot(
        order_matrix(count, False), inputs_ref[...].reshape(count, model)
    ).astype(bf16)
    gain = gain_ref[0:1, :]

    def body(rows):
        normed, unused = normalize(values_ref[rows, :].astype(f32))
        valid = spread(flags_ref[2, rows, :], model)
        scaled_ref[rows, :] = (normed * gain * valid).astype(bf16)

    over_blocks(count, body)
    drive_totals(
        flags_ref, tables_ref, 0, scaled_ref, in_ref, bar_ref, drive_ref, ends_ref, totals_ref
    )


def middle_kernel(
    layer, length, place_ref, gathered_ref, flags_ref, blocks_ref, tables_ref, gain_ref, skip_ref,
    drive_ref, ends_ref, values_ref, scaled_ref, out_ref, glu_ref, in_ref,
    states_ref, low_ref, enter_ref, mixed_ref, act_ref, gate_ref,
    next_values_ref, next_scaled_ref, next_drive_ref, next_ends_ref, next_totals_ref, bar_ref,
):
    settled_states(
        place_ref[0], gathered_ref, flags_ref, blocks_ref, tables_ref, layer, drive_ref, ends_ref, length,
        states_ref, low_ref, enter_ref,
    )
    mix_and_gate(
        layer, low_ref, scaled_ref, out_ref, glu_ref, skip_ref, mixed_ref, act_ref, gate_ref
    )
    model = values_ref.shape[1]
    gain = gain_ref[layer + 1 : layer + 2, :]

    def body(rows):
        valid = spread(flags_ref[2, rows, :], model)
        gate = jax.nn.sigmoid(gate_ref[rows, :])
        gate_ref[rows, :] = gate
        result = values_ref[rows, :].astype(f32) + valid * act_ref[rows, :].astype(f32) * gate
        next_values_ref[rows, :] = result
        normed, unused = normalize(result)
        next_scaled_ref[rows, :] = (normed * gain * valid).astype(bf16)

    over_blocks(values_ref.shape[0], body)
    drive_totals(
        flags_ref, tables_ref, layer + 1, next_scaled_ref, in_ref, bar_ref, next_drive_ref,
        next_ends_ref, next_totals_ref,
    )


def turn_kernel(
    layer, length, place_ref, gathered_ref, flags_ref, blocks_ref, tables_ref, skip_ref,
    drive_ref, ends_ref, values_ref, scaled_ref, out_ref, glu_ref, cotangent_ref,
    *rest,
):
    unit_refs, rest = rest[: 2 * len(turn_units)], rest[2 * len(turn_units) :]
    (
        output_ref, grad_ref, states_ref, enter_ref, d_mixed_ref, d_states_ref,
        skip_grad_ref, back_ends_ref, back_totals_ref,
        low_ref, mixed_ref, act_ref, gate_ref, result_ref, logits_ref, work_ref, mixed_low_ref,
        glu_grad_ref, out_grad_ref,
    ) = rest
    emit = Emit(turn_units, unit_refs, values_ref.shape[1], tables_ref.shape[1])
    settled_states(
        place_ref[0], gathered_ref, flags_ref, blocks_ref, tables_ref, layer, drive_ref, ends_ref, length,
        states_ref, low_ref, enter_ref,
    )
    mix_and_gate(
        layer, low_ref, scaled_ref, out_ref, glu_ref, skip_ref, mixed_ref, act_ref, gate_ref
    )
    count, model = values_ref.shape

    def body(rows):
        valid = spread(flags_ref[2, rows, :], model)
        gate = jax.nn.sigmoid(gate_ref[rows, :])
        gate_ref[rows, :] = gate
        result = values_ref[rows, :] + valid * act_ref[rows, :].astype(f32) * gate
        result_ref[rows, :] = result.astype(bf16)

    over_blocks(count, body)
    output_ref[...] = (
        dot(order_matrix(count, True), result_ref[...]).astype(bf16).reshape(output_ref.shape)
    )
    grad_ref[...] = dot(order_matrix(count, False), cotangent_ref[...].reshape(count, model))
    back_tail(
        layer, flags_ref, tables_ref, grad_ref, mixed_ref, act_ref, gate_ref, scaled_ref, low_ref,
        out_ref, glu_ref, skip_ref, logits_ref, work_ref, mixed_low_ref,
        d_mixed_ref, d_states_ref, glu_grad_ref, out_grad_ref, skip_grad_ref, back_ends_ref,
        back_totals_ref, emit,
    )


def back_middle_kernel(
    layer, length, place_ref, gathered_ref, flags_ref, blocks_ref, tables_ref, gain_ref, skip_ref, in_ref,
    d_states_ref, ends_ref, states_ref, enter_ref, scaled_ref, values_ref, d_mixed_ref, grad_ref,
    out_ref, glu_ref, below_mixed_ref, below_act_ref, below_gate_ref, below_scaled_ref, below_low_ref,
    *rest,
):
    unit_refs, rest = rest[: 2 * len(middle_units)], rest[2 * len(middle_units) :]
    (
        gain_grad_ref, rate_grad_ref, next_grad_ref, below_d_mixed_ref,
        below_d_states_ref, skip_grad_ref, below_ends_ref, below_totals_ref,
        lam_ref, mu_ref, low_ref, bar_ref, work_ref, logits_ref, mixed_low_ref,
        in_grad_ref, glu_grad_ref, out_grad_ref,
    ) = rest
    emit = Emit(middle_units, unit_refs, values_ref.shape[1], tables_ref.shape[1])

    def put_gradient(rows, gradient):
        next_grad_ref[rows, :] = gradient

    back_front(
        place_ref[0], layer, length, gathered_ref, flags_ref, blocks_ref, tables_ref, gain_ref, skip_ref,
        in_ref, d_states_ref, ends_ref, states_ref, enter_ref, scaled_ref, values_ref, d_mixed_ref,
        grad_ref, lam_ref, mu_ref, low_ref, bar_ref, work_ref,
        in_grad_ref, gain_grad_ref, rate_grad_ref, put_gradient, emit,
    )
    back_tail(
        layer - 1, flags_ref, tables_ref, next_grad_ref, below_mixed_ref, below_act_ref, below_gate_ref,
        below_scaled_ref, below_low_ref, out_ref, glu_ref, skip_ref, logits_ref, work_ref, mixed_low_ref,
        below_d_mixed_ref, below_d_states_ref, glu_grad_ref, out_grad_ref, skip_grad_ref,
        below_ends_ref, below_totals_ref, emit,
    )


def back_last_kernel(
    length, place_ref, gathered_ref, flags_ref, blocks_ref, tables_ref, gain_ref, skip_ref, in_ref,
    d_states_ref, ends_ref, states_ref, enter_ref, scaled_ref, values_ref, d_mixed_ref, grad_ref,
    *rest,
):
    layer_count = gain_ref.shape[0]
    skip_grads = rest[:layer_count]
    rest = rest[layer_count:]
    gain_grads = rest[: layer_count - 1]
    rate_grads = rest[layer_count - 1 : 2 * layer_count - 2]
    unit_refs = rest[2 * layer_count - 2 : 2 * layer_count]
    (
        input_grad_ref,
        lam_ref, mu_ref, low_ref, bar_ref, work_ref, result_ref,
        in_grad_ref, gain_grad_ref, rate_grad_ref, small_ref,
    ) = rest[2 * layer_count :]
    emit = Emit(last_units, unit_refs, values_ref.shape[1], tables_ref.shape[1])
    def put_gradient(rows, gradient):
        result_ref[rows, :] = gradient.astype(bf16)

    back_front(
        place_ref[0], 0, length, gathered_ref, flags_ref, blocks_ref, tables_ref, gain_ref, skip_ref,
        in_ref, d_states_ref, ends_ref, states_ref, enter_ref, scaled_ref, values_ref, d_mixed_ref,
        grad_ref, lam_ref, mu_ref, low_ref, bar_ref, work_ref,
        in_grad_ref, gain_grad_ref, rate_grad_ref, put_gradient, emit,
    )
    small_ref[...] = jnp.zeros(small_ref.shape, f32)
    row = 0
    for vectors in ((gain_grad_ref, *gain_grads), skip_grads, (rate_grad_ref, *rate_grads)):
        for vector_ref in vectors:
            for line in range(vector_ref.shape[0]):
                for first in range(0, vector_ref.shape[1], lane_count):
                    small_ref[row : row + 1, :] = vector_ref[line : line + 1, first : first + lane_count]
                    row += 1
    emit.put("small", small_ref)
    count = result_ref.shape[0]
    input_grad_ref[...] = (
        dot(order_matrix(count, True), result_ref[...]).astype(bf16).reshape(input_grad_ref.shape)
    )


halvings = 3
half_blocks = 1 << halvings
turn_units = (("a", ("out", "glu"), "plane"),)
middle_units = (("b", ("out", "glu"), "plane"), ("d", ("in",), "plane"))
last_units = (("c", ("in", "small"), "plane"),)
after_turn = "=a"
into_middle = "=a"
after_middle = "bd =a"
into_last = "=bda"
after_last = "bc a d c b d a b c d a c a b c d b c d a c b d A c b d B c"


def mesh_bits():
    seq_bits = lax.axis_size("seq").bit_length() - 1
    batch_bits = lax.axis_size("batch").bit_length() - 1
    deep = [1 << place for place in range(batch_bits)]
    core = 1 << batch_bits
    plane = [core << place for place in range(1, seq_bits)]
    return deep, core, plane[: len(plane) // 2], plane[len(plane) // 2 :]


def axis_orders(kind):
    deep, core, across, along = mesh_bits()
    if kind.endswith(" turned"):
        kind = kind[: -len(" turned")]
        across, along = along, across
    near, far = deep[:1], deep[1:]
    orders = {
        "plane": (across + along + deep, along + across + deep),
        "mixed": (across + along + deep, along + deep + across),
        "inner": (across + near + along + far, along + near + across + far),
        "second": (across + along + deep, near + across + along + far),
        "late": (across + along + deep, along + near + across + far),
        "first": (near + across + along + far, near + along + across + far),
        "cross": (across + along + deep, near + along + across + far),
    }
    return core, orders[kind]


def half_bases(kind):
    core, orders = axis_orders(kind)
    index = lax.axis_index("seq") * lax.axis_size("batch") + lax.axis_index("batch")
    side = lax.rem(lax.div(index, core), 2)
    numbers = []
    for order in orders:
        number = 0
        for bit in order[:halvings]:
            number = 2 * number + lax.rem(lax.div(index, bit), 2)
        numbers.append(number)
    keep = (1 - side) * numbers[0] + side * numbers[1]
    send = (1 - side) * numbers[1] + side * numbers[0]
    return side * half_blocks + keep, (1 - side) * half_blocks + send


def swap(array, first, second):
    core = mesh_bits()[1]
    total = lax.axis_size("seq") * lax.axis_size("batch")
    pairs = [(index, index ^ (second if index & core else first)) for index in range(total)]
    return lax.ppermute(array, ("seq", "batch"), pairs)


class UnitSum:
    def __init__(self, keep, send, kind):
        self.core, orders = axis_orders(kind)
        self.steps = list(zip(*orders))
        self.parts = [keep]
        self.top = keep.shape[0]
        self.runs = None
        self.rounds = self.plan(send)
        self.outgoing = next(self.rounds)

    def added(self, low, high):
        total = self.parts[0][low:high]
        for part in self.parts[1:]:
            total = total + part[low:high]
        return total

    def plan(self, send):
        sent = yield send
        self.parts.append(swap(sent, self.core, self.core))
        for step, (first, second) in enumerate(self.steps):
            if step < halvings:
                self.top //= 2
                sent = yield self.added(self.top, 2 * self.top)
                self.parts.append(swap(sent, first, second))
            else:
                own = yield self.added(0, self.top)
                self.parts = [own, swap(own, first, second)]
        full = self.added(0, self.top)
        for first, second in self.steps[halvings - 1 : 0 : -1]:
            full = yield full
            full = jnp.concatenate([full, swap(full, first, second)])
        full = yield full
        rest = swap(full, *self.steps[0])
        other = swap(full, self.core, self.core)
        rest = yield rest
        self.runs = (full, rest, other, swap(rest, self.core, self.core))
        yield None

    def launch(self, sent):
        self.outgoing = self.rounds.send(sent)


class Line:
    def __init__(self):
        self.last = ()

    def advance(self, units, payload=()):
        units = [unit for unit in units if unit.runs is None]
        sends, payload, unused = lax.optimization_barrier(
            ([unit.outgoing for unit in units], payload, self.last)
        )
        for unit, sent in zip(units, sends):
            unit.launch(sent)
        self.last = sends
        return payload

    def settle(self, arrays):
        arrays, self.last = lax.optimization_barrier((arrays, self.last))
        return arrays


def aligned(first, rows):
    return pl.ds(pl.multiple_of(first, 8), rows)


class Layout:
    def __init__(self, rows, columns, kind):
        self.rows, self.columns, self.kind = rows, columns, kind
        self.sections = {}

    def add(self, key, array_rows, array_first, block_first, count, columns=slice(None)):
        self.sections.setdefault(key, []).append(
            (
                lambda owner: (aligned(owner * array_rows + array_first, count), slice(None)),
                lambda place: (aligned(place * self.rows + block_first, count), columns),
            )
        )

    def half(self):
        return ((half_blocks * self.rows, self.columns), f32)


def unit_layout(keys, kind, model, width):
    total = 2 * half_blocks
    out_rows, rows, wide = 4 * width // total, model // total, 2 * width
    if keys == ("out",):
        layout = Layout(out_rows, model, kind)
        layout.add("out", out_rows, 0, 0, out_rows)
    elif keys == ("glu",):
        layout = Layout(rows, model, kind)
        layout.add("glu", rows, 0, 0, rows)
    elif keys == ("out", "glu"):
        layout = Layout(out_rows + rows, model, kind)
        layout.add("out", out_rows, 0, 0, out_rows)
        layout.add("glu", rows, 0, out_rows, rows)
    elif keys == ("in",):
        layout = Layout(rows, wide, kind)
        layout.add("in", rows, 0, 0, rows)
    elif keys == ("glu", "in"):
        layout = Layout(rows, model + wide, kind)
        layout.add("glu", rows, 0, 0, rows, slice(0, model))
        layout.add("in", rows, 0, 0, rows, slice(model, model + wide))
    else:
        pieces = rows // 8
        layout = Layout(8, pieces * wide + lane_count, kind)
        for piece in range(pieces):
            layout.add("in", rows, 8 * piece, 0, 8, slice(piece * wide, (piece + 1) * wide))
        layout.add("small", 8, 0, 0, 8, slice(pieces * wide, pieces * wide + lane_count))
    return layout


class Emit:
    def __init__(self, units, refs, model, width):
        self.homes = {}
        for index, (unused, keys, kind) in enumerate(units):
            layout = unit_layout(keys, kind, model, width)
            for key in keys:
                self.homes[key] = (layout, refs[2 * index : 2 * index + 2], half_bases(kind))

    def put(self, key, array_ref):
        layout, halves, bases = self.homes[key]

        def one(place, carry):
            for half in (1, 0):
                owner = lax.bitwise_xor(bases[half], place)
                for array_at, block_at in layout.sections[key]:
                    halves[half][block_at(place)] = array_ref[array_at(owner)]
            return carry

        lax.fori_loop(0, half_blocks, one, 0)


run_places = ((0, 0), (0, half_blocks // 2), (1, 0), (1, half_blocks // 2))


def place_kernel(layout, goals, *refs):
    outs = refs[len(refs) - 1 - len(goals) : -1]
    semaphores = refs[-1]
    bases = half_bases(layout.kind)
    for index, (half, first) in enumerate(run_places):

        def one(place, carry, run=refs[index], half=half, first=first, index=index):
            owner = lax.bitwise_xor(bases[half], first + place)
            for out, (key, layer) in zip(outs, goals):
                for array_at, block_at in layout.sections[key]:
                    pltpu.make_async_copy(
                        run.at[block_at(place)],
                        (out if layer is None else out.at[layer]).at[array_at(owner)],
                        semaphores.at[index],
                    ).start()
            return carry

        lax.fori_loop(0, half_blocks // 2, one, 0)
    for index in range(len(run_places)):
        run = refs[index]
        pltpu.make_async_copy(run, run, semaphores.at[index]).wait()


def place_unit(runs, layout, goals, shapes, sums):
    operands = [("run", run) for run in runs]
    aliases = {}
    for index, (key, unused) in enumerate(goals):
        if key in sums:
            aliases[len(operands)] = index
            operands.append(("before", (sums[key], None)))
    outs = call(
        functools.partial(place_kernel, layout, goals),
        "place_" + "_".join(key for key, unused in goals),
        operands,
        tuple((shapes[key], f32) for key, unused in goals),
        (pltpu.SemaphoreType.DMA((len(run_places),)),),
        written=range(len(goals)),
        aliases=aliases,
        plain=True,
    )
    for (key, unused), out in zip(goals, outs):
        sums[key] = out


class Fetch:
    def __init__(self, stack_ref, layer, target, semaphore):
        self.copy = pltpu.make_async_copy(stack_ref.at[layer], target, semaphore)
        self.target = target
        self.waiting = True
        self.copy.start()

    def ready(self):
        if self.waiting:
            self.copy.wait()
            self.waiting = False
        return self.target


def call(body, name, operands, outs, scratch, written=(), aliases=None, plain=False, micros=4, final=()):
    scalars = {"place", "docs"}
    arrays = []
    specs = []
    layers = {}
    pieces = None
    flat = []
    for key, operand in operands:
        if isinstance(operand, list):
            pieces = (len(flat), len(operand))
            flat.extend((key, piece) for piece in operand)
        else:
            flat.append((key, operand))
    for position, (key, operand) in enumerate(flat):
        space = pltpu.SMEM if key in scalars else pltpu.VMEM
        if isinstance(operand, tuple):
            operand, layer = operand
            space = pl.ANY
            if layer is not None:
                layers[position] = layer
                operand = pltpu.with_memory_space_constraint(operand, pltpu.HBM)
        specs.append(pl.BlockSpec(memory_space=space))
        arrays.append(operand)
    fetched = [
        pltpu.VMEM(arrays[position].shape[1:], arrays[position].dtype) for position in layers
    ]

    gathered = []
    if pieces is not None:
        first, count = pieces
        rows, columns = arrays[first].shape
        gathered = [pltpu.VMEM((count * rows, columns), arrays[first].dtype)]

    def kernel(*refs):
        if plain:
            body(*refs)
            return
        given = list(refs[: len(arrays)])
        rest = refs[len(arrays) : len(refs) - len(fetched) - 1]
        targets = refs[len(refs) - len(fetched) - 1 : -1]
        for index, (position, layer) in enumerate(layers.items()):
            given[position] = Fetch(given[position], layer, targets[index], refs[-1].at[index])
        if pieces is not None:
            first, count = pieces
            rows = given[first].shape[0]
            whole, rest = rest[-1], rest[:-1]
            for offset in range(count):
                source = lax.bitwise_xor(given[0][0], offset)
                whole[aligned(source * rows, rows), :] = given[first + offset][...]
            given[first : first + count] = [whole]
        body(*given, *rest)

    return pl.pallas_call(
        kernel,
        name=name,
        in_specs=specs,
        out_specs=[
            pl.BlockSpec(memory_space=pl.ANY if place in written else pltpu.VMEM)
            for place in range(len(outs))
        ],
        out_shape=[
            jax.ShapeDtypeStruct(shape, kind)
            if place in written or place in final
            else pltpu.VMEM(shape, kind)
            for place, (shape, kind) in enumerate(outs)
        ],
        scratch_shapes=[
            entry if not isinstance(entry, tuple) else pltpu.VMEM(*entry) for entry in scratch
        ]
        + gathered
        + fetched
        + ([] if plain else [pltpu.SemaphoreType.DMA((max(1, len(fetched)),))]),
        input_output_aliases=aliases or {},
        cost_estimate=pl.CostEstimate(
            flops=micros * 1_000_000_000, bytes_accessed=micros * 3_600_000, transcendentals=0
        ),
        compiler_params=pltpu.CompilerParams(vmem_limit_bytes=vmem_bytes),
    )(*arrays)


def on_device(
    inputs,
    doc_lengths,
    norm_gain,
    decay_log,
    frequency,
    step_log,
    in_weight,
    skip_weight,
    out_weight,
    glu_weight,
    cotangent,
):
    row_count, length, model = inputs.shape
    layer_count, width = decay_log.shape
    count = row_count * length
    device_count = lax.axis_size("seq")
    place = lax.axis_index("seq").astype(jnp.int32).reshape(1)
    rate_tables, rates_back = jax.vjp(rates, decay_log, frequency, step_log)
    tables = jnp.stack(rate_tables, axis=1).reshape(4 * layer_count, width)

    def gather(totals):
        if device_count != 8:
            return lax.all_gather(totals, "seq", axis=0, tiled=True)

        def from_other(array, bits):
            return lax.ppermute(
                array, "seq", [(index, index ^ bits) for index in range(device_count)]
            )

        pieces = [None] * device_count
        pieces[0] = totals
        for bits in range(2, device_count, 2):
            pieces[bits] = from_other(totals, bits)
        for bits in range(0, device_count, 2):
            pieces[bits + 1] = from_other(pieces[bits], 1)
        return pieces

    flags_out = ((3, count, lane_count), f32)
    blocks_out = ((2, device_count * row_count, lane_count), f32)
    wide_out = ((count, 4 * width), f32)
    ends_out = ((chunk_count, 4 * width), f32)
    totals_out = ((4 * row_count, width), f32)
    tokens = ((count, model), f32)
    tokens_low = ((count, model), bf16)
    drive_out = ((count, 2 * width), f32)
    bar_out = ((model, 2 * width), bf16)
    glu_out = ((model, model), f32)
    out_out = ((4 * width, model), f32)
    in_out = ((model, 2 * width), f32)
    vector = ((1, model), f32)

    def in_place(array):
        return pltpu.with_memory_space_constraint(array, pltpu.HBM)

    flags, blocks, values, scaled, drive, ends, totals = call(
        functools.partial(first_kernel, length),
        "first",
        (
            ("place", place),
            ("docs", in_place(doc_lengths)),
            ("inputs", in_place(inputs)),
            ("gain", in_place(norm_gain)),
            ("tables", tables),
            ("in", (in_weight, 0)),
        ),
        (flags_out, blocks_out, tokens_low, tokens_low, drive_out, ends_out, totals_out),
        (bar_out,),
    )
    shared = (("flags", flags), ("blocks", blocks), ("tables", tables))
    kept = []
    for layer in range(layer_count - 1):
        gathered = gather(totals)
        (
            states, low, enter, mixed, act, gate, next_values, next_scaled, drive, ends, totals,
        ) = call(
            functools.partial(middle_kernel, layer, length),
            "middle",
            (
                ("place", place),
                ("gathered", gathered),
                *shared,
                ("gain", norm_gain),
                ("skip", skip_weight),
                ("drive", drive),
                ("ends", ends),
                ("values", values),
                ("scaled", scaled),
                ("out", (out_weight, layer)),
                ("glu", (glu_weight, layer)),
                ("in", (in_weight, layer + 1)),
            ),
            (
                wide_out, ((count, 4 * width), bf16), ends_out, tokens, tokens_low, tokens,
                tokens, tokens_low, drive_out, ends_out, totals_out,
            ),
            (bar_out,),
        )
        kept.append((states, low, enter, mixed, act, gate, values, scaled))
        values, scaled = next_values, next_scaled
    layer = layer_count - 1
    gathered = gather(totals)
    small_out = ((8 * 2 * half_blocks, lane_count), f32)
    shapes = {
        "out": (layer_count, 4 * width, model),
        "glu": (layer_count, model, model),
        "in": (layer_count, model, 2 * width),
        "small": small_out[0],
    }
    sums = {}
    line = Line()
    layouts, goals, units = {}, {}, {}

    def unit_outs(entries):
        outs = []
        for name, keys, kind in entries:
            layouts[name] = unit_layout(keys, kind, model, width)
            outs.extend([((half_blocks * layouts[name].rows, layouts[name].columns), f32)] * 2)
        return tuple(outs)

    def open_units(entries, halves, layer_of):
        for index, (name, keys, kind) in enumerate(entries):
            units[name] = UnitSum(halves[2 * index], halves[2 * index + 1], kind)
            goals[name] = [(key, layer_of[key]) for key in keys]

    placed = set()

    def place_sums(name):
        placed.add(name)
        runs = line.settle(units[name].runs)
        place_unit(runs, layouts[name], goals[name], shapes, sums)
        line.last = [sums[key] for key, unused in goals[name]]

    def follow(plan, payload=()):
        for group in plan.split():
            if group.isupper():
                for name in group.lower():
                    if units[name].runs is not None and name not in placed:
                        place_sums(name)
            elif group[0] == "=":
                payload = line.advance([units[name] for name in group[1:]], payload)
            else:
                line.advance([units[name] for name in group])
        return payload

    results = call(
        functools.partial(turn_kernel, layer, length),
        "turn",
        (
            ("place", place),
            ("gathered", gathered),
            *shared,
            ("skip", skip_weight),
            ("drive", drive),
            ("ends", ends),
            ("values", values),
            ("scaled", scaled),
            ("out", (out_weight, layer)),
            ("glu", (glu_weight, layer)),
            ("cotangent", cotangent),
        ),
        (
            *unit_outs(turn_units), (inputs.shape, bf16), tokens, wide_out, ends_out, tokens, wide_out,
            vector, ends_out, totals_out,
        ),
        (
            ((count, 4 * width), bf16), tokens, tokens_low, tokens, tokens_low, tokens_low, tokens,
            tokens_low, glu_out, out_out,
        ),
        final=(2 * len(turn_units),),
        micros=6,
    )
    halves, results = results[: 2 * len(turn_units)], results[2 * len(turn_units) :]
    output, grad, states, enter, d_mixed, d_states, skip_grad, ends, totals = results
    open_units(turn_units, halves, {"out": layer, "glu": layer})
    gathered = follow(into_middle, gather(follow(after_turn, totals)))
    back_scratch = (
        drive_out, drive_out, ((count, 2 * width), bf16), bar_out, tokens,
    )
    rate_out = ((4, width), f32)
    low_states, low, low_enter, mixed, act, gate, low_values, low_scaled = kept[0]
    results = call(
        functools.partial(back_middle_kernel, layer, length),
        "back_middle",
        (
            ("place", place),
            ("gathered", gathered),
            *shared,
            ("gain", norm_gain),
            ("skip", skip_weight),
            ("in", (in_weight, layer)),
            ("d_states", d_states),
            ("ends", ends),
            ("states", states),
            ("enter", enter),
            ("scaled", scaled),
            ("values", values),
            ("d_mixed", d_mixed),
            ("grad", grad),
            ("out", (out_weight, layer - 1)),
            ("glu", (glu_weight, layer - 1)),
            ("mixed", mixed),
            ("act", act),
            ("gate", gate),
            ("below_scaled", low_scaled),
            ("low", low),
        ),
        (
            *unit_outs(middle_units), vector, rate_out, tokens, tokens, wide_out, vector, ends_out,
            totals_out,
        ),
        back_scratch + (tokens_low, tokens_low, in_out, glu_out, out_out),
        micros=6,
    )
    halves, results = results[: 2 * len(middle_units)], results[2 * len(middle_units) :]
    gain_grad, rate_grad, grad, d_mixed, d_states, low_skip_grad, ends, totals = results
    open_units(middle_units, halves, {"out": layer - 1, "glu": layer - 1, "in": layer})
    gathered = follow(into_last, gather(follow(after_middle, totals)))
    keep, send, input_grad = call(
        functools.partial(back_last_kernel, length),
        "back_last",
        (
            ("place", place),
            ("gathered", gathered),
            *shared,
            ("gain", norm_gain),
            ("skip", skip_weight),
            ("in", (in_weight, 0)),
            ("d_states", d_states),
            ("ends", ends),
            ("states", low_states),
            ("enter", low_enter),
            ("scaled", low_scaled),
            ("values", low_values),
            ("d_mixed", d_mixed),
            ("grad", grad),
            ("skip_grad", low_skip_grad),
            ("skip_grad", skip_grad),
            ("gain_grad", gain_grad),
            ("rate_grad", rate_grad),
        ),
        (*unit_outs(last_units), (inputs.shape, bf16)),
        back_scratch + (tokens_low, in_out, vector, rate_out, small_out),
        final=(2,),
        micros=4,
    )
    open_units(last_units, (keep, send), {"in": 0, "small": None})
    follow(after_last)
    for name, unit in units.items():
        while unit.runs is None:
            follow(name)
    for name in units:
        if name not in placed:
            place_sums(name)
    small = sums["small"]

    def taken(first, shape):
        rows = math.prod(shape) // lane_count
        return small[first : first + rows].reshape(shape), first + rows

    gain_sum, row = taken(0, (layer_count, model))
    skip_sum, row = taken(row, (layer_count, model))
    rate_sum, row = taken(row, (layer_count, 4, width))
    decay_grad, frequency_grad, step_grad = rates_back(
        tuple(rate_sum[:, member] for member in range(4))
    )
    return (
        output,
        input_grad,
        gain_sum,
        decay_grad,
        frequency_grad,
        step_grad,
        sums["in"],
        skip_sum,
        sums["out"],
        sums["glu"],
    )


def solution(mesh):
    in_specs = (
        P("batch", "seq", None),
        P("batch", None),
        P(),
        P(),
        P(),
        P(),
        P(),
        P(),
        P(),
        P(),
        P("batch", "seq", None),
    )
    out_specs = (
        P("batch", "seq", None),
        P("batch", "seq", None),
        P(),
        P(),
        P(),
        P(),
        P(),
        P(),
        P(),
        P(),
    )
    return jax.shard_map(
        on_device, mesh=mesh, in_specs=in_specs, out_specs=out_specs, check_vma=False
    )
```

```python
import functools
import math

import jax
import jax.numpy as jnp
from jax import lax
from jax.experimental import pallas as pl
from jax.experimental.pallas import tpu as pltpu
from jax.sharding import PartitionSpec as P

epsilon = 1e-05
chunk_count = 8
lane_count = 128
block_rows = 32
vmem_bytes = 32 * 1024 * 1024
gelu_scale = math.sqrt(2.0 / math.pi)
gelu_cubic = 0.044715
f32 = jnp.float32
bf16 = jnp.bfloat16


def complex_mul(left_real, left_imag, right_real, right_imag):
    return (
        left_real * right_real - left_imag * right_imag,
        left_real * right_imag + left_imag * right_real,
    )


def complex_power(real, imag, exponent):
    result = None
    while exponent:
        if exponent & 1:
            result = (real, imag) if result is None else complex_mul(*result, real, imag)
        exponent >>= 1
        if exponent:
            real, imag = complex_mul(real, imag, real, imag)
    return result


def rates(decay_log, frequency, step_log):
    step_size = jnp.exp(step_log)
    pole_real = -jnp.exp(decay_log)
    shrink = step_size * pole_real
    rotation = step_size * frequency
    radius = jnp.exp(shrink)
    decay_real = radius * jnp.cos(rotation)
    decay_imag = radius * jnp.sin(rotation)
    minus_real = jnp.expm1(shrink) * jnp.cos(rotation) - 2.0 * jnp.sin(0.5 * rotation) ** 2
    modulus = pole_real * pole_real + frequency * frequency
    factor_real = (minus_real * pole_real + decay_imag * frequency) / modulus
    factor_imag = (decay_imag * pole_real - minus_real * frequency) / modulus
    return (decay_real, decay_imag, factor_real, factor_imag)


def dot(left, right):
    return lax.dot_general(left, right, (((1,), (0,)), ((), ())), preferred_element_type=f32)


def dot_right(left, right):
    return lax.dot_general(left, right, (((1,), (1,)), ((), ())), preferred_element_type=f32)


def dot_left(left, right):
    return lax.dot_general(left, right, (((0,), (0,)), ((), ())), preferred_element_type=f32)


def spread(narrow, width):
    return jnp.concatenate([narrow] * (width // lane_count), axis=1)


def order_matrix(count, inverse):
    rows = lax.broadcasted_iota(jnp.int32, (count, count), 0)
    cols = lax.broadcasted_iota(jnp.int32, (count, count), 1)
    if inverse:
        rows, cols = cols, rows
    source = lax.rem(rows, chunk_count) * (count // chunk_count) + lax.div(rows, chunk_count)
    return jnp.where(cols == source, 1.0, 0.0).astype(bf16)


def over_blocks(count, body):
    def one(index, carry):
        body(pl.ds(pl.multiple_of(index * block_rows, block_rows), block_rows))
        return carry

    lax.fori_loop(0, count // block_rows, one, 0, unroll=min(8, count // block_rows))


def normalize(values):
    average = jnp.mean(values, axis=-1, keepdims=True)
    centered = values - average
    inverse = lax.rsqrt(jnp.mean(centered * centered, axis=-1, keepdims=True) + epsilon)
    return centered * inverse, inverse


def gelu_parts(mixed):
    square = mixed * mixed
    bend = jnp.tanh(gelu_scale * mixed * (1.0 + gelu_cubic * square))
    half = 0.5 + 0.5 * bend
    slope = half + 0.5 * mixed * (1.0 - bend * bend) * gelu_scale * (
        1.0 + 3.0 * gelu_cubic * square
    )
    return mixed * half, slope


def write_flags(place, docs_ref, flags_ref, blocks_ref, length):
    row_count, doc_count = docs_ref.shape
    span = row_count * length // chunk_count
    per_row = chunk_count // row_count
    offsets = []
    for row in range(row_count):
        running = [jnp.int32(0)]
        for doc in range(doc_count):
            running.append(running[-1] + docs_ref[row, doc])
        offsets.append(running)

    def by_row(row_of, member):
        chosen = jnp.full(row_of.shape, offsets[0][member], jnp.int32)
        for row in range(1, row_count):
            chosen = jnp.where(row_of == row, offsets[row][member], chosen)
        return chosen

    chunk = lax.broadcasted_iota(jnp.int32, (chunk_count, lane_count), 0)
    row_of = lax.div(chunk, per_row)
    bounds = [by_row(row_of, member) for member in range(doc_count + 1)]
    base = place * length + lax.rem(chunk, per_row) * span
    for step in range(span):
        position = base + step
        starts = position == bounds[0]
        endings = position + 1 == bounds[0]
        for bound in bounds[1:]:
            starts = starts | (position == bound)
            endings = endings | (position + 1 == bound)
        window = pl.ds(chunk_count * step, chunk_count)
        flags_ref[0, window, :] = jnp.where(starts, 0.0, 1.0)
        flags_ref[1, window, :] = jnp.where(endings, 0.0, 1.0)
        flags_ref[2, window, :] = jnp.where(position < bounds[-1], 1.0, 0.0)
    entry = lax.broadcasted_iota(jnp.int32, blocks_ref.shape[1:], 0)
    row_of = lax.rem(entry, row_count)
    first = lax.div(entry, row_count) * length
    starts = jnp.zeros(entry.shape, jnp.bool_)
    endings = starts
    for member in range(doc_count + 1):
        bound = by_row(row_of, member)
        starts = starts | ((bound >= first) & (bound < first + length))
        endings = endings | ((bound > first) & (bound <= first + length))
    blocks_ref[0] = jnp.where(starts, 0.0, 1.0)
    blocks_ref[1] = jnp.where(endings, 0.0, 1.0)


def chunk_keeps(flags_ref):
    span = flags_ref.shape[1] // chunk_count
    ahead = flags_ref[0, :chunk_count, :]
    behind = flags_ref[1, :chunk_count, :]
    for step in range(1, span):
        window = pl.ds(chunk_count * step, chunk_count)
        ahead = ahead * flags_ref[0, window, :]
        behind = behind * flags_ref[1, window, :]
    return ahead, behind


def toward(array, distance, reverse):
    return pltpu.roll(array, chunk_count - distance if reverse else distance, axis=0)


def chunk_prefix(ends, factor, entering, per_row, reverse):
    width = ends[0].shape[1]
    chunk = lax.broadcasted_iota(jnp.int32, (chunk_count, width), 0)
    within = lax.rem(chunk, per_row)
    within = per_row - 1 - within if reverse else within
    first = within == 0
    total_real, total_imag = ends
    if entering is not None:
        moved_real, moved_imag = complex_mul(*factor, *entering)
        total_real = total_real + jnp.where(first, moved_real, 0.0)
        total_imag = total_imag + jnp.where(first, moved_imag, 0.0)
    distance = 1
    while distance < per_row:
        reach = within >= distance
        near_real = toward(total_real, distance, reverse)
        near_imag = toward(total_imag, distance, reverse)
        moved_real, moved_imag = complex_mul(*factor, near_real, near_imag)
        total_real = total_real + jnp.where(reach, moved_real, 0.0)
        total_imag = total_imag + jnp.where(reach, moved_imag, 0.0)
        if 2 * distance < per_row:
            far_real = toward(factor[0], distance, reverse)
            far_imag = toward(factor[1], distance, reverse)
            both_real, both_imag = complex_mul(*factor, far_real, far_imag)
            factor = (
                jnp.where(reach, both_real, factor[0]),
                jnp.where(reach, both_imag, factor[1]),
            )
        distance *= 2
    enter_real = toward(total_real, 1, reverse)
    enter_imag = toward(total_imag, 1, reverse)
    none = (jnp.zeros_like(total_real),) * 2 if entering is None else entering
    return (
        (total_real, total_imag),
        (jnp.where(first, none[0], enter_real), jnp.where(first, none[1], enter_imag)),
    )


def sweep(flags_ref, pole_real, pole_imag, forward_at, reverse_at, start, put_forward, put_reverse):
    width = pole_real.shape[1]
    span = flags_ref.shape[1] // chunk_count

    def one(step, state):
        ahead_real, ahead_imag, behind_real, behind_imag = state
        here = pl.ds(pl.multiple_of(chunk_count * step, chunk_count), chunk_count)
        there = pl.ds(pl.multiple_of(chunk_count * (span - 1 - step), chunk_count), chunk_count)
        keep = spread(flags_ref[0, here, :], width)
        moved_real, moved_imag = complex_mul(pole_real * keep, pole_imag * keep, ahead_real, ahead_imag)
        drive_real, drive_imag = forward_at(here)
        ahead_real = moved_real + drive_real
        ahead_imag = moved_imag + drive_imag
        keep = spread(flags_ref[1, there, :], width)
        moved_real, moved_imag = complex_mul(
            pole_real * keep, pole_imag * keep, behind_real, behind_imag
        )
        drive_real, drive_imag = reverse_at(there)
        behind_real = moved_real + drive_real
        behind_imag = moved_imag + drive_imag
        if put_forward is not None:
            put_forward(here, ahead_real, ahead_imag)
            put_reverse(there, behind_real, behind_imag)
        return (ahead_real, ahead_imag, behind_real, behind_imag)

    return lax.fori_loop(0, span, one, start, unroll=4)


def local_totals(flags_ref, pole_real, pole_imag, forward_at, reverse_at, ends_ref, totals_ref):
    width = pole_real.shape[1]
    span = flags_ref.shape[1] // chunk_count
    row_count = totals_ref.shape[0] // 4
    per_row = chunk_count // row_count
    pole_real = jnp.broadcast_to(pole_real, (chunk_count, width))
    pole_imag = jnp.broadcast_to(pole_imag, (chunk_count, width))
    zero = jnp.zeros((chunk_count, width), f32)
    ends = sweep(
        flags_ref, pole_real, pole_imag, forward_at, reverse_at, (zero,) * 4, None, None
    )
    for member in range(4):
        ends_ref[:, member * width : (member + 1) * width] = ends[member]
    power_real, power_imag = complex_power(pole_real, pole_imag, span)
    for direction, keep in enumerate(chunk_keeps(flags_ref)):
        keep = spread(keep, width)
        pair = ends[2 * direction : 2 * direction + 2]
        totals, unused = chunk_prefix(
            pair, (power_real * keep, power_imag * keep), None, per_row, direction == 1
        )
        for part in range(2):
            for row in range(row_count):
                chunk = row * per_row if direction == 1 else (row + 1) * per_row - 1
                entry = (2 * direction + part) * row_count + row
                totals_ref[entry : entry + 1, :] = totals[part][chunk : chunk + 1, :]


def chunk_entrances(place, gathered_ref, flags_ref, blocks_ref, ends_ref, pole_real, pole_imag, length):
    width = pole_real.shape[1]
    span = flags_ref.shape[1] // chunk_count
    row_count = chunk_count * span // length
    per_row = chunk_count // row_count
    device_count = gathered_ref.shape[0] // (4 * row_count)
    pole_real = jnp.broadcast_to(pole_real, (chunk_count, width))
    pole_imag = jnp.broadcast_to(pole_imag, (chunk_count, width))
    power_real, power_imag = complex_power(pole_real, pole_imag, span)
    device_real, device_imag = complex_power(power_real, power_imag, per_row)
    device_real = device_real[:row_count]
    device_imag = device_imag[:row_count]
    entrances = []
    for direction, keep in enumerate(chunk_keeps(flags_ref)):
        real = jnp.zeros((row_count, width), f32)
        imag = real
        for lap in range(device_count):
            source = device_count - 1 - lap if direction == 1 else lap
            live = source > place if direction == 1 else source < place
            open_ = spread(
                blocks_ref[direction, source * row_count : (source + 1) * row_count, :], width
            )
            moved_real, moved_imag = complex_mul(device_real * open_, device_imag * open_, real, imag)
            first = (4 * source + 2 * direction) * row_count
            moved_real = moved_real + gathered_ref[first : first + row_count, :]
            moved_imag = moved_imag + gathered_ref[first + row_count : first + 2 * row_count, :]
            real = jnp.where(live, moved_real, real)
            imag = jnp.where(live, moved_imag, imag)
        entering = tuple(
            jnp.concatenate(
                [
                    jnp.broadcast_to(part[row : row + 1, :], (per_row, width))
                    for row in range(row_count)
                ],
                axis=0,
            )
            for part in (real, imag)
        )
        keep = spread(keep, width)
        first = 2 * direction * width
        ends = (ends_ref[:, first : first + width], ends_ref[:, first + width : first + 2 * width])
        unused, entrance = chunk_prefix(
            ends, (power_real * keep, power_imag * keep), entering, per_row, direction == 1
        )
        entrances.extend(entrance)
    return tuple(entrances)


def layer_poles(tables_ref, layer):
    return tables_ref[4 * layer : 4 * layer + 1, :], tables_ref[4 * layer + 1 : 4 * layer + 2, :]


def layer_factors(tables_ref, layer):
    return tables_ref[4 * layer + 2 : 4 * layer + 3, :], tables_ref[4 * layer + 3 : 4 * layer + 4, :]


def write_bar(tables_ref, layer, in_ref, bar_ref):
    width = tables_ref.shape[1]
    factor_real, factor_imag = layer_factors(tables_ref, layer)

    def body(rows):
        weight_real = in_ref[rows, :width].astype(f32)
        weight_imag = in_ref[rows, width:].astype(f32)
        real, imag = complex_mul(factor_real, factor_imag, weight_real, weight_imag)
        bar_ref[rows, :width] = real.astype(bf16)
        bar_ref[rows, width:] = imag.astype(bf16)

    over_blocks(in_ref.shape[0], body)


def pair_at(ref, first, width):
    def at(rows):
        return ref[rows, first : first + width], ref[rows, first + width : first + 2 * width]

    return at


def drive_totals(flags_ref, tables_ref, layer, scaled_ref, in_ref, bar_ref, drive_ref, ends_ref, totals_ref):
    width = tables_ref.shape[1]
    write_bar(tables_ref, layer, in_ref.ready(), bar_ref)
    drive_ref[...] = dot(scaled_ref[...], bar_ref[...])
    at = pair_at(drive_ref, 0, width)
    local_totals(flags_ref, *layer_poles(tables_ref, layer), at, at, ends_ref, totals_ref)


def settled_states(
    place, gathered_ref, flags_ref, blocks_ref, tables_ref, layer, drive_ref, ends_ref, length,
    states_ref, low_ref, enter_ref,
):
    width = tables_ref.shape[1]
    pole_real, pole_imag = layer_poles(tables_ref, layer)
    entrances = chunk_entrances(
        place, gathered_ref, flags_ref, blocks_ref, ends_ref, pole_real, pole_imag, length
    )
    for member in range(4):
        enter_ref[:, member * width : (member + 1) * width] = entrances[member]

    def put_forward(rows, real, imag):
        states_ref[rows, :width] = real
        states_ref[rows, width : 2 * width] = imag

    def put_reverse(rows, real, imag):
        states_ref[rows, 2 * width : 3 * width] = real
        states_ref[rows, 3 * width :] = imag

    at = pair_at(drive_ref, 0, width)
    sweep(
        flags_ref,
        jnp.broadcast_to(pole_real, (chunk_count, width)),
        jnp.broadcast_to(pole_imag, (chunk_count, width)),
        at, at, entrances, put_forward, put_reverse,
    )

    def body(rows):
        low_ref[rows, :] = states_ref[rows, :].astype(bf16)

    over_blocks(states_ref.shape[0], body)


def mix_and_gate(layer, low_ref, scaled_ref, out_ref, glu_ref, skip_ref, mixed_ref, act_ref, gate_ref):
    mixed_ref[...] = dot(low_ref[...], out_ref.ready()[...])
    skip = skip_ref[layer : layer + 1, :]

    def body(rows):
        mixed = mixed_ref[rows, :] + skip * scaled_ref[rows, :].astype(f32)
        mixed_ref[rows, :] = mixed
        act_ref[rows, :] = gelu_parts(mixed)[0].astype(bf16)

    over_blocks(mixed_ref.shape[0], body)
    gate_ref[...] = dot(act_ref[...], glu_ref.ready()[...])


def back_tail(
    layer, flags_ref, tables_ref, grad_ref, mixed_ref, act_ref, gate_ref, scaled_ref, low_ref,
    out_ref, glu_ref, skip_ref, logits_ref, work_ref, mixed_low_ref,
    d_mixed_ref, d_states_ref, glu_grad_ref, out_grad_ref, skip_grad_ref, ends_ref, totals_ref, emit,
):
    width = tables_ref.shape[1]
    model = mixed_ref.shape[1]

    def first(rows):
        valid = spread(flags_ref[2, rows, :], model)
        gate = gate_ref[rows, :]
        rate = grad_ref[rows, :] * valid * gate
        logits_ref[rows, :] = (rate * act_ref[rows, :].astype(f32) * (1.0 - gate)).astype(bf16)

    over_blocks(mixed_ref.shape[0], first)
    glu_grad_ref[...] = dot_left(act_ref[...], logits_ref[...])
    emit.put("glu", glu_grad_ref)
    work_ref[...] = dot_right(logits_ref[...], glu_ref.ready()[...])
    skip_grad_ref[...] = jnp.zeros(skip_grad_ref.shape, f32)

    def second(rows):
        valid = spread(flags_ref[2, rows, :], model)
        d_act = grad_ref[rows, :] * valid * gate_ref[rows, :] + work_ref[rows, :]
        d_mixed = d_act * gelu_parts(mixed_ref[rows, :])[1]
        d_mixed_ref[rows, :] = d_mixed
        mixed_low_ref[rows, :] = d_mixed.astype(bf16)
        skip_grad_ref[...] += jnp.sum(
            d_mixed * scaled_ref[rows, :].astype(f32), axis=0, keepdims=True
        )

    over_blocks(mixed_ref.shape[0], second)
    out_grad_ref[...] = dot_left(low_ref[...], mixed_low_ref[...])
    emit.put("out", out_grad_ref)
    d_states_ref[...] = dot_right(mixed_low_ref[...], out_ref.ready()[...])
    pole_real, pole_imag = layer_poles(tables_ref, layer)
    local_totals(
        flags_ref, pole_real, -pole_imag, pair_at(d_states_ref, 2 * width, width),
        pair_at(d_states_ref, 0, width), ends_ref, totals_ref,
    )


def back_front(
    place, layer, length, gathered_ref, flags_ref, blocks_ref, tables_ref, gain_ref, skip_ref, in_ref,
    d_states_ref, ends_ref, states_ref, enter_ref, scaled_ref, values_ref, d_mixed_ref, grad_ref,
    lam_ref, mu_ref, low_ref, bar_ref, work_ref,
    in_grad_ref, gain_grad_ref, rate_grad_ref, put_gradient, emit,
):
    width = tables_ref.shape[1]
    model = values_ref.shape[1]
    count = values_ref.shape[0]
    pole_real, pole_imag = layer_poles(tables_ref, layer)
    entrances = chunk_entrances(
        place, gathered_ref, flags_ref, blocks_ref, ends_ref, pole_real, -pole_imag, length
    )

    def put_forward(rows, real, imag):
        mu_ref[rows, :width] = real
        mu_ref[rows, width:] = imag

    def put_reverse(rows, real, imag):
        lam_ref[rows, :width] = real
        lam_ref[rows, width:] = imag

    sweep(
        flags_ref,
        jnp.broadcast_to(pole_real, (chunk_count, width)),
        jnp.broadcast_to(-pole_imag, (chunk_count, width)),
        pair_at(d_states_ref, 2 * width, width), pair_at(d_states_ref, 0, width),
        entrances, put_forward, put_reverse,
    )
    span = count // chunk_count

    def decay_terms(here, before_real, before_imag, after_real, after_imag, sums):
        keep = spread(flags_ref[0, here, :], width)
        lam_real, lam_imag = lam_ref[here, :width], lam_ref[here, width:]
        mu_real, mu_imag = mu_ref[here, :width], mu_ref[here, width:]
        real = keep * (lam_real * before_real + lam_imag * before_imag)
        imag = keep * (lam_imag * before_real - lam_real * before_imag)
        keep = spread(flags_ref[1, here, :], width)
        real = real + keep * (mu_real * after_real + mu_imag * after_imag)
        imag = imag + keep * (mu_imag * after_real - mu_real * after_imag)
        return sums[0] + real, sums[1] + imag

    def window(step):
        start = chunk_count * step
        return pl.ds(start if isinstance(step, int) else pl.multiple_of(start, chunk_count), chunk_count)

    def before_at(step):
        rows = window(step)
        return states_ref[rows, :width], states_ref[rows, width : 2 * width]

    def after_at(step):
        rows = window(step)
        return states_ref[rows, 2 * width : 3 * width], states_ref[rows, 3 * width :]

    def middle(step, sums):
        return decay_terms(window(step), *before_at(step - 1), *after_at(step + 1), sums)

    zero = jnp.zeros((chunk_count, width), f32)
    sums = decay_terms(
        window(0), enter_ref[:, :width], enter_ref[:, width : 2 * width], *after_at(1), (zero, zero)
    )
    sums = lax.fori_loop(1, span - 1, middle, sums, unroll=2)
    sums = decay_terms(
        window(span - 1), *before_at(span - 2),
        enter_ref[:, 2 * width : 3 * width], enter_ref[:, 3 * width :], sums,
    )
    rate_grad_ref[0:1, :] = jnp.sum(sums[0], axis=0, keepdims=True)
    rate_grad_ref[1:2, :] = jnp.sum(sums[1], axis=0, keepdims=True)

    def narrow(rows):
        low_ref[rows, :] = (lam_ref[rows, :] + mu_ref[rows, :]).astype(bf16)

    over_blocks(count, narrow)
    in_ref = in_ref.ready()
    write_bar(tables_ref, layer, in_ref, bar_ref)
    work_ref[...] = dot_right(low_ref[...], bar_ref[...])
    skip = skip_ref[layer : layer + 1, :]
    gain = gain_ref[layer : layer + 1, :]
    gain_grad_ref[...] = jnp.zeros(gain_grad_ref.shape, f32)

    def norm_back(rows):
        valid = spread(flags_ref[2, rows, :], model)
        normed, inverse = normalize(values_ref[rows, :].astype(f32))
        d_scaled = (work_ref[rows, :] + d_mixed_ref[rows, :] * skip) * valid
        gain_grad_ref[...] += jnp.sum(d_scaled * normed, axis=0, keepdims=True)
        d_normed = d_scaled * gain
        put_gradient(
            rows,
            inverse
            * (
                d_normed
                - jnp.mean(d_normed, axis=-1, keepdims=True)
                - normed * jnp.mean(d_normed * normed, axis=-1, keepdims=True)
            )
            + grad_ref[rows, :].astype(f32),
        )

    over_blocks(count, norm_back)
    in_grad_ref[...] = dot_left(scaled_ref[...], low_ref[...])
    factor_real, factor_imag = layer_factors(tables_ref, layer)
    rate_grad_ref[2:4, :] = jnp.zeros((2, width), f32)

    def weigh(rows):
        grad_real, grad_imag = in_grad_ref[rows, :width], in_grad_ref[rows, width:]
        weight_real = in_ref[rows, :width].astype(f32)
        weight_imag = in_ref[rows, width:].astype(f32)
        rate_grad_ref[2:3, :] += jnp.sum(
            grad_real * weight_real + grad_imag * weight_imag, axis=0, keepdims=True
        )
        rate_grad_ref[3:4, :] += jnp.sum(
            grad_imag * weight_real - grad_real * weight_imag, axis=0, keepdims=True
        )
        in_grad_ref[rows, :width] = factor_real * grad_real + factor_imag * grad_imag
        in_grad_ref[rows, width:] = factor_real * grad_imag - factor_imag * grad_real

    over_blocks(in_ref.shape[0], weigh)
    emit.put("in", in_grad_ref)


def first_kernel(
    length, place_ref, docs_ref, inputs_ref, gain_ref, tables_ref, in_ref,
    flags_ref, blocks_ref, values_ref, scaled_ref, drive_ref, ends_ref, totals_ref, bar_ref,
):
    write_flags(place_ref[0], docs_ref, flags_ref, blocks_ref, length)
    count, model = values_ref.shape
    values_ref[...] = dot(
        order_matrix(count, False), inputs_ref[...].reshape(count, model)
    ).astype(bf16)
    gain = gain_ref[0:1, :]

    def body(rows):
        normed, unused = normalize(values_ref[rows, :].astype(f32))
        valid = spread(flags_ref[2, rows, :], model)
        scaled_ref[rows, :] = (normed * gain * valid).astype(bf16)

    over_blocks(count, body)
    drive_totals(
        flags_ref, tables_ref, 0, scaled_ref, in_ref, bar_ref, drive_ref, ends_ref, totals_ref
    )


def middle_kernel(
    layer, length, place_ref, gathered_ref, flags_ref, blocks_ref, tables_ref, gain_ref, skip_ref,
    drive_ref, ends_ref, values_ref, scaled_ref, out_ref, glu_ref, in_ref,
    states_ref, low_ref, enter_ref, mixed_ref, act_ref, gate_ref,
    next_values_ref, next_scaled_ref, next_drive_ref, next_ends_ref, next_totals_ref, bar_ref,
):
    settled_states(
        place_ref[0], gathered_ref, flags_ref, blocks_ref, tables_ref, layer, drive_ref, ends_ref, length,
        states_ref, low_ref, enter_ref,
    )
    mix_and_gate(
        layer, low_ref, scaled_ref, out_ref, glu_ref, skip_ref, mixed_ref, act_ref, gate_ref
    )
    model = values_ref.shape[1]
    gain = gain_ref[layer + 1 : layer + 2, :]

    def body(rows):
        valid = spread(flags_ref[2, rows, :], model)
        gate = jax.nn.sigmoid(gate_ref[rows, :])
        gate_ref[rows, :] = gate
        result = values_ref[rows, :].astype(f32) + valid * act_ref[rows, :].astype(f32) * gate
        next_values_ref[rows, :] = result
        normed, unused = normalize(result)
        next_scaled_ref[rows, :] = (normed * gain * valid).astype(bf16)

    over_blocks(values_ref.shape[0], body)
    drive_totals(
        flags_ref, tables_ref, layer + 1, next_scaled_ref, in_ref, bar_ref, next_drive_ref,
        next_ends_ref, next_totals_ref,
    )


def turn_kernel(
    layer, length, place_ref, gathered_ref, flags_ref, blocks_ref, tables_ref, skip_ref,
    drive_ref, ends_ref, values_ref, scaled_ref, out_ref, glu_ref, cotangent_ref,
    *rest,
):
    unit_refs, rest = rest[: 2 * len(turn_units)], rest[2 * len(turn_units) :]
    (
        output_ref, grad_ref, states_ref, enter_ref, d_mixed_ref, d_states_ref,
        skip_grad_ref, back_ends_ref, back_totals_ref, glu_grad_ref,
        low_ref, mixed_ref, act_ref, gate_ref, result_ref, logits_ref, work_ref, mixed_low_ref,
        out_grad_ref,
    ) = rest
    emit = Emit(turn_units, unit_refs, values_ref.shape[1], tables_ref.shape[1])
    settled_states(
        place_ref[0], gathered_ref, flags_ref, blocks_ref, tables_ref, layer, drive_ref, ends_ref, length,
        states_ref, low_ref, enter_ref,
    )
    mix_and_gate(
        layer, low_ref, scaled_ref, out_ref, glu_ref, skip_ref, mixed_ref, act_ref, gate_ref
    )
    count, model = values_ref.shape

    def body(rows):
        valid = spread(flags_ref[2, rows, :], model)
        gate = jax.nn.sigmoid(gate_ref[rows, :])
        gate_ref[rows, :] = gate
        result = values_ref[rows, :] + valid * act_ref[rows, :].astype(f32) * gate
        result_ref[rows, :] = result.astype(bf16)

    over_blocks(count, body)
    output_ref[...] = (
        dot(order_matrix(count, True), result_ref[...]).astype(bf16).reshape(output_ref.shape)
    )
    grad_ref[...] = dot(order_matrix(count, False), cotangent_ref[...].reshape(count, model))
    back_tail(
        layer, flags_ref, tables_ref, grad_ref, mixed_ref, act_ref, gate_ref, scaled_ref, low_ref,
        out_ref, glu_ref, skip_ref, logits_ref, work_ref, mixed_low_ref,
        d_mixed_ref, d_states_ref, glu_grad_ref, out_grad_ref, skip_grad_ref, back_ends_ref,
        back_totals_ref, emit,
    )


def back_middle_kernel(
    layer, length, place_ref, gathered_ref, flags_ref, blocks_ref, tables_ref, gain_ref, skip_ref, in_ref,
    d_states_ref, ends_ref, states_ref, enter_ref, scaled_ref, values_ref, d_mixed_ref, grad_ref,
    out_ref, glu_ref, below_mixed_ref, below_act_ref, below_gate_ref, below_scaled_ref, below_low_ref,
    over_grad_ref, *rest,
):
    unit_refs, rest = rest[: 2 * len(middle_units)], rest[2 * len(middle_units) :]
    (
        gain_grad_ref, rate_grad_ref, next_grad_ref, below_d_mixed_ref,
        below_d_states_ref, skip_grad_ref, below_ends_ref, below_totals_ref,
        lam_ref, mu_ref, low_ref, bar_ref, work_ref, logits_ref, mixed_low_ref,
        in_grad_ref, glu_grad_ref, out_grad_ref,
    ) = rest
    emit = Emit(middle_units, unit_refs, values_ref.shape[1], tables_ref.shape[1])
    emit.put("over", over_grad_ref)

    def put_gradient(rows, gradient):
        next_grad_ref[rows, :] = gradient

    back_front(
        place_ref[0], layer, length, gathered_ref, flags_ref, blocks_ref, tables_ref, gain_ref, skip_ref,
        in_ref, d_states_ref, ends_ref, states_ref, enter_ref, scaled_ref, values_ref, d_mixed_ref,
        grad_ref, lam_ref, mu_ref, low_ref, bar_ref, work_ref,
        in_grad_ref, gain_grad_ref, rate_grad_ref, put_gradient, emit,
    )
    back_tail(
        layer - 1, flags_ref, tables_ref, next_grad_ref, below_mixed_ref, below_act_ref, below_gate_ref,
        below_scaled_ref, below_low_ref, out_ref, glu_ref, skip_ref, logits_ref, work_ref, mixed_low_ref,
        below_d_mixed_ref, below_d_states_ref, glu_grad_ref, out_grad_ref, skip_grad_ref,
        below_ends_ref, below_totals_ref, emit,
    )


def back_last_kernel(
    length, place_ref, gathered_ref, flags_ref, blocks_ref, tables_ref, gain_ref, skip_ref, in_ref,
    d_states_ref, ends_ref, states_ref, enter_ref, scaled_ref, values_ref, d_mixed_ref, grad_ref,
    *rest,
):
    layer_count = gain_ref.shape[0]
    skip_grads = rest[:layer_count]
    rest = rest[layer_count:]
    gain_grads = rest[: layer_count - 1]
    rate_grads = rest[layer_count - 1 : 2 * layer_count - 2]
    unit_refs = rest[2 * layer_count - 2 : 2 * layer_count]
    (
        input_grad_ref,
        lam_ref, mu_ref, low_ref, bar_ref, work_ref, result_ref,
        in_grad_ref, gain_grad_ref, rate_grad_ref, small_ref,
    ) = rest[2 * layer_count :]
    emit = Emit(last_units, unit_refs, values_ref.shape[1], tables_ref.shape[1])
    def put_gradient(rows, gradient):
        result_ref[rows, :] = gradient.astype(bf16)

    back_front(
        place_ref[0], 0, length, gathered_ref, flags_ref, blocks_ref, tables_ref, gain_ref, skip_ref,
        in_ref, d_states_ref, ends_ref, states_ref, enter_ref, scaled_ref, values_ref, d_mixed_ref,
        grad_ref, lam_ref, mu_ref, low_ref, bar_ref, work_ref,
        in_grad_ref, gain_grad_ref, rate_grad_ref, put_gradient, emit,
    )
    small_ref[...] = jnp.zeros(small_ref.shape, f32)
    row = 0
    for vectors in ((gain_grad_ref, *gain_grads), skip_grads, (rate_grad_ref, *rate_grads)):
        for vector_ref in vectors:
            for line in range(vector_ref.shape[0]):
                for first in range(0, vector_ref.shape[1], lane_count):
                    small_ref[row : row + 1, :] = vector_ref[line : line + 1, first : first + lane_count]
                    row += 1
    emit.put("small", small_ref)
    count = result_ref.shape[0]
    input_grad_ref[...] = (
        dot(order_matrix(count, True), result_ref[...]).astype(bf16).reshape(input_grad_ref.shape)
    )


halvings = 3
half_blocks = 1 << halvings
turn_units = (("a", ("out", "glu"), "plane"),)
middle_units = (("b", ("out", "glu"), "plane"), ("d", ("in",), "plane"))
last_units = (("c", ("in", "small"), "plane"),)
after_turn = ("=a",)
into_middle = ("=a",)
after_middle = ("bd", "=a")
into_last = ("=bda",)
after_last = ("a", "bc", "d", "cb", *"dabcdacadbcbcdacbd", "A", "cb", "d", "B", "c")


def mesh_bits():
    seq_bits = lax.axis_size("seq").bit_length() - 1
    batch_bits = lax.axis_size("batch").bit_length() - 1
    deep = [1 << place for place in range(batch_bits)]
    core = 1 << batch_bits
    plane = [core << place for place in range(1, seq_bits)]
    return deep, core, plane[: len(plane) // 2], plane[len(plane) // 2 :]


def axis_orders(kind):
    deep, core, across, along = mesh_bits()
    if kind.endswith(" turned"):
        kind = kind[: -len(" turned")]
        across, along = along, across
    near, far = deep[:1], deep[1:]
    orders = {
        "plane": (across + along + deep, along + across + deep),
        "mixed": (across + along + deep, along + deep + across),
        "inner": (across + near + along + far, along + near + across + far),
        "second": (across + along + deep, near + across + along + far),
        "late": (across + along + deep, along + near + across + far),
        "first": (near + across + along + far, near + along + across + far),
        "cross": (across + along + deep, near + along + across + far),
    }
    return core, orders[kind]


def half_bases(kind):
    core, orders = axis_orders(kind)
    index = lax.axis_index("seq") * lax.axis_size("batch") + lax.axis_index("batch")
    side = lax.rem(lax.div(index, core), 2)
    numbers = []
    for order in orders:
        number = 0
        for bit in order[:halvings]:
            number = 2 * number + lax.rem(lax.div(index, bit), 2)
        numbers.append(number)
    keep = (1 - side) * numbers[0] + side * numbers[1]
    send = (1 - side) * numbers[1] + side * numbers[0]
    return side * half_blocks + keep, (1 - side) * half_blocks + send


def swap(array, first, second):
    core = mesh_bits()[1]
    total = lax.axis_size("seq") * lax.axis_size("batch")
    pairs = [(index, index ^ (second if index & core else first)) for index in range(total)]
    return lax.ppermute(array, ("seq", "batch"), pairs)


class UnitSum:
    def __init__(self, keep, send, kind):
        self.core, orders = axis_orders(kind)
        self.steps = list(zip(*orders))
        self.parts = [keep]
        self.top = keep.shape[0]
        self.runs = None
        self.rounds = self.plan(send)
        self.outgoing = next(self.rounds)

    def added(self, low, high):
        total = self.parts[0][low:high]
        for part in self.parts[1:]:
            total = total + part[low:high]
        return total

    def plan(self, send):
        sent = yield send
        self.parts.append(swap(sent, self.core, self.core))
        for step, (first, second) in enumerate(self.steps):
            if step < halvings:
                self.top //= 2
                sent = yield self.added(self.top, 2 * self.top)
                self.parts.append(swap(sent, first, second))
            else:
                own = yield self.added(0, self.top)
                self.parts = [own, swap(own, first, second)]
        full = self.added(0, self.top)
        for first, second in self.steps[halvings - 1 : 0 : -1]:
            full = yield full
            full = jnp.concatenate([full, swap(full, first, second)])
        full = yield full
        rest = swap(full, *self.steps[0])
        other = swap(full, self.core, self.core)
        rest = yield rest
        self.runs = (full, rest, other, swap(rest, self.core, self.core))
        yield None

    def launch(self, sent):
        self.outgoing = self.rounds.send(sent)


class Line:
    def __init__(self):
        self.last = ()

    def advance(self, units, payload=()):
        units = [unit for unit in units if unit.runs is None]
        sends, payload, unused = lax.optimization_barrier(
            ([unit.outgoing for unit in units], payload, self.last)
        )
        for unit, sent in zip(units, sends):
            unit.launch(sent)
        self.last = sends
        return payload

    def settle(self, arrays):
        arrays, self.last = lax.optimization_barrier((arrays, self.last))
        return arrays


def aligned(first, rows):
    return pl.ds(pl.multiple_of(first, 8), rows)


class Layout:
    def __init__(self, rows, columns, kind):
        self.rows, self.columns, self.kind = rows, columns, kind
        self.sections = {}

    def add(self, key, array_rows, array_first, block_first, count, columns=slice(None)):
        self.sections.setdefault(key, []).append(
            (
                lambda owner: (aligned(owner * array_rows + array_first, count), slice(None)),
                lambda place: (aligned(place * self.rows + block_first, count), columns),
            )
        )

    def half(self):
        return ((half_blocks * self.rows, self.columns), f32)


def unit_layout(keys, kind, model, width):
    total = 2 * half_blocks
    out_rows, rows, wide = 4 * width // total, model // total, 2 * width
    if keys == ("out",):
        layout = Layout(out_rows, model, kind)
        layout.add("out", out_rows, 0, 0, out_rows)
    elif keys == ("glu",):
        layout = Layout(rows, model, kind)
        layout.add("glu", rows, 0, 0, rows)
    elif keys == ("out", "glu"):
        layout = Layout(out_rows + rows, model, kind)
        layout.add("out", out_rows, 0, 0, out_rows)
        layout.add("glu", rows, 0, out_rows, rows)
    elif keys == ("in",):
        layout = Layout(rows, wide, kind)
        layout.add("in", rows, 0, 0, rows)
    elif keys[1:] == ("in",):
        layout = Layout(rows, model + wide, kind)
        layout.add(keys[0], rows, 0, 0, rows, slice(0, model))
        layout.add("in", rows, 0, 0, rows, slice(model, model + wide))
    else:
        pieces = rows // 8
        layout = Layout(8, pieces * wide + lane_count, kind)
        for piece in range(pieces):
            layout.add("in", rows, 8 * piece, 0, 8, slice(piece * wide, (piece + 1) * wide))
        layout.add("small", 8, 0, 0, 8, slice(pieces * wide, pieces * wide + lane_count))
    return layout


class Emit:
    def __init__(self, units, refs, model, width):
        self.homes = {}
        for index, (unused, keys, kind) in enumerate(units):
            layout = unit_layout(keys, kind, model, width)
            for key in keys:
                self.homes[key] = (layout, refs[2 * index : 2 * index + 2], half_bases(kind))

    def put(self, key, array_ref):
        if key not in self.homes:
            return
        layout, halves, bases = self.homes[key]

        def one(place, carry):
            for half in (1, 0):
                owner = lax.bitwise_xor(bases[half], place)
                for array_at, block_at in layout.sections[key]:
                    halves[half][block_at(place)] = array_ref[array_at(owner)]
            return carry

        lax.fori_loop(0, half_blocks, one, 0)


run_places = ((0, 0), (0, half_blocks // 2), (1, 0), (1, half_blocks // 2))


def start_places(layout, goals, runs, outs, semaphores):
    bases = half_bases(layout.kind)
    for index, (half, first) in enumerate(run_places):

        def one(place, carry, run=runs[index], half=half, first=first, index=index):
            owner = lax.bitwise_xor(bases[half], first + place)
            for key, which, layer in goals:
                for array_at, block_at in layout.sections[key]:
                    pltpu.make_async_copy(
                        run.at[block_at(place)],
                        outs[which].at[layer].at[array_at(owner)],
                        semaphores.at[index],
                    ).start()
            return carry

        lax.fori_loop(0, half_blocks // 2, one, 0)


def place_kernel(layout, goals, out_count, *refs):
    runs, semaphores = refs[: len(run_places)], refs[-1]
    start_places(layout, goals, runs, refs[len(refs) - 1 - out_count : -1], semaphores)
    for index, run in enumerate(runs):
        pltpu.make_async_copy(run, run, semaphores.at[index]).wait()


def finish_kernel(layout, goals, fixed, *refs):
    runs = refs[: len(run_places)]
    slopes_ref, unused, out_ref, gain_ref, skip_ref, decay_ref, frequency_ref, step_ref = refs[4:12]
    small_ref, semaphores = refs[12:]
    start_places(layout, goals, runs, (out_ref,), semaphores)
    bases = half_bases(layout.kind)
    for run, (half, first) in zip(runs, run_places):
        for place in range(half_blocks // 2):
            owner = lax.bitwise_xor(bases[half], first + place)
            for array_at, block_at in layout.sections["small"]:
                small_ref[array_at(owner)] = run[block_at(place)]
    row = 0
    for ref in (gain_ref, skip_ref):
        for layer in range(ref.shape[0]):
            for column in range(0, ref.shape[1], lane_count):
                ref[layer : layer + 1, column : column + lane_count] = small_ref[row : row + 1, :]
                row += 1
    layer_count, width = decay_ref.shape
    steps = width // lane_count
    for layer in range(layer_count):
        for piece in range(steps):
            columns = slice(piece * lane_count, (piece + 1) * lane_count)
            for index, ref in enumerate((decay_ref, frequency_ref, step_ref)):
                total = None
                for member in range(4):
                    line = row + member * steps + piece
                    slope = slopes_ref[
                        (4 * index + member) * layer_count + layer : (4 * index + member) * layer_count
                        + layer + 1,
                        columns,
                    ]
                    term = slope * small_ref[line : line + 1, :]
                    total = term if total is None else total + term
                ref[layer : layer + 1, columns] = total
        row += 4 * steps
    for index, run in enumerate(runs):
        moved = run.at[:, fixed]
        pltpu.make_async_copy(moved, moved, semaphores.at[index]).wait()


def place_unit(runs, layout, goals, shapes, sums):
    arrays = sorted({array for unused, array, unused_too in goals})
    operands = [("run", run) for run in runs]
    aliases = {}
    for index, array in enumerate(arrays):
        if array in sums:
            aliases[len(operands)] = index
            operands.append(("before", (sums[array], None)))
    outs = call(
        functools.partial(
            place_kernel, layout, [(key, arrays.index(array), layer) for key, array, layer in goals],
            len(arrays),
        ),
        "place_" + "_".join(arrays),
        operands,
        tuple((shapes[array], f32) for array in arrays),
        (pltpu.SemaphoreType.DMA((len(run_places),)),),
        written=range(len(arrays)),
        aliases=aliases,
        plain=True,
    )
    sums.update(zip(arrays, outs))


def finish_unit(runs, layout, slopes, shape, before, vectors, small_out):
    return call(
        functools.partial(
            finish_kernel, layout, [("in", 0, 0)], slice(0, layout.columns - lane_count)
        ),
        "place_last",
        [("run", run) for run in runs] + [("slopes", slopes), ("before", (before, None))],
        ((shape, f32),) + tuple((each, f32) for each in vectors),
        (small_out, pltpu.SemaphoreType.DMA((len(run_places),))),
        written=(0,),
        final=range(1, 1 + len(vectors)),
        aliases={len(runs) + 1: 0},
        plain=True,
    )


class Fetch:
    def __init__(self, stack_ref, layer, target, semaphore):
        self.copy = pltpu.make_async_copy(stack_ref.at[layer], target, semaphore)
        self.target = target
        self.waiting = True
        self.copy.start()

    def ready(self):
        if self.waiting:
            self.copy.wait()
            self.waiting = False
        return self.target


def call(body, name, operands, outs, scratch, written=(), aliases=None, plain=False, micros=4, final=()):
    scalars = {"place", "docs"}
    arrays = []
    specs = []
    layers = {}
    pieces = None
    flat = []
    for key, operand in operands:
        if isinstance(operand, list):
            pieces = (len(flat), len(operand))
            flat.extend((key, piece) for piece in operand)
        else:
            flat.append((key, operand))
    for position, (key, operand) in enumerate(flat):
        space = pltpu.SMEM if key in scalars else pltpu.VMEM
        if isinstance(operand, tuple):
            operand, layer = operand
            space = pl.ANY
            if layer is not None:
                layers[position] = layer
                operand = pltpu.with_memory_space_constraint(operand, pltpu.HBM)
        specs.append(pl.BlockSpec(memory_space=space))
        arrays.append(operand)
    fetched = [
        pltpu.VMEM(arrays[position].shape[1:], arrays[position].dtype) for position in layers
    ]

    gathered = []
    if pieces is not None:
        first, count = pieces
        rows, columns = arrays[first].shape
        gathered = [pltpu.VMEM((count * rows, columns), arrays[first].dtype)]

    def kernel(*refs):
        if plain:
            body(*refs)
            return
        given = list(refs[: len(arrays)])
        rest = refs[len(arrays) : len(refs) - len(fetched) - 1]
        targets = refs[len(refs) - len(fetched) - 1 : -1]
        for index, (position, layer) in enumerate(layers.items()):
            given[position] = Fetch(given[position], layer, targets[index], refs[-1].at[index])
        if pieces is not None:
            first, count = pieces
            rows = given[first].shape[0]
            whole, rest = rest[-1], rest[:-1]
            for offset in range(count):
                source = lax.bitwise_xor(given[0][0], offset)
                whole[aligned(source * rows, rows), :] = given[first + offset][...]
            given[first : first + count] = [whole]
        body(*given, *rest)

    return pl.pallas_call(
        kernel,
        name=name,
        in_specs=specs,
        out_specs=[
            pl.BlockSpec(memory_space=pl.ANY if place in written else pltpu.VMEM)
            for place in range(len(outs))
        ],
        out_shape=[
            jax.ShapeDtypeStruct(shape, kind)
            if place in written or place in final
            else pltpu.VMEM(shape, kind)
            for place, (shape, kind) in enumerate(outs)
        ],
        scratch_shapes=[
            entry if not isinstance(entry, tuple) else pltpu.VMEM(*entry) for entry in scratch
        ]
        + gathered
        + fetched
        + ([] if plain else [pltpu.SemaphoreType.DMA((max(1, len(fetched)),))]),
        input_output_aliases=aliases or {},
        cost_estimate=pl.CostEstimate(
            flops=micros * 1_000_000_000, bytes_accessed=micros * 3_600_000, transcendentals=0
        ),
        compiler_params=pltpu.CompilerParams(vmem_limit_bytes=vmem_bytes),
    )(*arrays)


def on_device(
    inputs,
    doc_lengths,
    norm_gain,
    decay_log,
    frequency,
    step_log,
    in_weight,
    skip_weight,
    out_weight,
    glu_weight,
    cotangent,
):
    row_count, length, model = inputs.shape
    layer_count, width = decay_log.shape
    count = row_count * length
    device_count = lax.axis_size("seq")
    place = lax.axis_index("seq").astype(jnp.int32).reshape(1)
    rate_tables, rates_back = jax.vjp(rates, decay_log, frequency, step_log)
    tables = jnp.stack(rate_tables, axis=1).reshape(4 * layer_count, width)
    none = jnp.zeros((layer_count, width), f32)
    by_rate = [
        rates_back(tuple(none + 1.0 if member == rate else none for member in range(4)))
        for rate in range(4)
    ]
    slopes = jnp.concatenate(
        [by_rate[rate][parameter] for parameter in range(3) for rate in range(4)], axis=0
    )

    def gather(totals):
        if device_count != 8:
            return lax.all_gather(totals, "seq", axis=0, tiled=True)

        def from_other(array, bits):
            return lax.ppermute(
                array, "seq", [(index, index ^ bits) for index in range(device_count)]
            )

        pieces = [None] * device_count
        pieces[0] = totals
        for bits in range(2, device_count, 2):
            pieces[bits] = from_other(totals, bits)
        for bits in range(0, device_count, 2):
            pieces[bits + 1] = from_other(pieces[bits], 1)
        return pieces

    flags_out = ((3, count, lane_count), f32)
    blocks_out = ((2, device_count * row_count, lane_count), f32)
    wide_out = ((count, 4 * width), f32)
    ends_out = ((chunk_count, 4 * width), f32)
    totals_out = ((4 * row_count, width), f32)
    tokens = ((count, model), f32)
    tokens_low = ((count, model), bf16)
    drive_out = ((count, 2 * width), f32)
    bar_out = ((model, 2 * width), bf16)
    glu_out = ((model, model), f32)
    out_out = ((4 * width, model), f32)
    in_out = ((model, 2 * width), f32)
    vector = ((1, model), f32)

    def in_place(array):
        return pltpu.with_memory_space_constraint(array, pltpu.HBM)

    flags, blocks, values, scaled, drive, ends, totals = call(
        functools.partial(first_kernel, length),
        "first",
        (
            ("place", place),
            ("docs", in_place(doc_lengths)),
            ("inputs", in_place(inputs)),
            ("gain", in_place(norm_gain)),
            ("tables", tables),
            ("in", (in_weight, 0)),
        ),
        (flags_out, blocks_out, tokens_low, tokens_low, drive_out, ends_out, totals_out),
        (bar_out,),
    )
    shared = (("flags", flags), ("blocks", blocks), ("tables", tables))
    kept = []
    for layer in range(layer_count - 1):
        gathered = gather(totals)
        (
            states, low, enter, mixed, act, gate, next_values, next_scaled, drive, ends, totals,
        ) = call(
            functools.partial(middle_kernel, layer, length),
            "middle",
            (
                ("place", place),
                ("gathered", gathered),
                *shared,
                ("gain", norm_gain),
                ("skip", skip_weight),
                ("drive", drive),
                ("ends", ends),
                ("values", values),
                ("scaled", scaled),
                ("out", (out_weight, layer)),
                ("glu", (glu_weight, layer)),
                ("in", (in_weight, layer + 1)),
            ),
            (
                wide_out, ((count, 4 * width), bf16), ends_out, tokens, tokens_low, tokens,
                tokens, tokens_low, drive_out, ends_out, totals_out,
            ),
            (bar_out,),
        )
        kept.append((states, low, enter, mixed, act, gate, values, scaled))
        values, scaled = next_values, next_scaled
    layer = layer_count - 1
    gathered = gather(totals)
    small_out = ((8 * 2 * half_blocks, lane_count), f32)
    shapes = {
        "out": (layer_count, 4 * width, model),
        "glu": (layer_count, model, model),
        "in": (layer_count, model, 2 * width),
        "small": small_out[0],
    }
    sums = {}
    line = Line()
    layouts, goals, units = {}, {}, {}

    def unit_outs(entries):
        outs = []
        for name, keys, kind in entries:
            layouts[name] = unit_layout(keys, kind, model, width)
            outs.extend([((half_blocks * layouts[name].rows, layouts[name].columns), f32)] * 2)
        return tuple(outs)

    def open_units(entries, halves, layer_of):
        for index, (name, keys, kind) in enumerate(entries):
            units[name] = UnitSum(halves[2 * index], halves[2 * index + 1], kind)
            goals[name] = [(key, "glu" if key == "over" else key, layer_of[key]) for key in keys]

    placed = set()

    def place_sums(name):
        placed.add(name)
        runs = line.settle(units[name].runs)
        place_unit(runs, layouts[name], goals[name], shapes, sums)
        line.last = [sums[array] for unused, array, unused_too in goals[name]]

    def follow(plan, payload=()):
        for group in plan:
            if group.isupper():
                for name in group.lower():
                    if units[name].runs is not None and name not in placed:
                        place_sums(name)
            elif group[0] == "=":
                payload = line.advance([units[name] for name in group[1:]], payload)
            else:
                line.advance([units[name] for name in group])
        return payload

    results = call(
        functools.partial(turn_kernel, layer, length),
        "turn",
        (
            ("place", place),
            ("gathered", gathered),
            *shared,
            ("skip", skip_weight),
            ("drive", drive),
            ("ends", ends),
            ("values", values),
            ("scaled", scaled),
            ("out", (out_weight, layer)),
            ("glu", (glu_weight, layer)),
            ("cotangent", cotangent),
        ),
        (
            *unit_outs(turn_units), (inputs.shape, bf16), tokens, wide_out, ends_out, tokens, wide_out,
            vector, ends_out, totals_out, glu_out,
        ),
        (
            ((count, 4 * width), bf16), tokens, tokens_low, tokens, tokens_low, tokens_low, tokens,
            tokens_low, out_out,
        ),
        final=(2 * len(turn_units),),
        micros=6,
    )
    halves, results = results[: 2 * len(turn_units)], results[2 * len(turn_units) :]
    output, grad, states, enter, d_mixed, d_states, skip_grad, ends, totals, over_grad = results
    open_units(turn_units, halves, {"out": layer, "glu": layer})
    gathered = follow(into_middle, gather(follow(after_turn, totals)))
    back_scratch = (
        drive_out, drive_out, ((count, 2 * width), bf16), bar_out, tokens,
    )
    rate_out = ((4, width), f32)
    low_states, low, low_enter, mixed, act, gate, low_values, low_scaled = kept[0]
    results = call(
        functools.partial(back_middle_kernel, layer, length),
        "back_middle",
        (
            ("place", place),
            ("gathered", gathered),
            *shared,
            ("gain", norm_gain),
            ("skip", skip_weight),
            ("in", (in_weight, layer)),
            ("d_states", d_states),
            ("ends", ends),
            ("states", states),
            ("enter", enter),
            ("scaled", scaled),
            ("values", values),
            ("d_mixed", d_mixed),
            ("grad", grad),
            ("out", (out_weight, layer - 1)),
            ("glu", (glu_weight, layer - 1)),
            ("mixed", mixed),
            ("act", act),
            ("gate", gate),
            ("below_scaled", low_scaled),
            ("low", low),
            ("over", over_grad),
        ),
        (
            *unit_outs(middle_units), vector, rate_out, tokens, tokens, wide_out, vector, ends_out,
            totals_out,
        ),
        back_scratch + (tokens_low, tokens_low, in_out, glu_out, out_out),
        micros=6,
    )
    halves, results = results[: 2 * len(middle_units)], results[2 * len(middle_units) :]
    gain_grad, rate_grad, grad, d_mixed, d_states, low_skip_grad, ends, totals = results
    open_units(middle_units, halves, {"out": layer - 1, "glu": layer - 1, "over": layer, "in": layer})
    gathered = follow(into_last, gather(follow(after_middle, totals)))
    keep, send, input_grad = call(
        functools.partial(back_last_kernel, length),
        "back_last",
        (
            ("place", place),
            ("gathered", gathered),
            *shared,
            ("gain", norm_gain),
            ("skip", skip_weight),
            ("in", (in_weight, 0)),
            ("d_states", d_states),
            ("ends", ends),
            ("states", low_states),
            ("enter", low_enter),
            ("scaled", low_scaled),
            ("values", low_values),
            ("d_mixed", d_mixed),
            ("grad", grad),
            ("skip_grad", low_skip_grad),
            ("skip_grad", skip_grad),
            ("gain_grad", gain_grad),
            ("rate_grad", rate_grad),
        ),
        (*unit_outs(last_units), (inputs.shape, bf16)),
        back_scratch + (tokens_low, in_out, vector, rate_out, small_out),
        final=(2,),
        micros=4,
    )
    open_units(last_units, (keep, send), {"in": 0, "small": None})
    follow(after_last)
    for name, unit in units.items():
        while unit.runs is None:
            follow(name)
    for name in units:
        if name not in placed and name != last_units[0][0]:
            place_sums(name)
    name = last_units[0][0]
    in_sum, gain_sum, skip_sum, decay_grad, frequency_grad, step_grad = finish_unit(
        line.settle(units[name].runs), layouts[name], slopes, shapes["in"], sums["in"],
        ((layer_count, model),) * 2 + ((layer_count, width),) * 3, small_out,
    )
    return (
        output,
        input_grad,
        gain_sum,
        decay_grad,
        frequency_grad,
        step_grad,
        in_sum,
        skip_sum,
        sums["out"],
        sums["glu"],
    )


def solution(mesh):
    in_specs = (
        P("batch", "seq", None),
        P("batch", None),
        P(),
        P(),
        P(),
        P(),
        P(),
        P(),
        P(),
        P(),
        P("batch", "seq", None),
    )
    out_specs = (
        P("batch", "seq", None),
        P("batch", "seq", None),
        P(),
        P(),
        P(),
        P(),
        P(),
        P(),
        P(),
        P(),
    )
    return jax.shard_map(
        on_device, mesh=mesh, in_specs=in_specs, out_specs=out_specs, check_vma=False
    )
```

```python
import functools
import math

import jax
import jax.numpy as jnp
from jax import lax
from jax.experimental import pallas as pl
from jax.experimental.pallas import tpu as pltpu
from jax.sharding import PartitionSpec as P

epsilon = 1e-05
chunk_count = 8
lane_count = 128
block_rows = 64
vmem_bytes = 32 * 1024 * 1024
gelu_scale = math.sqrt(2.0 / math.pi)
gelu_cubic = 0.044715
f32 = jnp.float32
bf16 = jnp.bfloat16


def complex_mul(left_real, left_imag, right_real, right_imag):
    return (
        left_real * right_real - left_imag * right_imag,
        left_real * right_imag + left_imag * right_real,
    )


def complex_power(real, imag, exponent):
    result = None
    while exponent:
        if exponent & 1:
            result = (real, imag) if result is None else complex_mul(*result, real, imag)
        exponent >>= 1
        if exponent:
            real, imag = complex_mul(real, imag, real, imag)
    return result


def rates(decay_log, frequency, step_log):
    step_size = jnp.exp(step_log)
    pole_real = -jnp.exp(decay_log)
    shrink = step_size * pole_real
    rotation = step_size * frequency
    radius = jnp.exp(shrink)
    decay_real = radius * jnp.cos(rotation)
    decay_imag = radius * jnp.sin(rotation)
    minus_real = jnp.expm1(shrink) * jnp.cos(rotation) - 2.0 * jnp.sin(0.5 * rotation) ** 2
    modulus = pole_real * pole_real + frequency * frequency
    factor_real = (minus_real * pole_real + decay_imag * frequency) / modulus
    factor_imag = (decay_imag * pole_real - minus_real * frequency) / modulus
    return (decay_real, decay_imag, factor_real, factor_imag)


def dot(left, right):
    return lax.dot_general(left, right, (((1,), (0,)), ((), ())), preferred_element_type=f32)


def dot_right(left, right):
    return lax.dot_general(left, right, (((1,), (1,)), ((), ())), preferred_element_type=f32)


def dot_left(left, right):
    return lax.dot_general(left, right, (((0,), (0,)), ((), ())), preferred_element_type=f32)


def spread(narrow, width):
    return jnp.concatenate([narrow] * (width // lane_count), axis=1)


def order_matrix(count, inverse):
    rows = lax.broadcasted_iota(jnp.int32, (count, count), 0)
    cols = lax.broadcasted_iota(jnp.int32, (count, count), 1)
    if inverse:
        rows, cols = cols, rows
    source = lax.rem(rows, chunk_count) * (count // chunk_count) + lax.div(rows, chunk_count)
    return jnp.where(cols == source, 1.0, 0.0).astype(bf16)


def over_blocks(count, body):
    def one(index, carry):
        body(pl.ds(pl.multiple_of(index * block_rows, block_rows), block_rows))
        return carry

    lax.fori_loop(0, count // block_rows, one, 0, unroll=min(8, count // block_rows))


def normalize(values):
    average = jnp.mean(values, axis=-1, keepdims=True)
    centered = values - average
    inverse = lax.rsqrt(jnp.mean(centered * centered, axis=-1, keepdims=True) + epsilon)
    return centered * inverse, inverse


def gelu_parts(mixed):
    square = mixed * mixed
    bend = jnp.tanh(gelu_scale * mixed * (1.0 + gelu_cubic * square))
    half = 0.5 + 0.5 * bend
    slope = half + 0.5 * mixed * (1.0 - bend * bend) * gelu_scale * (
        1.0 + 3.0 * gelu_cubic * square
    )
    return mixed * half, slope


def write_flags(place, docs_ref, flags_ref, blocks_ref, length):
    row_count, doc_count = docs_ref.shape
    span = row_count * length // chunk_count
    per_row = chunk_count // row_count
    offsets = []
    for row in range(row_count):
        running = [jnp.int32(0)]
        for doc in range(doc_count):
            running.append(running[-1] + docs_ref[row, doc])
        offsets.append(running)

    def by_row(row_of, member):
        chosen = jnp.full(row_of.shape, offsets[0][member], jnp.int32)
        for row in range(1, row_count):
            chosen = jnp.where(row_of == row, offsets[row][member], chosen)
        return chosen

    chunk = lax.broadcasted_iota(jnp.int32, (chunk_count, lane_count), 0)
    row_of = lax.div(chunk, per_row)
    bounds = [by_row(row_of, member) for member in range(doc_count + 1)]
    base = place * length + lax.rem(chunk, per_row) * span
    for step in range(span):
        position = base + step
        starts = position == bounds[0]
        endings = position + 1 == bounds[0]
        for bound in bounds[1:]:
            starts = starts | (position == bound)
            endings = endings | (position + 1 == bound)
        window = pl.ds(chunk_count * step, chunk_count)
        flags_ref[0, window, :] = jnp.where(starts, 0.0, 1.0)
        flags_ref[1, window, :] = jnp.where(endings, 0.0, 1.0)
        flags_ref[2, window, :] = jnp.where(position < bounds[-1], 1.0, 0.0)
    entry = lax.broadcasted_iota(jnp.int32, blocks_ref.shape[1:], 0)
    row_of = lax.rem(entry, row_count)
    first = lax.div(entry, row_count) * length
    starts = jnp.zeros(entry.shape, jnp.bool_)
    endings = starts
    for member in range(doc_count + 1):
        bound = by_row(row_of, member)
        starts = starts | ((bound >= first) & (bound < first + length))
        endings = endings | ((bound > first) & (bound <= first + length))
    blocks_ref[0] = jnp.where(starts, 0.0, 1.0)
    blocks_ref[1] = jnp.where(endings, 0.0, 1.0)


def chunk_keeps(flags_ref):
    span = flags_ref.shape[1] // chunk_count
    ahead = flags_ref[0, :chunk_count, :]
    behind = flags_ref[1, :chunk_count, :]
    for step in range(1, span):
        window = pl.ds(chunk_count * step, chunk_count)
        ahead = ahead * flags_ref[0, window, :]
        behind = behind * flags_ref[1, window, :]
    return ahead, behind


def toward(array, distance, reverse):
    return pltpu.roll(array, chunk_count - distance if reverse else distance, axis=0)


def chunk_prefix(ends, factor, entering, per_row, reverse):
    width = ends[0].shape[1]
    chunk = lax.broadcasted_iota(jnp.int32, (chunk_count, width), 0)
    within = lax.rem(chunk, per_row)
    within = per_row - 1 - within if reverse else within
    first = within == 0
    total_real, total_imag = ends
    if entering is not None:
        moved_real, moved_imag = complex_mul(*factor, *entering)
        total_real = total_real + jnp.where(first, moved_real, 0.0)
        total_imag = total_imag + jnp.where(first, moved_imag, 0.0)
    distance = 1
    while distance < per_row:
        reach = within >= distance
        near_real = toward(total_real, distance, reverse)
        near_imag = toward(total_imag, distance, reverse)
        moved_real, moved_imag = complex_mul(*factor, near_real, near_imag)
        total_real = total_real + jnp.where(reach, moved_real, 0.0)
        total_imag = total_imag + jnp.where(reach, moved_imag, 0.0)
        if 2 * distance < per_row:
            far_real = toward(factor[0], distance, reverse)
            far_imag = toward(factor[1], distance, reverse)
            both_real, both_imag = complex_mul(*factor, far_real, far_imag)
            factor = (
                jnp.where(reach, both_real, factor[0]),
                jnp.where(reach, both_imag, factor[1]),
            )
        distance *= 2
    enter_real = toward(total_real, 1, reverse)
    enter_imag = toward(total_imag, 1, reverse)
    none = (jnp.zeros_like(total_real),) * 2 if entering is None else entering
    return (
        (total_real, total_imag),
        (jnp.where(first, none[0], enter_real), jnp.where(first, none[1], enter_imag)),
    )


def sweep(flags_ref, pole_real, pole_imag, forward_at, reverse_at, start, put_forward, put_reverse):
    width = pole_real.shape[1]
    span = flags_ref.shape[1] // chunk_count

    def one(step, state):
        ahead_real, ahead_imag, behind_real, behind_imag = state
        here = pl.ds(pl.multiple_of(chunk_count * step, chunk_count), chunk_count)
        there = pl.ds(pl.multiple_of(chunk_count * (span - 1 - step), chunk_count), chunk_count)
        keep = spread(flags_ref[0, here, :], width)
        moved_real, moved_imag = complex_mul(pole_real * keep, pole_imag * keep, ahead_real, ahead_imag)
        drive_real, drive_imag = forward_at(here)
        ahead_real = moved_real + drive_real
        ahead_imag = moved_imag + drive_imag
        keep = spread(flags_ref[1, there, :], width)
        moved_real, moved_imag = complex_mul(
            pole_real * keep, pole_imag * keep, behind_real, behind_imag
        )
        drive_real, drive_imag = reverse_at(there)
        behind_real = moved_real + drive_real
        behind_imag = moved_imag + drive_imag
        if put_forward is not None:
            put_forward(here, ahead_real, ahead_imag)
            put_reverse(there, behind_real, behind_imag)
        return (ahead_real, ahead_imag, behind_real, behind_imag)

    return lax.fori_loop(0, span, one, start, unroll=4)


def local_totals(flags_ref, pole_real, pole_imag, forward_at, reverse_at, ends_ref, totals_ref):
    width = pole_real.shape[1]
    span = flags_ref.shape[1] // chunk_count
    row_count = totals_ref.shape[0] // 4
    per_row = chunk_count // row_count
    pole_real = jnp.broadcast_to(pole_real, (chunk_count, width))
    pole_imag = jnp.broadcast_to(pole_imag, (chunk_count, width))
    zero = jnp.zeros((chunk_count, width), f32)
    ends = sweep(
        flags_ref, pole_real, pole_imag, forward_at, reverse_at, (zero,) * 4, None, None
    )
    for member in range(4):
        ends_ref[:, member * width : (member + 1) * width] = ends[member]
    power_real, power_imag = complex_power(pole_real, pole_imag, span)
    for direction, keep in enumerate(chunk_keeps(flags_ref)):
        keep = spread(keep, width)
        pair = ends[2 * direction : 2 * direction + 2]
        totals, unused = chunk_prefix(
            pair, (power_real * keep, power_imag * keep), None, per_row, direction == 1
        )
        for part in range(2):
            for row in range(row_count):
                chunk = row * per_row if direction == 1 else (row + 1) * per_row - 1
                entry = (2 * direction + part) * row_count + row
                totals_ref[entry : entry + 1, :] = totals[part][chunk : chunk + 1, :]


def chunk_entrances(place, gathered_ref, flags_ref, blocks_ref, ends_ref, pole_real, pole_imag, length):
    width = pole_real.shape[1]
    span = flags_ref.shape[1] // chunk_count
    row_count = chunk_count * span // length
    per_row = chunk_count // row_count
    device_count = gathered_ref.shape[0] // (4 * row_count)
    pole_real = jnp.broadcast_to(pole_real, (chunk_count, width))
    pole_imag = jnp.broadcast_to(pole_imag, (chunk_count, width))
    power_real, power_imag = complex_power(pole_real, pole_imag, span)
    device_real, device_imag = complex_power(power_real, power_imag, per_row)
    device_real = device_real[:row_count]
    device_imag = device_imag[:row_count]
    entrances = []
    for direction, keep in enumerate(chunk_keeps(flags_ref)):
        real = jnp.zeros((row_count, width), f32)
        imag = real
        for lap in range(device_count):
            source = device_count - 1 - lap if direction == 1 else lap
            live = source > place if direction == 1 else source < place
            open_ = spread(
                blocks_ref[direction, source * row_count : (source + 1) * row_count, :], width
            )
            moved_real, moved_imag = complex_mul(device_real * open_, device_imag * open_, real, imag)
            first = (4 * source + 2 * direction) * row_count
            moved_real = moved_real + gathered_ref[first : first + row_count, :]
            moved_imag = moved_imag + gathered_ref[first + row_count : first + 2 * row_count, :]
            real = jnp.where(live, moved_real, real)
            imag = jnp.where(live, moved_imag, imag)
        entering = tuple(
            jnp.concatenate(
                [
                    jnp.broadcast_to(part[row : row + 1, :], (per_row, width))
                    for row in range(row_count)
                ],
                axis=0,
            )
            for part in (real, imag)
        )
        keep = spread(keep, width)
        first = 2 * direction * width
        ends = (ends_ref[:, first : first + width], ends_ref[:, first + width : first + 2 * width])
        unused, entrance = chunk_prefix(
            ends, (power_real * keep, power_imag * keep), entering, per_row, direction == 1
        )
        entrances.extend(entrance)
    return tuple(entrances)


def layer_poles(tables_ref, layer):
    return tables_ref[4 * layer : 4 * layer + 1, :], tables_ref[4 * layer + 1 : 4 * layer + 2, :]


def layer_factors(tables_ref, layer):
    return tables_ref[4 * layer + 2 : 4 * layer + 3, :], tables_ref[4 * layer + 3 : 4 * layer + 4, :]


def write_bar(tables_ref, layer, in_ref, bar_ref):
    width = tables_ref.shape[1]
    factor_real, factor_imag = layer_factors(tables_ref, layer)

    def body(rows):
        weight_real = in_ref[rows, :width].astype(f32)
        weight_imag = in_ref[rows, width:].astype(f32)
        real, imag = complex_mul(factor_real, factor_imag, weight_real, weight_imag)
        bar_ref[rows, :width] = real.astype(bf16)
        bar_ref[rows, width:] = imag.astype(bf16)

    over_blocks(in_ref.shape[0], body)


def pair_at(ref, first, width):
    def at(rows):
        return ref[rows, first : first + width], ref[rows, first + width : first + 2 * width]

    return at


def drive_totals(flags_ref, tables_ref, layer, scaled_ref, in_ref, bar_ref, drive_ref, ends_ref, totals_ref):
    width = tables_ref.shape[1]
    write_bar(tables_ref, layer, in_ref.ready(), bar_ref)
    drive_ref[...] = dot(scaled_ref[...], bar_ref[...])
    at = pair_at(drive_ref, 0, width)
    local_totals(flags_ref, *layer_poles(tables_ref, layer), at, at, ends_ref, totals_ref)


def settled_states(
    place, gathered_ref, flags_ref, blocks_ref, tables_ref, layer, drive_ref, ends_ref, length,
    states_ref, low_ref, enter_ref,
):
    width = tables_ref.shape[1]
    pole_real, pole_imag = layer_poles(tables_ref, layer)
    entrances = chunk_entrances(
        place, gathered_ref, flags_ref, blocks_ref, ends_ref, pole_real, pole_imag, length
    )
    for member in range(4):
        enter_ref[:, member * width : (member + 1) * width] = entrances[member]

    def put_forward(rows, real, imag):
        states_ref[rows, :width] = real
        states_ref[rows, width : 2 * width] = imag

    def put_reverse(rows, real, imag):
        states_ref[rows, 2 * width : 3 * width] = real
        states_ref[rows, 3 * width :] = imag

    at = pair_at(drive_ref, 0, width)
    sweep(
        flags_ref,
        jnp.broadcast_to(pole_real, (chunk_count, width)),
        jnp.broadcast_to(pole_imag, (chunk_count, width)),
        at, at, entrances, put_forward, put_reverse,
    )

    def body(rows):
        low_ref[rows, :] = states_ref[rows, :].astype(bf16)

    over_blocks(states_ref.shape[0], body)


def mix_and_gate(layer, low_ref, scaled_ref, out_ref, glu_ref, skip_ref, mixed_ref, act_ref, gate_ref):
    mixed_ref[...] = dot(low_ref[...], out_ref.ready()[...])
    skip = skip_ref[layer : layer + 1, :]

    def body(rows):
        mixed = mixed_ref[rows, :] + skip * scaled_ref[rows, :].astype(f32)
        mixed_ref[rows, :] = mixed
        act_ref[rows, :] = gelu_parts(mixed)[0].astype(bf16)

    over_blocks(mixed_ref.shape[0], body)
    gate_ref[...] = dot(act_ref[...], glu_ref.ready()[...])


def back_tail(
    layer, flags_ref, tables_ref, grad_ref, mixed_ref, act_ref, gate_ref, scaled_ref, low_ref,
    out_ref, glu_ref, skip_ref, logits_ref, work_ref, mixed_low_ref,
    d_mixed_ref, d_states_ref, glu_grad_ref, out_grad_ref, skip_grad_ref, ends_ref, totals_ref, emit,
):
    width = tables_ref.shape[1]
    model = mixed_ref.shape[1]

    def first(rows):
        valid = spread(flags_ref[2, rows, :], model)
        gate = gate_ref[rows, :]
        rate = grad_ref[rows, :] * valid * gate
        logits_ref[rows, :] = (rate * act_ref[rows, :].astype(f32) * (1.0 - gate)).astype(bf16)

    over_blocks(mixed_ref.shape[0], first)
    glu_grad_ref[...] = dot_left(act_ref[...], logits_ref[...])
    emit.put("glu", glu_grad_ref)
    work_ref[...] = dot_right(logits_ref[...], glu_ref.ready()[...])
    skip_grad_ref[...] = jnp.zeros(skip_grad_ref.shape, f32)

    def second(rows):
        valid = spread(flags_ref[2, rows, :], model)
        d_act = grad_ref[rows, :] * valid * gate_ref[rows, :] + work_ref[rows, :]
        d_mixed = d_act * gelu_parts(mixed_ref[rows, :])[1]
        d_mixed_ref[rows, :] = d_mixed
        mixed_low_ref[rows, :] = d_mixed.astype(bf16)
        skip_grad_ref[...] += jnp.sum(
            d_mixed * scaled_ref[rows, :].astype(f32), axis=0, keepdims=True
        )

    over_blocks(mixed_ref.shape[0], second)
    out_grad_ref[...] = dot_left(low_ref[...], mixed_low_ref[...])
    emit.put("out", out_grad_ref)
    d_states_ref[...] = dot_right(mixed_low_ref[...], out_ref.ready()[...])
    pole_real, pole_imag = layer_poles(tables_ref, layer)
    local_totals(
        flags_ref, pole_real, -pole_imag, pair_at(d_states_ref, 2 * width, width),
        pair_at(d_states_ref, 0, width), ends_ref, totals_ref,
    )


def back_front(
    place, layer, length, gathered_ref, flags_ref, blocks_ref, tables_ref, gain_ref, skip_ref, in_ref,
    d_states_ref, ends_ref, states_ref, enter_ref, scaled_ref, values_ref, d_mixed_ref, grad_ref,
    lam_ref, mu_ref, low_ref, bar_ref, work_ref,
    in_grad_ref, gain_grad_ref, rate_grad_ref, put_gradient, emit,
):
    width = tables_ref.shape[1]
    model = values_ref.shape[1]
    count = values_ref.shape[0]
    pole_real, pole_imag = layer_poles(tables_ref, layer)
    entrances = chunk_entrances(
        place, gathered_ref, flags_ref, blocks_ref, ends_ref, pole_real, -pole_imag, length
    )

    def put_forward(rows, real, imag):
        mu_ref[rows, :width] = real
        mu_ref[rows, width:] = imag

    def put_reverse(rows, real, imag):
        lam_ref[rows, :width] = real
        lam_ref[rows, width:] = imag

    sweep(
        flags_ref,
        jnp.broadcast_to(pole_real, (chunk_count, width)),
        jnp.broadcast_to(-pole_imag, (chunk_count, width)),
        pair_at(d_states_ref, 2 * width, width), pair_at(d_states_ref, 0, width),
        entrances, put_forward, put_reverse,
    )
    span = count // chunk_count

    def decay_terms(here, before_real, before_imag, after_real, after_imag, sums):
        keep = spread(flags_ref[0, here, :], width)
        lam_real, lam_imag = lam_ref[here, :width], lam_ref[here, width:]
        mu_real, mu_imag = mu_ref[here, :width], mu_ref[here, width:]
        real = keep * (lam_real * before_real + lam_imag * before_imag)
        imag = keep * (lam_imag * before_real - lam_real * before_imag)
        keep = spread(flags_ref[1, here, :], width)
        real = real + keep * (mu_real * after_real + mu_imag * after_imag)
        imag = imag + keep * (mu_imag * after_real - mu_real * after_imag)
        return sums[0] + real, sums[1] + imag

    def window(step):
        start = chunk_count * step
        return pl.ds(start if isinstance(step, int) else pl.multiple_of(start, chunk_count), chunk_count)

    def before_at(step):
        rows = window(step)
        return states_ref[rows, :width], states_ref[rows, width : 2 * width]

    def after_at(step):
        rows = window(step)
        return states_ref[rows, 2 * width : 3 * width], states_ref[rows, 3 * width :]

    def middle(step, sums):
        return decay_terms(window(step), *before_at(step - 1), *after_at(step + 1), sums)

    zero = jnp.zeros((chunk_count, width), f32)
    sums = decay_terms(
        window(0), enter_ref[:, :width], enter_ref[:, width : 2 * width], *after_at(1), (zero, zero)
    )
    sums = lax.fori_loop(1, span - 1, middle, sums, unroll=2)
    sums = decay_terms(
        window(span - 1), *before_at(span - 2),
        enter_ref[:, 2 * width : 3 * width], enter_ref[:, 3 * width :], sums,
    )
    rate_grad_ref[0:1, :] = jnp.sum(sums[0], axis=0, keepdims=True)
    rate_grad_ref[1:2, :] = jnp.sum(sums[1], axis=0, keepdims=True)

    def narrow(rows):
        low_ref[rows, :] = (lam_ref[rows, :] + mu_ref[rows, :]).astype(bf16)

    over_blocks(count, narrow)
    in_ref = in_ref.ready()
    write_bar(tables_ref, layer, in_ref, bar_ref)
    work_ref[...] = dot_right(low_ref[...], bar_ref[...])
    skip = skip_ref[layer : layer + 1, :]
    gain = gain_ref[layer : layer + 1, :]
    gain_grad_ref[...] = jnp.zeros(gain_grad_ref.shape, f32)

    def norm_back(rows):
        valid = spread(flags_ref[2, rows, :], model)
        normed, inverse = normalize(values_ref[rows, :].astype(f32))
        d_scaled = (work_ref[rows, :] + d_mixed_ref[rows, :] * skip) * valid
        gain_grad_ref[...] += jnp.sum(d_scaled * normed, axis=0, keepdims=True)
        d_normed = d_scaled * gain
        put_gradient(
            rows,
            inverse
            * (
                d_normed
                - jnp.mean(d_normed, axis=-1, keepdims=True)
                - normed * jnp.mean(d_normed * normed, axis=-1, keepdims=True)
            )
            + grad_ref[rows, :].astype(f32),
        )

    over_blocks(count, norm_back)
    in_grad_ref[...] = dot_left(scaled_ref[...], low_ref[...])
    factor_real, factor_imag = layer_factors(tables_ref, layer)
    rate_grad_ref[2:4, :] = jnp.zeros((2, width), f32)

    def weigh(rows):
        grad_real, grad_imag = in_grad_ref[rows, :width], in_grad_ref[rows, width:]
        weight_real = in_ref[rows, :width].astype(f32)
        weight_imag = in_ref[rows, width:].astype(f32)
        rate_grad_ref[2:3, :] += jnp.sum(
            grad_real * weight_real + grad_imag * weight_imag, axis=0, keepdims=True
        )
        rate_grad_ref[3:4, :] += jnp.sum(
            grad_imag * weight_real - grad_real * weight_imag, axis=0, keepdims=True
        )
        in_grad_ref[rows, :width] = factor_real * grad_real + factor_imag * grad_imag
        in_grad_ref[rows, width:] = factor_real * grad_imag - factor_imag * grad_real

    over_blocks(in_ref.shape[0], weigh)
    emit.put("in", in_grad_ref)


def first_kernel(
    length, place_ref, docs_ref, inputs_ref, gain_ref, tables_ref, in_ref,
    flags_ref, blocks_ref, values_ref, scaled_ref, drive_ref, ends_ref, totals_ref, bar_ref,
):
    write_flags(place_ref[0], docs_ref, flags_ref, blocks_ref, length)
    count, model = values_ref.shape
    values_ref[...] = dot(
        order_matrix(count, False), inputs_ref[...].reshape(count, model)
    ).astype(bf16)
    gain = gain_ref[0:1, :]

    def body(rows):
        normed, unused = normalize(values_ref[rows, :].astype(f32))
        valid = spread(flags_ref[2, rows, :], model)
        scaled_ref[rows, :] = (normed * gain * valid).astype(bf16)

    over_blocks(count, body)
    drive_totals(
        flags_ref, tables_ref, 0, scaled_ref, in_ref, bar_ref, drive_ref, ends_ref, totals_ref
    )


def middle_kernel(
    layer, length, place_ref, gathered_ref, flags_ref, blocks_ref, tables_ref, gain_ref, skip_ref,
    drive_ref, ends_ref, values_ref, scaled_ref, out_ref, glu_ref, in_ref,
    states_ref, low_ref, enter_ref, mixed_ref, act_ref, gate_ref,
    next_values_ref, next_scaled_ref, next_drive_ref, next_ends_ref, next_totals_ref, bar_ref,
):
    settled_states(
        place_ref[0], gathered_ref, flags_ref, blocks_ref, tables_ref, layer, drive_ref, ends_ref, length,
        states_ref, low_ref, enter_ref,
    )
    mix_and_gate(
        layer, low_ref, scaled_ref, out_ref, glu_ref, skip_ref, mixed_ref, act_ref, gate_ref
    )
    model = values_ref.shape[1]
    gain = gain_ref[layer + 1 : layer + 2, :]

    def body(rows):
        valid = spread(flags_ref[2, rows, :], model)
        gate = jax.nn.sigmoid(gate_ref[rows, :])
        gate_ref[rows, :] = gate
        result = values_ref[rows, :].astype(f32) + valid * act_ref[rows, :].astype(f32) * gate
        next_values_ref[rows, :] = result
        normed, unused = normalize(result)
        next_scaled_ref[rows, :] = (normed * gain * valid).astype(bf16)

    over_blocks(values_ref.shape[0], body)
    drive_totals(
        flags_ref, tables_ref, layer + 1, next_scaled_ref, in_ref, bar_ref, next_drive_ref,
        next_ends_ref, next_totals_ref,
    )


def turn_kernel(
    layer, length, place_ref, gathered_ref, flags_ref, blocks_ref, tables_ref, skip_ref,
    drive_ref, ends_ref, values_ref, scaled_ref, out_ref, glu_ref, cotangent_ref,
    *rest,
):
    unit_refs, rest = rest[: 2 * len(turn_units)], rest[2 * len(turn_units) :]
    (
        output_ref, grad_ref, states_ref, enter_ref, d_mixed_ref, d_states_ref,
        skip_grad_ref, back_ends_ref, back_totals_ref, glu_grad_ref,
        low_ref, mixed_ref, act_ref, gate_ref, result_ref, logits_ref, work_ref, mixed_low_ref,
        out_grad_ref,
    ) = rest
    emit = Emit(turn_units, unit_refs, values_ref.shape[1], tables_ref.shape[1])
    settled_states(
        place_ref[0], gathered_ref, flags_ref, blocks_ref, tables_ref, layer, drive_ref, ends_ref, length,
        states_ref, low_ref, enter_ref,
    )
    mix_and_gate(
        layer, low_ref, scaled_ref, out_ref, glu_ref, skip_ref, mixed_ref, act_ref, gate_ref
    )
    count, model = values_ref.shape

    def body(rows):
        valid = spread(flags_ref[2, rows, :], model)
        gate = jax.nn.sigmoid(gate_ref[rows, :])
        gate_ref[rows, :] = gate
        result = values_ref[rows, :] + valid * act_ref[rows, :].astype(f32) * gate
        result_ref[rows, :] = result.astype(bf16)

    over_blocks(count, body)
    output_ref[...] = (
        dot(order_matrix(count, True), result_ref[...]).astype(bf16).reshape(output_ref.shape)
    )
    grad_ref[...] = dot(order_matrix(count, False), cotangent_ref[...].reshape(count, model))
    back_tail(
        layer, flags_ref, tables_ref, grad_ref, mixed_ref, act_ref, gate_ref, scaled_ref, low_ref,
        out_ref, glu_ref, skip_ref, logits_ref, work_ref, mixed_low_ref,
        d_mixed_ref, d_states_ref, glu_grad_ref, out_grad_ref, skip_grad_ref, back_ends_ref,
        back_totals_ref, emit,
    )


def back_middle_kernel(
    layer, length, place_ref, gathered_ref, flags_ref, blocks_ref, tables_ref, gain_ref, skip_ref, in_ref,
    d_states_ref, ends_ref, states_ref, enter_ref, scaled_ref, values_ref, d_mixed_ref, grad_ref,
    out_ref, glu_ref, below_mixed_ref, below_act_ref, below_gate_ref, below_scaled_ref, below_low_ref,
    over_grad_ref, *rest,
):
    unit_refs, rest = rest[: 2 * len(middle_units)], rest[2 * len(middle_units) :]
    (
        gain_grad_ref, rate_grad_ref, next_grad_ref, below_d_mixed_ref,
        below_d_states_ref, skip_grad_ref, below_ends_ref, below_totals_ref,
        lam_ref, mu_ref, low_ref, bar_ref, work_ref, logits_ref, mixed_low_ref,
        in_grad_ref, glu_grad_ref, out_grad_ref,
    ) = rest
    emit = Emit(middle_units, unit_refs, values_ref.shape[1], tables_ref.shape[1])
    emit.put("over", over_grad_ref)

    def put_gradient(rows, gradient):
        next_grad_ref[rows, :] = gradient

    back_front(
        place_ref[0], layer, length, gathered_ref, flags_ref, blocks_ref, tables_ref, gain_ref, skip_ref,
        in_ref, d_states_ref, ends_ref, states_ref, enter_ref, scaled_ref, values_ref, d_mixed_ref,
        grad_ref, lam_ref, mu_ref, low_ref, bar_ref, work_ref,
        in_grad_ref, gain_grad_ref, rate_grad_ref, put_gradient, emit,
    )
    back_tail(
        layer - 1, flags_ref, tables_ref, next_grad_ref, below_mixed_ref, below_act_ref, below_gate_ref,
        below_scaled_ref, below_low_ref, out_ref, glu_ref, skip_ref, logits_ref, work_ref, mixed_low_ref,
        below_d_mixed_ref, below_d_states_ref, glu_grad_ref, out_grad_ref, skip_grad_ref,
        below_ends_ref, below_totals_ref, emit,
    )


def back_last_kernel(
    length, place_ref, gathered_ref, flags_ref, blocks_ref, tables_ref, gain_ref, skip_ref, in_ref,
    d_states_ref, ends_ref, states_ref, enter_ref, scaled_ref, values_ref, d_mixed_ref, grad_ref,
    *rest,
):
    layer_count = gain_ref.shape[0]
    skip_grads = rest[:layer_count]
    rest = rest[layer_count:]
    gain_grads = rest[: layer_count - 1]
    rate_grads = rest[layer_count - 1 : 2 * layer_count - 2]
    unit_refs = rest[2 * layer_count - 2 : 2 * layer_count]
    (
        input_grad_ref,
        lam_ref, mu_ref, low_ref, bar_ref, work_ref, result_ref,
        in_grad_ref, gain_grad_ref, rate_grad_ref, small_ref,
    ) = rest[2 * layer_count :]
    emit = Emit(last_units, unit_refs, values_ref.shape[1], tables_ref.shape[1])
    def put_gradient(rows, gradient):
        result_ref[rows, :] = gradient.astype(bf16)

    back_front(
        place_ref[0], 0, length, gathered_ref, flags_ref, blocks_ref, tables_ref, gain_ref, skip_ref,
        in_ref, d_states_ref, ends_ref, states_ref, enter_ref, scaled_ref, values_ref, d_mixed_ref,
        grad_ref, lam_ref, mu_ref, low_ref, bar_ref, work_ref,
        in_grad_ref, gain_grad_ref, rate_grad_ref, put_gradient, emit,
    )
    small_ref[...] = jnp.zeros(small_ref.shape, f32)
    row = 0
    for vectors in ((gain_grad_ref, *gain_grads), skip_grads, (rate_grad_ref, *rate_grads)):
        for vector_ref in vectors:
            for line in range(vector_ref.shape[0]):
                for first in range(0, vector_ref.shape[1], lane_count):
                    small_ref[row : row + 1, :] = vector_ref[line : line + 1, first : first + lane_count]
                    row += 1
    emit.put("small", small_ref)
    count = result_ref.shape[0]
    input_grad_ref[...] = (
        dot(order_matrix(count, True), result_ref[...]).astype(bf16).reshape(input_grad_ref.shape)
    )


halvings = 3
half_blocks = 1 << halvings
turn_units = (("a", ("out", "glu"), "plane"),)
middle_units = (("b", ("out", "glu"), "plane"), ("d", ("in",), "inner"))
last_units = (("c", ("in", "small"), "plane"),)
after_turn = ("=a",)
into_middle = ("=a",)
after_middle = ("bd", "=a")
into_last = ("=bda",)
after_last = ("a", "bc", "d", "cb", *"dabcdacadbcbcdacbd", "A", "cb", "d", "B", "c")


def mesh_bits():
    seq_bits = lax.axis_size("seq").bit_length() - 1
    batch_bits = lax.axis_size("batch").bit_length() - 1
    deep = [1 << place for place in range(batch_bits)]
    core = 1 << batch_bits
    plane = [core << place for place in range(1, seq_bits)]
    return deep, core, plane[: len(plane) // 2], plane[len(plane) // 2 :]


def axis_orders(kind):
    deep, core, across, along = mesh_bits()
    if kind.endswith(" turned"):
        kind = kind[: -len(" turned")]
        across, along = along, across
    near, far = deep[:1], deep[1:]
    orders = {
        "plane": (across + along + deep, along + across + deep),
        "mixed": (across + along + deep, along + deep + across),
        "inner": (across + near + along + far, along + near + across + far),
        "second": (across + along + deep, near + across + along + far),
        "late": (across + along + deep, along + near + across + far),
        "first": (near + across + along + far, near + along + across + far),
        "cross": (across + along + deep, near + along + across + far),
    }
    return core, orders[kind]


def half_bases(kind):
    core, orders = axis_orders(kind)
    index = lax.axis_index("seq") * lax.axis_size("batch") + lax.axis_index("batch")
    side = lax.rem(lax.div(index, core), 2)
    numbers = []
    for order in orders:
        number = 0
        for bit in order[:halvings]:
            number = 2 * number + lax.rem(lax.div(index, bit), 2)
        numbers.append(number)
    keep = (1 - side) * numbers[0] + side * numbers[1]
    send = (1 - side) * numbers[1] + side * numbers[0]
    return side * half_blocks + keep, (1 - side) * half_blocks + send


def swap(array, first, second):
    core = mesh_bits()[1]
    total = lax.axis_size("seq") * lax.axis_size("batch")
    pairs = [(index, index ^ (second if index & core else first)) for index in range(total)]
    return lax.ppermute(array, ("seq", "batch"), pairs)


class UnitSum:
    def __init__(self, keep, send, kind):
        self.core, orders = axis_orders(kind)
        self.steps = list(zip(*orders))
        self.parts = [keep]
        self.top = keep.shape[0]
        self.runs = None
        self.rounds = self.plan(send)
        self.outgoing = next(self.rounds)

    def added(self, low, high):
        total = self.parts[0][low:high]
        for part in self.parts[1:]:
            total = total + part[low:high]
        return total

    def plan(self, send):
        sent = yield send
        self.parts.append(swap(sent, self.core, self.core))
        for step, (first, second) in enumerate(self.steps):
            if step < halvings:
                self.top //= 2
                sent = yield self.added(self.top, 2 * self.top)
                self.parts.append(swap(sent, first, second))
            else:
                own = yield self.added(0, self.top)
                self.parts = [own, swap(own, first, second)]
        full = self.added(0, self.top)
        for first, second in self.steps[halvings - 1 : 0 : -1]:
            full = yield full
            full = jnp.concatenate([full, swap(full, first, second)])
        full = yield full
        rest = swap(full, *self.steps[0])
        other = swap(full, self.core, self.core)
        rest = yield rest
        self.runs = (full, rest, other, swap(rest, self.core, self.core))
        yield None

    def launch(self, sent):
        self.outgoing = self.rounds.send(sent)


class Line:
    def __init__(self):
        self.last = ()

    def advance(self, units, payload=()):
        units = [unit for unit in units if unit.runs is None]
        sends, payload, unused = lax.optimization_barrier(
            ([unit.outgoing for unit in units], payload, self.last)
        )
        for unit, sent in zip(units, sends):
            unit.launch(sent)
        self.last = sends
        return payload

    def settle(self, arrays):
        arrays, self.last = lax.optimization_barrier((arrays, self.last))
        return arrays


def aligned(first, rows):
    return pl.ds(pl.multiple_of(first, 8), rows)


class Layout:
    def __init__(self, rows, columns, kind):
        self.rows, self.columns, self.kind = rows, columns, kind
        self.sections = {}

    def add(self, key, array_rows, array_first, block_first, count, columns=slice(None)):
        self.sections.setdefault(key, []).append(
            (
                lambda owner: (aligned(owner * array_rows + array_first, count), slice(None)),
                lambda place: (aligned(place * self.rows + block_first, count), columns),
            )
        )

    def half(self):
        return ((half_blocks * self.rows, self.columns), f32)


def unit_layout(keys, kind, model, width):
    total = 2 * half_blocks
    out_rows, rows, wide = 4 * width // total, model // total, 2 * width
    if keys == ("out",):
        layout = Layout(out_rows, model, kind)
        layout.add("out", out_rows, 0, 0, out_rows)
    elif keys == ("glu",):
        layout = Layout(rows, model, kind)
        layout.add("glu", rows, 0, 0, rows)
    elif keys == ("out", "glu"):
        layout = Layout(out_rows + rows, model, kind)
        layout.add("out", out_rows, 0, 0, out_rows)
        layout.add("glu", rows, 0, out_rows, rows)
    elif keys == ("in",):
        layout = Layout(rows, wide, kind)
        layout.add("in", rows, 0, 0, rows)
    elif keys[1:] == ("in",):
        layout = Layout(rows, model + wide, kind)
        layout.add(keys[0], rows, 0, 0, rows, slice(0, model))
        layout.add("in", rows, 0, 0, rows, slice(model, model + wide))
    else:
        pieces = rows // 8
        layout = Layout(8, pieces * wide + lane_count, kind)
        for piece in range(pieces):
            layout.add("in", rows, 8 * piece, 0, 8, slice(piece * wide, (piece + 1) * wide))
        layout.add("small", 8, 0, 0, 8, slice(pieces * wide, pieces * wide + lane_count))
    return layout


class Emit:
    def __init__(self, units, refs, model, width):
        self.homes = {}
        for index, (unused, keys, kind) in enumerate(units):
            layout = unit_layout(keys, kind, model, width)
            for key in keys:
                self.homes[key] = (layout, refs[2 * index : 2 * index + 2], half_bases(kind))

    def put(self, key, array_ref):
        if key not in self.homes:
            return
        layout, halves, bases = self.homes[key]

        def one(place, carry):
            for half in (1, 0):
                owner = lax.bitwise_xor(bases[half], place)
                for array_at, block_at in layout.sections[key]:
                    halves[half][block_at(place)] = array_ref[array_at(owner)]
            return carry

        lax.fori_loop(0, half_blocks, one, 0)


run_places = ((0, 0), (0, half_blocks // 2), (1, 0), (1, half_blocks // 2))


def start_places(layout, goals, runs, outs, semaphores):
    bases = half_bases(layout.kind)
    for index, (half, first) in enumerate(run_places):

        def one(place, carry, run=runs[index], half=half, first=first, index=index):
            owner = lax.bitwise_xor(bases[half], first + place)
            for key, which, layer in goals:
                for array_at, block_at in layout.sections[key]:
                    pltpu.make_async_copy(
                        run.at[block_at(place)],
                        outs[which].at[layer].at[array_at(owner)],
                        semaphores.at[index],
                    ).start()
            return carry

        lax.fori_loop(0, half_blocks // 2, one, 0)


def place_kernel(layout, goals, out_count, *refs):
    runs, semaphores = refs[: len(run_places)], refs[-1]
    start_places(layout, goals, runs, refs[len(refs) - 1 - out_count : -1], semaphores)
    for index, run in enumerate(runs):
        pltpu.make_async_copy(run, run, semaphores.at[index]).wait()


def finish_kernel(layout, goals, fixed, *refs):
    runs = refs[: len(run_places)]
    slopes_ref, unused, out_ref, gain_ref, skip_ref, decay_ref, frequency_ref, step_ref = refs[4:12]
    small_ref, semaphores = refs[12:]
    start_places(layout, goals, runs, (out_ref,), semaphores)
    bases = half_bases(layout.kind)
    for run, (half, first) in zip(runs, run_places):
        for place in range(half_blocks // 2):
            owner = lax.bitwise_xor(bases[half], first + place)
            for array_at, block_at in layout.sections["small"]:
                small_ref[array_at(owner)] = run[block_at(place)]
    row = 0
    for ref in (gain_ref, skip_ref):
        for layer in range(ref.shape[0]):
            for column in range(0, ref.shape[1], lane_count):
                ref[layer : layer + 1, column : column + lane_count] = small_ref[row : row + 1, :]
                row += 1
    layer_count, width = decay_ref.shape
    steps = width // lane_count
    for layer in range(layer_count):
        for piece in range(steps):
            columns = slice(piece * lane_count, (piece + 1) * lane_count)
            for index, ref in enumerate((decay_ref, frequency_ref, step_ref)):
                total = None
                for member in range(4):
                    line = row + member * steps + piece
                    slope = slopes_ref[
                        (4 * index + member) * layer_count + layer : (4 * index + member) * layer_count
                        + layer + 1,
                        columns,
                    ]
                    term = slope * small_ref[line : line + 1, :]
                    total = term if total is None else total + term
                ref[layer : layer + 1, columns] = total
        row += 4 * steps
    for index, run in enumerate(runs):
        moved = run.at[:, fixed]
        pltpu.make_async_copy(moved, moved, semaphores.at[index]).wait()


def place_unit(runs, layout, goals, shapes, sums):
    arrays = sorted({array for unused, array, unused_too in goals})
    operands = [("run", run) for run in runs]
    aliases = {}
    for index, array in enumerate(arrays):
        if array in sums:
            aliases[len(operands)] = index
            operands.append(("before", (sums[array], None)))
    outs = call(
        functools.partial(
            place_kernel, layout, [(key, arrays.index(array), layer) for key, array, layer in goals],
            len(arrays),
        ),
        "place_" + "_".join(arrays),
        operands,
        tuple((shapes[array], f32) for array in arrays),
        (pltpu.SemaphoreType.DMA((len(run_places),)),),
        written=range(len(arrays)),
        aliases=aliases,
        plain=True,
    )
    sums.update(zip(arrays, outs))


def finish_unit(runs, layout, slopes, shape, before, vectors, small_out):
    return call(
        functools.partial(
            finish_kernel, layout, [("in", 0, 0)], slice(0, layout.columns - lane_count)
        ),
        "place_last",
        [("run", run) for run in runs] + [("slopes", slopes), ("before", (before, None))],
        ((shape, f32),) + tuple((each, f32) for each in vectors),
        (small_out, pltpu.SemaphoreType.DMA((len(run_places),))),
        written=(0,),
        final=range(1, 1 + len(vectors)),
        aliases={len(runs) + 1: 0},
        plain=True,
    )


class Fetch:
    def __init__(self, stack_ref, layer, target, semaphore):
        self.copy = pltpu.make_async_copy(stack_ref.at[layer], target, semaphore)
        self.target = target
        self.waiting = True
        self.copy.start()

    def ready(self):
        if self.waiting:
            self.copy.wait()
            self.waiting = False
        return self.target


def call(body, name, operands, outs, scratch, written=(), aliases=None, plain=False, micros=4, final=()):
    scalars = {"place", "docs"}
    arrays = []
    specs = []
    layers = {}
    pieces = None
    flat = []
    for key, operand in operands:
        if isinstance(operand, list):
            pieces = (len(flat), len(operand))
            flat.extend((key, piece) for piece in operand)
        else:
            flat.append((key, operand))
    for position, (key, operand) in enumerate(flat):
        space = pltpu.SMEM if key in scalars else pltpu.VMEM
        if isinstance(operand, tuple):
            operand, layer = operand
            space = pl.ANY
            if layer is not None:
                layers[position] = layer
                operand = pltpu.with_memory_space_constraint(operand, pltpu.HBM)
        specs.append(pl.BlockSpec(memory_space=space))
        arrays.append(operand)
    fetched = [
        pltpu.VMEM(arrays[position].shape[1:], arrays[position].dtype) for position in layers
    ]

    gathered = []
    if pieces is not None:
        first, count = pieces
        rows, columns = arrays[first].shape
        gathered = [pltpu.VMEM((count * rows, columns), arrays[first].dtype)]

    def kernel(*refs):
        if plain:
            body(*refs)
            return
        given = list(refs[: len(arrays)])
        rest = refs[len(arrays) : len(refs) - len(fetched) - 1]
        targets = refs[len(refs) - len(fetched) - 1 : -1]
        for index, (position, layer) in enumerate(layers.items()):
            given[position] = Fetch(given[position], layer, targets[index], refs[-1].at[index])
        if pieces is not None:
            first, count = pieces
            rows = given[first].shape[0]
            whole, rest = rest[-1], rest[:-1]
            for offset in range(count):
                source = lax.bitwise_xor(given[0][0], offset)
                whole[aligned(source * rows, rows), :] = given[first + offset][...]
            given[first : first + count] = [whole]
        body(*given, *rest)

    return pl.pallas_call(
        kernel,
        name=name,
        in_specs=specs,
        out_specs=[
            pl.BlockSpec(memory_space=pl.ANY if place in written else pltpu.VMEM)
            for place in range(len(outs))
        ],
        out_shape=[
            jax.ShapeDtypeStruct(shape, kind)
            if place in written or place in final
            else pltpu.VMEM(shape, kind)
            for place, (shape, kind) in enumerate(outs)
        ],
        scratch_shapes=[
            entry if not isinstance(entry, tuple) else pltpu.VMEM(*entry) for entry in scratch
        ]
        + gathered
        + fetched
        + ([] if plain else [pltpu.SemaphoreType.DMA((max(1, len(fetched)),))]),
        input_output_aliases=aliases or {},
        cost_estimate=pl.CostEstimate(
            flops=micros * 1_000_000_000, bytes_accessed=micros * 3_600_000, transcendentals=0
        ),
        compiler_params=pltpu.CompilerParams(vmem_limit_bytes=vmem_bytes),
    )(*arrays)


def on_device(
    inputs,
    doc_lengths,
    norm_gain,
    decay_log,
    frequency,
    step_log,
    in_weight,
    skip_weight,
    out_weight,
    glu_weight,
    cotangent,
):
    row_count, length, model = inputs.shape
    layer_count, width = decay_log.shape
    count = row_count * length
    device_count = lax.axis_size("seq")
    place = lax.axis_index("seq").astype(jnp.int32).reshape(1)
    rate_tables, rates_back = jax.vjp(rates, decay_log, frequency, step_log)
    tables = jnp.stack(rate_tables, axis=1).reshape(4 * layer_count, width)
    none = jnp.zeros((layer_count, width), f32)
    by_rate = [
        rates_back(tuple(none + 1.0 if member == rate else none for member in range(4)))
        for rate in range(4)
    ]
    slopes = jnp.concatenate(
        [by_rate[rate][parameter] for parameter in range(3) for rate in range(4)], axis=0
    )

    def gather(totals):
        if device_count != 8:
            return lax.all_gather(totals, "seq", axis=0, tiled=True)

        def from_other(array, bits):
            return lax.ppermute(
                array, "seq", [(index, index ^ bits) for index in range(device_count)]
            )

        pieces = [None] * device_count
        pieces[0] = totals
        for bits in range(2, device_count, 2):
            pieces[bits] = from_other(totals, bits)
        for bits in range(0, device_count, 2):
            pieces[bits + 1] = from_other(pieces[bits], 1)
        return pieces

    flags_out = ((3, count, lane_count), f32)
    blocks_out = ((2, device_count * row_count, lane_count), f32)
    wide_out = ((count, 4 * width), f32)
    ends_out = ((chunk_count, 4 * width), f32)
    totals_out = ((4 * row_count, width), f32)
    tokens = ((count, model), f32)
    tokens_low = ((count, model), bf16)
    drive_out = ((count, 2 * width), f32)
    bar_out = ((model, 2 * width), bf16)
    glu_out = ((model, model), f32)
    out_out = ((4 * width, model), f32)
    in_out = ((model, 2 * width), f32)
    vector = ((1, model), f32)

    def in_place(array):
        return pltpu.with_memory_space_constraint(array, pltpu.HBM)

    flags, blocks, values, scaled, drive, ends, totals = call(
        functools.partial(first_kernel, length),
        "first",
        (
            ("place", place),
            ("docs", in_place(doc_lengths)),
            ("inputs", in_place(inputs)),
            ("gain", in_place(norm_gain)),
            ("tables", tables),
            ("in", (in_weight, 0)),
        ),
        (flags_out, blocks_out, tokens_low, tokens_low, drive_out, ends_out, totals_out),
        (bar_out,),
    )
    shared = (("flags", flags), ("blocks", blocks), ("tables", tables))
    kept = []
    for layer in range(layer_count - 1):
        gathered = gather(totals)
        (
            states, low, enter, mixed, act, gate, next_values, next_scaled, drive, ends, totals,
        ) = call(
            functools.partial(middle_kernel, layer, length),
            "middle",
            (
                ("place", place),
                ("gathered", gathered),
                *shared,
                ("gain", norm_gain),
                ("skip", skip_weight),
                ("drive", drive),
                ("ends", ends),
                ("values", values),
                ("scaled", scaled),
                ("out", (out_weight, layer)),
                ("glu", (glu_weight, layer)),
                ("in", (in_weight, layer + 1)),
            ),
            (
                wide_out, ((count, 4 * width), bf16), ends_out, tokens, tokens_low, tokens,
                tokens, tokens_low, drive_out, ends_out, totals_out,
            ),
            (bar_out,),
        )
        kept.append((states, low, enter, mixed, act, gate, values, scaled))
        values, scaled = next_values, next_scaled
    layer = layer_count - 1
    gathered = gather(totals)
    small_out = ((8 * 2 * half_blocks, lane_count), f32)
    shapes = {
        "out": (layer_count, 4 * width, model),
        "glu": (layer_count, model, model),
        "in": (layer_count, model, 2 * width),
        "small": small_out[0],
    }
    sums = {}
    line = Line()
    layouts, goals, units = {}, {}, {}

    def unit_outs(entries):
        outs = []
        for name, keys, kind in entries:
            layouts[name] = unit_layout(keys, kind, model, width)
            outs.extend([((half_blocks * layouts[name].rows, layouts[name].columns), f32)] * 2)
        return tuple(outs)

    def open_units(entries, halves, layer_of):
        for index, (name, keys, kind) in enumerate(entries):
            units[name] = UnitSum(halves[2 * index], halves[2 * index + 1], kind)
            goals[name] = [(key, "glu" if key == "over" else key, layer_of[key]) for key in keys]

    placed = set()

    def place_sums(name):
        placed.add(name)
        runs = line.settle(units[name].runs)
        place_unit(runs, layouts[name], goals[name], shapes, sums)
        line.last = [sums[array] for unused, array, unused_too in goals[name]]

    def follow(plan, payload=()):
        for group in plan:
            if group.isupper():
                for name in group.lower():
                    if units[name].runs is not None and name not in placed:
                        place_sums(name)
            elif group[0] == "=":
                payload = line.advance([units[name] for name in group[1:]], payload)
            else:
                line.advance([units[name] for name in group])
        return payload

    results = call(
        functools.partial(turn_kernel, layer, length),
        "turn",
        (
            ("place", place),
            ("gathered", gathered),
            *shared,
            ("skip", skip_weight),
            ("drive", drive),
            ("ends", ends),
            ("values", values),
            ("scaled", scaled),
            ("out", (out_weight, layer)),
            ("glu", (glu_weight, layer)),
            ("cotangent", cotangent),
        ),
        (
            *unit_outs(turn_units), (inputs.shape, bf16), tokens, wide_out, ends_out, tokens, wide_out,
            vector, ends_out, totals_out, glu_out,
        ),
        (
            ((count, 4 * width), bf16), tokens, tokens_low, tokens, tokens_low, tokens_low, tokens,
            tokens_low, out_out,
        ),
        final=(2 * len(turn_units),),
        micros=6,
    )
    halves, results = results[: 2 * len(turn_units)], results[2 * len(turn_units) :]
    output, grad, states, enter, d_mixed, d_states, skip_grad, ends, totals, over_grad = results
    open_units(turn_units, halves, {"out": layer, "glu": layer})
    gathered = follow(into_middle, gather(follow(after_turn, totals)))
    back_scratch = (
        drive_out, drive_out, ((count, 2 * width), bf16), bar_out, tokens,
    )
    rate_out = ((4, width), f32)
    low_states, low, low_enter, mixed, act, gate, low_values, low_scaled = kept[0]
    results = call(
        functools.partial(back_middle_kernel, layer, length),
        "back_middle",
        (
            ("place", place),
            ("gathered", gathered),
            *shared,
            ("gain", norm_gain),
            ("skip", skip_weight),
            ("in", (in_weight, layer)),
            ("d_states", d_states),
            ("ends", ends),
            ("states", states),
            ("enter", enter),
            ("scaled", scaled),
            ("values", values),
            ("d_mixed", d_mixed),
            ("grad", grad),
            ("out", (out_weight, layer - 1)),
            ("glu", (glu_weight, layer - 1)),
            ("mixed", mixed),
            ("act", act),
            ("gate", gate),
            ("below_scaled", low_scaled),
            ("low", low),
            ("over", over_grad),
        ),
        (
            *unit_outs(middle_units), vector, rate_out, tokens, tokens, wide_out, vector, ends_out,
            totals_out,
        ),
        back_scratch + (tokens_low, tokens_low, in_out, glu_out, out_out),
        micros=6,
    )
    halves, results = results[: 2 * len(middle_units)], results[2 * len(middle_units) :]
    gain_grad, rate_grad, grad, d_mixed, d_states, low_skip_grad, ends, totals = results
    open_units(middle_units, halves, {"out": layer - 1, "glu": layer - 1, "over": layer, "in": layer})
    gathered = follow(into_last, gather(follow(after_middle, totals)))
    keep, send, input_grad = call(
        functools.partial(back_last_kernel, length),
        "back_last",
        (
            ("place", place),
            ("gathered", gathered),
            *shared,
            ("gain", norm_gain),
            ("skip", skip_weight),
            ("in", (in_weight, 0)),
            ("d_states", d_states),
            ("ends", ends),
            ("states", low_states),
            ("enter", low_enter),
            ("scaled", low_scaled),
            ("values", low_values),
            ("d_mixed", d_mixed),
            ("grad", grad),
            ("skip_grad", low_skip_grad),
            ("skip_grad", skip_grad),
            ("gain_grad", gain_grad),
            ("rate_grad", rate_grad),
        ),
        (*unit_outs(last_units), (inputs.shape, bf16)),
        back_scratch + (tokens_low, in_out, vector, rate_out, small_out),
        final=(2,),
        micros=4,
    )
    open_units(last_units, (keep, send), {"in": 0, "small": None})
    follow(after_last)
    for name, unit in units.items():
        while unit.runs is None:
            follow(name)
    for name in units:
        if name not in placed and name != last_units[0][0]:
            place_sums(name)
    name = last_units[0][0]
    in_sum, gain_sum, skip_sum, decay_grad, frequency_grad, step_grad = finish_unit(
        line.settle(units[name].runs), layouts[name], slopes, shapes["in"], sums["in"],
        ((layer_count, model),) * 2 + ((layer_count, width),) * 3, small_out,
    )
    return (
        output,
        input_grad,
        gain_sum,
        decay_grad,
        frequency_grad,
        step_grad,
        in_sum,
        skip_sum,
        sums["out"],
        sums["glu"],
    )


def solution(mesh):
    in_specs = (
        P("batch", "seq", None),
        P("batch", None),
        P(),
        P(),
        P(),
        P(),
        P(),
        P(),
        P(),
        P(),
        P("batch", "seq", None),
    )
    out_specs = (
        P("batch", "seq", None),
        P("batch", "seq", None),
        P(),
        P(),
        P(),
        P(),
        P(),
        P(),
        P(),
        P(),
    )
    return jax.shard_map(
        on_device, mesh=mesh, in_specs=in_specs, out_specs=out_specs, check_vma=False
    )
```
